256 devices in a mesh: span: 64 (over z, y, core), plane: 4 (over x).
Axes of the slice: x: 4, y: 4, z: 8, core: 2. Of those that a mesh axis runs over, the one named last changes fastest.
Arguments:
- adjoint: float32 [3, 256, 81, 512], P(None, 'span', None, 'plane'), may hold values from -6 to 6
- checkpoints: bfloat16 [8, 2, 256, 81, 512], P(None, None, 'span', None, 'plane'), may hold values from -4 to 4
- checkpoint_step: int32 [3], replicated, may hold values from 0 to 7
- metric: float32 [2, 512], P(None, 'plane'), may hold values from 0.004 to 0.016
- helmholtz_inverse: float32 [256, 81, 81], P('span'), may hold values from -0.08 to 0.8
- wall_element: int32 [1024, 2], replicated, may hold values from 0 to 511
- wall_local: int32 [1024, 2], replicated, may hold values from 0 to 80
- wall_weight: float32 [256, 1024], P('span'), may hold values from 0.7 to 140
Outputs:
- adjoint_next: float32 [3, 256, 81, 512], P(None, 'span', None, 'plane')
- control_gradient: float32 [256, 1024], P('span', 'plane')
The draws below stay inside these ranges and needn't reach their ends.
All inputs are finite; a program needn't handle non-finite values.
Results may differ from the reference program's by a relative error of at most 0.00065.
Values may be sent and summed in bfloat16 or wider, within the bound.
No kernel may reach another device: no remote copies, remote signals or barrier semaphores. Data moves between devices by JAX's collectives and lax.ppermute only.
A program may use at most 128 MiB of HBM per device.

```python
import math
import jax
import jax.numpy as jnp
import numpy as np
from jax import lax

P_SIZE = 8
Q = 81
NZ = 256
NEL = 512
NWALL = 1024
NCK = 8
NSTEP = 3


def draw_helmholtz_inverse(key, part):
    key_diag = jax.random.fold_in(key, 11)
    key_off = jax.random.fold_in(key, 12)
    diagonal = jnp.exp(jax.random.uniform(key_diag, (NZ, Q), jnp.float32, math.log(0.3), math.log(0.8)))
    spread = jnp.clip(0.02 * jax.random.normal(key_off, (NZ, Q, Q), jnp.float32), -0.08, 0.08)
    unit_matrix = jnp.eye(Q, dtype=jnp.float32)
    return diagonal[:, :, None] * unit_matrix + spread * (1.0 - unit_matrix)


def draw_wall_weight(key, part):
    row_pos = jnp.arange(NZ, dtype=jnp.float32)[:, None] / (NZ - 1)
    col_pos = jnp.arange(NWALL, dtype=jnp.float32)[None, :] / (NWALL - 1)
    exponent = 0.5
    factor = jnp.exp(jax.random.uniform(jax.random.fold_in(key, 21), (NZ, NWALL), jnp.float32, math.log(0.7), math.log(1.4)))
    return factor * jnp.power(10.0, exponent * (row_pos + col_pos))


def touch_ends(drawn, stream_key, smallest, top_value):
    place = [jax.random.randint(jax.random.fold_in(stream_key, axis), (), 0, length) for axis, length in enumerate(drawn.shape)]
    main_axis = drawn.shape.index(max(drawn.shape))
    next_to = place[:main_axis] + [(place[main_axis] + 1) % drawn.shape[main_axis]] + place[main_axis + 1:]
    return drawn.at[tuple(place)].set(smallest).at[tuple(next_to)].set(top_value)


def shard_levels(rng, shape, shards, smallest, top_value):
    loudness = 1.0
    for dim, blocks in shards:
        draws = jax.random.uniform(jax.random.fold_in(jax.random.fold_in(rng, 6), dim), (blocks,), jnp.float32, smallest / len(shards), top_value / len(shards))
        loudness = loudness * jnp.repeat(jnp.exp(draws), shape[dim] // blocks).reshape((-1,) + (1,) * (len(shape) - 1 - dim))
    return loudness


def normal_values(stream_key, shape, scale, reach, split=(), kind=jnp.bfloat16):
    entries = scale * jax.random.normal(stream_key, shape, jnp.float32)
    if split:
        entries = entries * shard_levels(stream_key, shape, split, -0.22, 0.18)
    return jnp.clip(entries, -reach, reach).astype(kind)


def setup_inputs(seed: int = 0) -> dict:
    keys = jax.random.split(jax.random.key(seed), 9)
    adjoint = normal_values(keys[0], (3, NZ, Q, NEL), 1.0, 6.0, ((1, 64), (3, 4)), jnp.float32)
    checkpoints = normal_values(keys[1], (NCK, 2, NZ, Q, NEL), 0.7, 4.0, ((2, 64), (4, 4)))
    checkpoint_step = jax.random.randint(keys[2], (NSTEP,), 0, NCK).astype(jnp.int32)
    metric = jnp.clip(jnp.exp(math.log(0.016) - 1.3862944 * jax.random.uniform(keys[3], (2, NEL), jnp.float32) ** shard_levels(keys[3], (2, NEL), ((1, 4),), -0.2, 0.2)), 0.004, 0.016)
    helmholtz_inverse = draw_helmholtz_inverse(jax.random.fold_in(keys[8], 71), 0)
    wall_element = touch_ends(jax.random.randint(keys[5], (NWALL, 2), 0, NEL), jax.random.fold_in(keys[5], 1), 0, NEL - 1).astype(jnp.int32)
    wall_local = touch_ends(jax.random.randint(keys[6], (NWALL, 2), 0, Q), jax.random.fold_in(keys[6], 1), 0, Q - 1).astype(jnp.int32)
    wall_weight = draw_wall_weight(jax.random.fold_in(keys[8], 71), 0)
    return {"adjoint": adjoint, "checkpoints": checkpoints, "checkpoint_step": checkpoint_step, "metric": metric, "helmholtz_inverse": helmholtz_inverse, "wall_element": wall_element, "wall_local": wall_local, "wall_weight": wall_weight}


HIGHEST = lax.Precision.HIGHEST

def chebyshev_matrix(degree):
    points = np.arange(degree + 1)
    abscissa = np.cos(np.pi * points / degree)
    signed = np.where((points == 0) | (points == degree), 2.0, 1.0) * (-1.0) ** points
    spacing = abscissa[:, None] - abscissa[None, :] + np.eye(degree + 1)
    matrix = signed[:, None] / signed[None, :] / spacing
    return matrix - np.eye(degree + 1) * np.sum(matrix, axis=1)[:, None]

def fourier_table(length):
    row_index = np.arange(length)[:, None]
    column = np.arange(length)[None, :]
    wavenumber = (row_index + 1) // 2
    phase_angle = 2.0 * np.pi * wavenumber * column / length
    parity = row_index % 2
    base_rows = np.where(row_index == 0, 1.0, np.where(parity == 1, np.cos(phase_angle), np.sin(phase_angle)))
    row_scale = np.where((row_index == 0) | (row_index == length - 1), 1.0 / np.sqrt(length), np.sqrt(2.0 / length))
    return base_rows * row_scale

def transport(field_data, velocity, metric):
    side_nodes = P_SIZE + 1
    matrix = jnp.asarray(chebyshev_matrix(P_SIZE), jnp.float32)
    shaped = field_data.reshape(field_data.shape[0], field_data.shape[1], side_nodes, side_nodes, field_data.shape[3])
    first_dir = jnp.einsum('ai,czibe->czabe', matrix, shaped, precision=HIGHEST).reshape(field_data.shape)
    second_dir = jnp.einsum('bi,czaie->czabe', matrix, shaped, precision=HIGHEST).reshape(field_data.shape)
    speed_data = velocity.astype(jnp.float32)
    return field_data + speed_data[0] * (metric[0] * first_dir) + speed_data[1] * (metric[1] * second_dir)

def one_component(component, velocity, metric, helmholtz_inverse):
    advected = transport(component[None], velocity, metric)[0]
    basis_table = jnp.asarray(fourier_table(NZ), jnp.float32)
    coefficients = jnp.einsum('jz,zqe->jqe', basis_table, advected, precision=HIGHEST)
    solved = jnp.einsum('jqr,jre->jqe', helmholtz_inverse, coefficients, precision=HIGHEST)
    return jnp.einsum('jz,jqe->zqe', basis_table, solved, precision=HIGHEST)

def reference(adjoint, checkpoints, checkpoint_step, metric, helmholtz_inverse, wall_element, wall_local, wall_weight):
    gradient_sum = jnp.zeros((NZ, NWALL), jnp.float32)
    for substep in range(NSTEP):
        slot_index = checkpoint_step[substep]
        velocity = lax.dynamic_index_in_dim(checkpoints, slot_index, 0, keepdims=False)
        adjoint = lax.map(lambda component: one_component(component, velocity, metric, helmholtz_inverse), adjoint)
        values = adjoint[1][:, wall_local, wall_element]
        speeds = velocity[1][:, wall_local, wall_element].astype(jnp.float32)
        gradient_sum = gradient_sum + lax.optimization_barrier(jnp.sum(values * speeds, axis=2))
    weighted = wall_weight * gradient_sum
    inverse_rms = lax.rsqrt(jnp.mean(weighted * weighted) + 1e-06)
    return (adjoint, weighted * inverse_rms)
```

```python
import jax
import jax.numpy as jnp
import numpy as np
from jax import lax
from jax.experimental import pallas as pl
from jax.experimental.pallas import tpu as pltpu
from jax.sharding import PartitionSpec as P

P_SIZE = 8
Q = 81
QP = 88
NSTEP = 3
HIGHEST = lax.Precision.HIGHEST
F32 = jnp.float32
VMEM_BYTES = 56 * 1024 * 1024


def chebyshev_matrix(degree):
    points = np.arange(degree + 1)
    abscissa = np.cos(np.pi * points / degree)
    signed = np.where((points == 0) | (points == degree), 2.0, 1.0) * (-1.0) ** points
    spacing = abscissa[:, None] - abscissa[None, :] + np.eye(degree + 1)
    matrix = signed[:, None] / signed[None, :] / spacing
    return matrix - np.eye(degree + 1) * np.sum(matrix, axis=1)[:, None]


def fourier_table(length):
    row_index = np.arange(length)[:, None]
    column = np.arange(length)[None, :]
    wavenumber = (row_index + 1) // 2
    phase_angle = 2.0 * np.pi * wavenumber * column / length
    parity = row_index % 2
    base_rows = np.where(
        row_index == 0, 1.0, np.where(parity == 1, np.cos(phase_angle), np.sin(phase_angle))
    )
    row_scale = np.where(
        (row_index == 0) | (row_index == length - 1), 1.0 / np.sqrt(length), np.sqrt(2.0 / length)
    )
    return base_rows * row_scale


def tables():
    zl = np.arange(256)
    z_of = 4 * (zl % 64) + zl // 64
    jl = np.arange(256)
    j_of = (jl % 128) // 4 * 8 + jl // 128 * 4 + jl % 4
    f = fourier_table(256).astype(np.float32)
    back = f[j_of][:, z_of]
    d = chebyshev_matrix(P_SIZE)
    eye = np.eye(P_SIZE + 1)
    both = np.zeros((2 * QP, QP), np.float32)
    both[:Q, :Q] = np.kron(d, eye)
    both[QP : QP + Q, :Q] = np.kron(eye, d)
    return np.ascontiguousarray(back.T), back, both


def vmem_spec():
    return pl.BlockSpec(memory_space=pltpu.VMEM)


def smem_spec():
    return pl.BlockSpec(memory_space=pltpu.SMEM)


def params():
    return pltpu.CompilerParams(vmem_limit_bytes=VMEM_BYTES)


def pack_inverse_kernel(h_ref, o_ref, t_ref):
    o_ref[...] = jnp.zeros_like(o_ref)
    for j in range(4):
        t_ref[j] = h_ref[j].T
        for r in range(Q):
            start = r * QP
            row, lane = divmod(start, 128)
            first = min(Q, 128 - lane)
            o_ref[j, row, lane : lane + first] = t_ref[j, r, 0:first]
            if first < Q:
                o_ref[j, row + 1, 0 : Q - first] = t_ref[j, r, first:Q]


def pack_inverse(inverse):
    return pl.pallas_call(
        pack_inverse_kernel,
        out_shape=jax.ShapeDtypeStruct((4, 56, 128), F32),
        in_specs=[vmem_spec()],
        out_specs=vmem_spec(),
        scratch_shapes=[pltpu.VMEM((4, Q, Q), F32)],
        compiler_params=params(),
    )(inverse)


def pack_points_kernel(step_ref, adj_ref, c0_ref, c1_ref, c2_ref, o_ref, t_ref):
    stored = (c0_ref, c1_ref, c2_ref)
    for z in range(4):
        for g in range(3):
            t_ref[g, z, 3 * Q : 256, :] = jnp.zeros((256 - 3 * Q, 128), F32)
            for i in range(3):
                if g == 0:
                    block = adj_ref[i, z]
                else:
                    block = stored[i][0, g - 1, z].astype(F32)
                t_ref[g, z, i * Q : (i + 1) * Q, :] = block
            turned = t_ref[g, z].T
            for e in range(2):
                o_ref[:, z * 2 + e, g * 256 : (g + 1) * 256] = turned[e * 64 : (e + 1) * 64, :]


def pack_points(adjoint, checkpoints, checkpoint_step):
    def slot(k):
        return pl.BlockSpec((1, 2, 4, Q, 128), lambda i, st: (st[k], 0, 0, 0, 0))

    return pl.pallas_call(
        pack_points_kernel,
        out_shape=jax.ShapeDtypeStruct((64, 8, 768), F32),
        grid_spec=pltpu.PrefetchScalarGridSpec(
            num_scalar_prefetch=1,
            grid=(1,),
            in_specs=[
                pl.BlockSpec((3, 4, Q, 128), lambda i, st: (0, 0, 0, 0)),
                slot(0),
                slot(1),
                slot(2),
            ],
            out_specs=pl.BlockSpec((64, 8, 768), lambda i, st: (0, 0, 0)),
            scratch_shapes=[pltpu.VMEM((3, 4, 256, 128), F32)],
        ),
        compiler_params=params(),
    )(checkpoint_step, adjoint, checkpoints, checkpoints, checkpoints)


def steps_kernel(
    place_ref, metric_ref, r_ref, own_ref, other_ref, fwd_ref, back_ref, both_ref,
    adj_ref, wall_ref,
    ht, x, v, coef, solved, wall, turn,
):
    chip = place_ref[0]
    core = place_ref[1]

    def turn_inverse(k, carry):
        row = pl.multiple_of(k * 128, 128)
        ht[core, pl.ds(row, 128), :] = own_ref[:, k, :].T
        ht[1 - core, pl.ds(row, 128), :] = other_ref[:, k, :].T
        return carry

    lax.fori_loop(0, 56, turn_inverse, 0)

    x[...] = jnp.zeros_like(x)
    v[...] = jnp.zeros_like(v)
    for e in range(2):
        for g in range(3):
            stack = jnp.concatenate(
                [r_ref[:, z * 2 + e, g * 256 : (g + 1) * 256] for z in range(4)], axis=0
            )
            turn[...] = stack.T
            for i in range(3):
                part = turn[i * Q : (i + 1) * Q, :]
                if g == 0:
                    x[e * 3 + i, 0:Q, :] = part
                else:
                    v[(g - 1), e, i, 0:Q, :] = part

    for step in range(NSTEP):
        for e in range(2):
            m0 = metric_ref[0, chip + 64 * e]
            m1 = metric_ref[1, chip + 64 * e]
            for c in range(3):
                field = x[e * 3 + c]
                slopes = jnp.dot(both_ref[...], field, precision=HIGHEST, preferred_element_type=F32)
                x[e * 3 + c] = (
                    field
                    + v[0, e, step] * (m0 * slopes[0:QP])
                    + v[1, e, step] * (m1 * slopes[QP : 2 * QP])
                )
        modes = jnp.dot(
            x[...].reshape(6 * QP, 256), fwd_ref[...], precision=HIGHEST, preferred_element_type=F32
        )
        coef[0] = modes[:, 0:128]
        coef[1] = modes[:, 128:256]
        for half in range(2):
            for e in range(2):

                def column(r, sums, half=half, e=e):
                    h = ht[half, pl.ds(pl.multiple_of(r * QP, 8), QP), :]
                    return tuple(
                        sums[c] + h * coef[half, pl.ds((e * 3 + c) * QP + r, 1), :] for c in range(3)
                    )

                zero = jnp.zeros((QP, 128), F32)
                sums = lax.fori_loop(0, Q, column, (zero, zero, zero), unroll=3)
                for c in range(3):
                    solved[e * 3 + c, :, half * 128 : (half + 1) * 128] = sums[c]
        planes = jnp.dot(
            solved[...].reshape(6 * QP, 256), back_ref[...], precision=HIGHEST, preferred_element_type=F32
        )
        x[...] = planes.reshape(6, QP, 256)
        for e in range(2):
            product = x[e * 3 + 1] * v[1, e, step]
            if step == 0:
                wall[e, 0:QP] = product
            else:
                wall[e, 0:QP] = wall[e, 0:QP] + product

    for e in range(2):
        wall[e, QP:128, :] = jnp.zeros((128 - QP, 256), F32)
        turned = wall[e].T
        for z in range(4):
            wall_ref[:, z * 2 + e, :] = turned[z * 64 : (z + 1) * 64, :]
        turn[3 * Q : 256, :] = jnp.zeros((256 - 3 * Q, 256), F32)
        for c in range(3):
            turn[c * Q : (c + 1) * Q, :] = x[e * 3 + c, 0:Q, :]
        turned = turn[...].T
        for z in range(4):
            adj_ref[:, z * 2 + e, :] = turned[z * 64 : (z + 1) * 64, :]


def steps(place, metric, points, own, other):
    fwd, back, both = tables()
    return pl.pallas_call(
        steps_kernel,
        out_shape=(
            jax.ShapeDtypeStruct((64, 8, 256), F32),
            jax.ShapeDtypeStruct((64, 8, 128), F32),
        ),
        in_specs=[smem_spec(), smem_spec()] + [vmem_spec()] * 6,
        out_specs=(vmem_spec(), vmem_spec()),
        scratch_shapes=[
            pltpu.VMEM((2, 56 * 128, 128), F32),
            pltpu.VMEM((6, QP, 256), F32),
            pltpu.VMEM((2, 2, 3, QP, 256), F32),
            pltpu.VMEM((2, 6 * QP, 128), F32),
            pltpu.VMEM((6, QP, 256), F32),
            pltpu.VMEM((2, 128, 256), F32),
            pltpu.VMEM((256, 256), F32),
        ],
        compiler_params=params(),
    )(place, metric, points, own, other, jnp.asarray(fwd), jnp.asarray(back), jnp.asarray(both))


def wall_kernel(r_ref, local_ref, element_ref, o_ref):
    points = local_ref.shape[1]
    mode = lax.broadcasted_iota(jnp.int32, (128, points), 0)
    pick = jnp.where(mode == local_ref[...], 1.0, 0.0).astype(jnp.bfloat16)
    here = mode == element_ref[...]
    for z in range(4):
        field = jnp.concatenate([r_ref[:, z * 2, :], r_ref[:, z * 2 + 1, :]], axis=0)
        high = field.astype(jnp.bfloat16)
        rest = field - high.astype(F32)
        middle = rest.astype(jnp.bfloat16)
        low = (rest - middle.astype(F32)).astype(jnp.bfloat16)
        values = (
            jnp.dot(low, pick, preferred_element_type=F32)
            + jnp.dot(middle, pick, preferred_element_type=F32)
            + jnp.dot(high, pick, preferred_element_type=F32)
        )
        total = jnp.sum(jnp.where(here, values, 0.0), axis=0, keepdims=True)
        o_ref[z : z + 1, :] = total[:, 0 : points // 2] + total[:, points // 2 :]


def wall_sums(received, local, element):
    return pl.pallas_call(
        wall_kernel,
        out_shape=jax.ShapeDtypeStruct((4, local.shape[1] // 2), F32),
        in_specs=[vmem_spec()] * 3,
        out_specs=vmem_spec(),
        compiler_params=params(),
    )(received, local, element)


def unpack_kernel(r_ref, o_ref, t_ref):
    for z in range(4):
        stack = jnp.concatenate([r_ref[:, z * 2, :], r_ref[:, z * 2 + 1, :]], axis=0)
        t_ref[z] = stack.T
        for c in range(3):
            o_ref[c, z] = t_ref[z, c * Q : (c + 1) * Q, :]


def unpack(received):
    return pl.pallas_call(
        unpack_kernel,
        out_shape=jax.ShapeDtypeStruct((3, 4, Q, 128), F32),
        in_specs=[vmem_spec()],
        out_specs=vmem_spec(),
        scratch_shapes=[pltpu.VMEM((4, 256, 128), F32)],
        compiler_params=params(),
    )(received)


def on_device(
    adjoint,
    checkpoints,
    checkpoint_step,
    metric,
    helmholtz_inverse,
    wall_element,
    wall_local,
    wall_weight,
):
    span = lax.axis_index("span")
    plane = lax.axis_index("plane")
    span_count = lax.axis_size("span")
    plane_count = lax.axis_size("plane")
    wall_count = wall_element.shape[0]
    place = jnp.stack([span, span % 2]).astype(jnp.int32)

    packed = pack_inverse(helmholtz_inverse)
    same_core = [list(range(core, span_count, 2)) for core in range(2)]
    own = lax.all_gather(packed, "span", axis=0, tiled=True, axis_index_groups=same_core)
    other = lax.ppermute(own, "span", [(i, i ^ 1) for i in range(span_count)])

    sent = pack_points(adjoint, checkpoints, checkpoint_step)
    points = lax.all_to_all(sent, "span", 0, 0, tiled=True)
    adj_out, wall_out = steps(place, metric, points, own, other)

    wall_in = lax.all_to_all(wall_out, "span", 0, 0, tiled=True)
    adj_in = lax.all_to_all(adj_out, "span", 0, 0, tiled=True)

    local = wall_local.T.reshape(1, 2 * wall_count)
    element = wall_element.T.reshape(1, 2 * wall_count) - plane * adjoint.shape[3]
    partial_sum = wall_sums(wall_in, local, element)
    gradient = partial_sum
    for k in range(1, plane_count):
        gradient = gradient + lax.ppermute(
            partial_sum, "plane", [(i, (i + k) % plane_count) for i in range(plane_count)]
        )
    weighted = wall_weight * gradient
    square = jnp.sum(weighted * weighted)
    squares = lax.all_to_all(
        jnp.broadcast_to(square, (span_count, 1, 128)), "span", 0, 0, tiled=True
    )
    total = jnp.sum(squares[:, 0, 0])
    share_width = wall_count // plane_count
    share = lax.dynamic_slice_in_dim(weighted, plane * share_width, share_width, 1)
    inverse_rms = lax.rsqrt(total / (adjoint.shape[1] * span_count * wall_count) + 1e-06)
    return (unpack(adj_in), share * inverse_rms)


def solution(mesh):
    placed = (
        P(None, "span", None, "plane"),
        P(None, None, "span", None, "plane"),
        P(),
        P(None, "plane"),
        P("span", None, None),
        P(),
        P(),
        P("span", None),
    )
    return jax.shard_map(
        on_device,
        mesh=mesh,
        in_specs=placed,
        out_specs=(P(None, "span", None, "plane"), P("span", "plane")),
        check_vma=False,
    )
```

```python
import jax
import jax.numpy as jnp
import numpy as np
from jax import lax
from jax.experimental import pallas as pl
from jax.experimental.pallas import tpu as pltpu
from jax.sharding import PartitionSpec as P

P_SIZE = 8
Q = 81
QP = 88
NSTEP = 3
HIGHEST = lax.Precision.HIGHEST
F32 = jnp.float32
VMEM_BYTES = 56 * 1024 * 1024
LEVELS = 32767.0
SCALE_LANE = 250


def chebyshev_matrix(degree):
    points = np.arange(degree + 1)
    abscissa = np.cos(np.pi * points / degree)
    signed = np.where((points == 0) | (points == degree), 2.0, 1.0) * (-1.0) ** points
    spacing = abscissa[:, None] - abscissa[None, :] + np.eye(degree + 1)
    matrix = signed[:, None] / signed[None, :] / spacing
    return matrix - np.eye(degree + 1) * np.sum(matrix, axis=1)[:, None]


def fourier_table(length):
    row_index = np.arange(length)[:, None]
    column = np.arange(length)[None, :]
    wavenumber = (row_index + 1) // 2
    phase_angle = 2.0 * np.pi * wavenumber * column / length
    parity = row_index % 2
    base_rows = np.where(
        row_index == 0, 1.0, np.where(parity == 1, np.cos(phase_angle), np.sin(phase_angle))
    )
    row_scale = np.where(
        (row_index == 0) | (row_index == length - 1), 1.0 / np.sqrt(length), np.sqrt(2.0 / length)
    )
    return base_rows * row_scale


def lane_order():
    chips = np.arange(32)
    pieces = [(np.arange(64) // 2, np.arange(64) % 2, 0, 0)]
    for part, shift in ((chips, 3), (chips, 1), (chips[:16], 2), (chips[16:], 2)):
        for core in range(2):
            pieces.append((part, np.full(part.shape, core), 1, shift))
    chip = np.concatenate([p[0] for p in pieces])
    core = np.concatenate([p[1] for p in pieces])
    relative = np.concatenate([np.full(p[0].shape, p[2]) for p in pieces])
    shift = np.concatenate([np.full(p[0].shape, p[3]) for p in pieces])
    return [v.astype(np.int32) for v in (chip, core, relative, shift)]


def transforms(core, plane):
    zl = np.arange(256)
    z_of = 4 * (zl % 64) + zl // 64
    table = jnp.asarray(fourier_table(256).astype(np.float32)[:, z_of])
    chip, lane_core, relative, shift = (jnp.asarray(v) for v in lane_order())
    span_of = 2 * chip + lane_core + relative * core * (1 - 2 * lane_core)
    order = 4 * span_of + (plane + shift) % 4
    pick = jnp.where(order[:, None] == jnp.arange(256)[None, :], 1.0, 0.0).astype(F32)
    back = jnp.dot(pick, table, precision=HIGHEST)
    return back.T, back


def slope_table():
    d = chebyshev_matrix(P_SIZE)
    eye = np.eye(P_SIZE + 1)
    both = np.zeros((2 * QP, QP), np.float32)
    both[:Q, :Q] = np.kron(d, eye)
    both[QP : QP + Q, :Q] = np.kron(eye, d)
    return jnp.asarray(both)


def vmem_spec():
    return pl.BlockSpec(memory_space=pltpu.VMEM)


def smem_spec():
    return pl.BlockSpec(memory_space=pltpu.SMEM)


def params():
    return pltpu.CompilerParams(vmem_limit_bytes=VMEM_BYTES)


def pair_up(low, high):
    return (high.astype(jnp.int32) << 16) | (low.astype(jnp.int32) & 0xFFFF)


def low_of(pair):
    return ((pair << 16) >> 16).astype(F32)


def high_of(pair):
    return (pair >> 16).astype(F32)


def pack_inverse_kernel(h_ref, o_ref, w_ref, f_ref):
    h = h_ref[...]
    largest = jnp.max(jnp.abs(h), axis=1, keepdims=True)
    code = jnp.floor(largest * 2.0**30) + 1.0
    upper = jnp.floor(code * 2.0**-15)
    lower = code - upper * 2.0**15
    w_ref[...] = jnp.zeros_like(w_ref)
    w_ref[0:Q, 0:Q] = jnp.round(h * (LEVELS / (code * 2.0**-30)))
    w_ref[0:Q, Q : Q + 1] = upper
    w_ref[0:Q, Q + 1 : Q + 2] = lower
    turned = w_ref[...].T
    w_ref[...] = turned
    f_ref[...] = jnp.zeros_like(f_ref)
    for r in range(Q):
        line, lane = divmod(r * QP, 128)
        first = min(Q, 128 - lane)
        f_ref[line, lane : lane + first] = w_ref[r, 0:first]
        if first < Q:
            f_ref[line + 1, 0 : Q - first] = w_ref[r, first:Q]
    f_ref[56, 0:Q] = w_ref[Q, 0:Q]
    f_ref[57, 0:Q] = w_ref[Q + 1, 0:Q]
    o_ref[...] = jnp.broadcast_to(pair_up(f_ref[0:32, :], f_ref[32:64, :])[None], o_ref.shape)


def pack_inverse(matrix, targets):
    return pl.pallas_call(
        pack_inverse_kernel,
        out_shape=jax.ShapeDtypeStruct((targets, 32, 128), jnp.int32),
        in_specs=[vmem_spec()],
        out_specs=vmem_spec(),
        scratch_shapes=[pltpu.VMEM((128, 128), F32), pltpu.VMEM((64, 128), F32)],
        compiler_params=params(),
    )(matrix)


def pack_points_kernel(step_ref, adj_ref, c0_ref, c1_ref, c2_ref, o_ref, t_ref):
    stored = (c0_ref, c1_ref, c2_ref)
    lane = lax.broadcasted_iota(jnp.int32, (64, 256), 1)
    for z in range(4):
        for g in range(3):
            t_ref[g, z, 3 * Q : 256, :] = jnp.zeros((256 - 3 * Q, 128), F32)
            for i in range(3):
                if g == 0:
                    block = adj_ref[i, z]
                else:
                    block = stored[i][0, g - 1, z].astype(F32)
                t_ref[g, z, i * Q : (i + 1) * Q, :] = block
            block = t_ref[g, z]
            largest = jnp.max(jnp.max(jnp.abs(block), axis=0, keepdims=True), axis=1, keepdims=True)
            code = jnp.floor(largest * 2.0**27) + 1.0
            turned = jnp.round(block * (LEVELS / (code * 2.0**-27))).T
            pair = pair_up(turned[0:64, :], turned[64:128, :])
            pair = jnp.where(lane == SCALE_LANE, code.astype(jnp.int32), pair)
            if g == 0:
                o_ref[:, z * 2, 0:256] = pair
            elif g == 1:
                o_ref[:, z * 2, 256:384] = pair[:, 0:128]
                o_ref[:, z * 2 + 1, 0:128] = pair[:, 128:256]
            else:
                o_ref[:, z * 2 + 1, 128:384] = pair


def pack_points(adjoint, checkpoints, checkpoint_step):
    def slot(k):
        return pl.BlockSpec((1, 2, 4, Q, 128), lambda i, st: (st[k], 0, 0, 0, 0))

    return pl.pallas_call(
        pack_points_kernel,
        out_shape=jax.ShapeDtypeStruct((64, 8, 384), jnp.int32),
        grid_spec=pltpu.PrefetchScalarGridSpec(
            num_scalar_prefetch=1,
            grid=(1,),
            in_specs=[
                pl.BlockSpec((3, 4, Q, 128), lambda i, st: (0, 0, 0, 0)),
                slot(0),
                slot(1),
                slot(2),
            ],
            out_specs=pl.BlockSpec((64, 8, 384), lambda i, st: (0, 0, 0)),
            scratch_shapes=[pltpu.VMEM((3, 4, 256, 128), F32)],
        ),
        compiler_params=params(),
    )(checkpoint_step, adjoint, checkpoints, checkpoints, checkpoints)


def steps_kernel(
    place_ref, metric_ref, r_ref, own_ref, left_ref, left2_ref, right_ref, right2_ref,
    oa_ref, oa2_ref, ob_ref, ob2_ref, fwd_ref, back_ref, both_ref,
    out_ref,
    ht, rows, x, v, coef, solved, wall, turn,
):
    chip = place_ref[0]
    lanes = (
        (own_ref, left_ref, left2_ref),
        (right_ref, right2_ref, oa_ref, oa2_ref, ob_ref, ob2_ref),
    )

    def turn_inverse(k, carry):
        row = pl.multiple_of(k * 128, 128)
        for half in range(2):
            pair = jnp.concatenate([ref[:, k, :] for ref in lanes[half]], axis=0).T
            ht[half, pl.ds(row, 128), :] = low_of(pair)
            ht[half, pl.ds(row + 4096, 128), :] = high_of(pair)
        return carry

    lax.fori_loop(0, 32, turn_inverse, 0)
    for half in range(2):
        rows[half] = (
            ht[half, 7168 : 7168 + QP, :] * 2.0**15 + ht[half, 7296 : 7296 + QP, :]
        ) * (2.0**-30 / LEVELS)

    x[...] = jnp.zeros_like(x)
    v[...] = jnp.zeros_like(v)
    for g in range(3):
        stack = []
        for z in range(4):
            if g == 0:
                stack.append(r_ref[:, z * 2, 0:256])
            elif g == 1:
                stack.append(
                    jnp.concatenate(
                        [r_ref[:, z * 2, 256:384], r_ref[:, z * 2 + 1, 0:128]], axis=1
                    )
                )
            else:
                stack.append(r_ref[:, z * 2 + 1, 128:384])
        pair = jnp.concatenate(stack, axis=0).T
        unit = pair[SCALE_LANE : SCALE_LANE + 1, :].astype(F32) * (2.0**-27 / LEVELS)
        for e in range(2):
            turn[...] = (low_of(pair) if e == 0 else high_of(pair)) * unit
            for i in range(3):
                part = turn[i * Q : (i + 1) * Q, :]
                if g == 0:
                    x[e * 3 + i, 0:Q, :] = part
                else:
                    v[(g - 1), e, i, 0:Q, :] = part

    for step in range(NSTEP):
        for e in range(2):
            m0 = metric_ref[0, chip + 64 * e]
            m1 = metric_ref[1, chip + 64 * e]
            for c in range(3):
                field = x[e * 3 + c]
                slopes = jnp.dot(both_ref[...], field, precision=HIGHEST, preferred_element_type=F32)
                x[e * 3 + c] = (
                    field
                    + v[0, e, step] * (m0 * slopes[0:QP])
                    + v[1, e, step] * (m1 * slopes[QP : 2 * QP])
                )
        modes = jnp.dot(
            x[...].reshape(6 * QP, 256), fwd_ref[...], precision=HIGHEST, preferred_element_type=F32
        )
        coef[0] = modes[:, 0:128]
        coef[1] = modes[:, 128:256]
        for half in range(2):
            for e in range(2):

                def column(r, sums, half=half, e=e):
                    h = ht[half, pl.ds(pl.multiple_of(r * QP, 8), QP), :]
                    return tuple(
                        sums[c] + h * coef[half, pl.ds((e * 3 + c) * QP + r, 1), :] for c in range(3)
                    )

                zero = jnp.zeros((QP, 128), F32)
                sums = lax.fori_loop(0, Q, column, (zero, zero, zero), unroll=3)
                for c in range(3):
                    solved[e * 3 + c, :, half * 128 : (half + 1) * 128] = sums[c] * rows[half]
        planes = jnp.dot(
            solved[...].reshape(6 * QP, 256), back_ref[...], precision=HIGHEST, preferred_element_type=F32
        )
        x[...] = planes.reshape(6, QP, 256)
        for e in range(2):
            product = x[e * 3 + 1] * v[1, e, step]
            if step == 0:
                wall[e, 0:QP] = product
            else:
                wall[e, 0:QP] = wall[e, 0:QP] + product

    for e in range(2):
        wall[e, QP:128, :] = jnp.zeros((128 - QP, 256), F32)
        turned = wall[e].T
        for z in range(4):
            out_ref[:, z * 2 + e, 256:384] = turned[z * 64 : (z + 1) * 64, :]
        turn[3 * Q : 256, :] = jnp.zeros((256 - 3 * Q, 256), F32)
        for c in range(3):
            turn[c * Q : (c + 1) * Q, :] = x[e * 3 + c, 0:Q, :]
        turned = turn[...].T
        for z in range(4):
            out_ref[:, z * 2 + e, 0:256] = turned[z * 64 : (z + 1) * 64, :]


def steps(place, metric, points, inverse, fwd, back):
    return pl.pallas_call(
        steps_kernel,
        out_shape=jax.ShapeDtypeStruct((64, 8, 384), F32),
        in_specs=[smem_spec(), smem_spec()] + [vmem_spec()] * (len(inverse) + 4),
        out_specs=vmem_spec(),
        scratch_shapes=[
            pltpu.VMEM((2, 64 * 128, 128), F32),
            pltpu.VMEM((2, QP, 128), F32),
            pltpu.VMEM((6, QP, 256), F32),
            pltpu.VMEM((2, 2, 3, QP, 256), F32),
            pltpu.VMEM((2, 6 * QP, 128), F32),
            pltpu.VMEM((6, QP, 256), F32),
            pltpu.VMEM((2, 128, 256), F32),
            pltpu.VMEM((256, 256), F32),
        ],
        compiler_params=params(),
    )(place, metric, points, *inverse, fwd, back, slope_table())


def wall_kernel(r_ref, local_ref, element_ref, o_ref):
    points = local_ref.shape[1]
    mode = lax.broadcasted_iota(jnp.int32, (128, points), 0)
    pick = jnp.where(mode == local_ref[...], 1.0, 0.0).astype(jnp.bfloat16)
    here = mode == element_ref[...]
    for z in range(4):
        field = jnp.concatenate([r_ref[:, z * 2, :], r_ref[:, z * 2 + 1, :]], axis=0)
        high = field.astype(jnp.bfloat16)
        rest = field - high.astype(F32)
        middle = rest.astype(jnp.bfloat16)
        low = (rest - middle.astype(F32)).astype(jnp.bfloat16)
        values = (
            jnp.dot(low, pick, preferred_element_type=F32)
            + jnp.dot(middle, pick, preferred_element_type=F32)
            + jnp.dot(high, pick, preferred_element_type=F32)
        )
        total = jnp.sum(jnp.where(here, values, 0.0), axis=0, keepdims=True)
        o_ref[z : z + 1, :] = total[:, 0 : points // 2] + total[:, points // 2 :]


def wall_sums(received, local, element):
    return pl.pallas_call(
        wall_kernel,
        out_shape=jax.ShapeDtypeStruct((4, local.shape[1] // 2), F32),
        grid=(1,),
        in_specs=[
            pl.BlockSpec((64, 8, 128), lambda i: (0, 0, 2)),
            pl.BlockSpec(local.shape, lambda i: (0, 0)),
            pl.BlockSpec(element.shape, lambda i: (0, 0)),
        ],
        out_specs=pl.BlockSpec((4, local.shape[1] // 2), lambda i: (0, 0)),
        compiler_params=params(),
    )(received, local, element)


def unpack_kernel(r_ref, o_ref, t_ref):
    for z in range(4):
        stack = jnp.concatenate([r_ref[:, z * 2, :], r_ref[:, z * 2 + 1, :]], axis=0)
        t_ref[z] = stack.T
        for c in range(3):
            o_ref[c, z] = t_ref[z, c * Q : (c + 1) * Q, :]


def unpack(received):
    return pl.pallas_call(
        unpack_kernel,
        out_shape=jax.ShapeDtypeStruct((3, 4, Q, 128), F32),
        grid=(1,),
        in_specs=[pl.BlockSpec((64, 8, 256), lambda i: (0, 0, 0))],
        out_specs=pl.BlockSpec((3, 4, Q, 128), lambda i: (0, 0, 0, 0)),
        scratch_shapes=[pltpu.VMEM((4, 256, 128), F32)],
        compiler_params=params(),
    )(received)


def on_device(
    adjoint,
    checkpoints,
    checkpoint_step,
    metric,
    helmholtz_inverse,
    wall_element,
    wall_local,
    wall_weight,
):
    span = lax.axis_index("span")
    plane = lax.axis_index("plane")
    span_count = lax.axis_size("span")
    plane_count = lax.axis_size("plane")
    wall_count = wall_element.shape[0]
    core = span % 2
    place = jnp.stack([span, core]).astype(jnp.int32)
    fwd, back = transforms(core, plane)

    def around(block, step):
        return lax.ppermute(
            block, "plane", [(i, (i + step) % plane_count) for i in range(plane_count)]
        )

    def across(block):
        return lax.ppermute(block, "span", [(i, i ^ 1) for i in range(span_count)])

    matrix = lax.dynamic_index_in_dim(helmholtz_inverse, plane, 0, keepdims=False)
    every = lax.all_to_all(pack_inverse(matrix, span_count), "span", 0, 0, tiled=True)
    sent = pack_points(adjoint, checkpoints, checkpoint_step)
    every, sent = lax.optimization_barrier((every, sent))
    mine = lax.dynamic_index_in_dim(
        every.reshape(span_count // 2, 2, 32, 128), core, 1, keepdims=False
    )
    left = around(mine, 1)
    right = around(mine, 3)
    oa = around(left[:16], 1)
    ob = around(right[16:], 3)
    inverse = (every, left, across(left), right, across(right), oa, across(oa), ob, across(ob))
    points = lax.all_to_all(sent, "span", 0, 0, tiled=True)
    out = steps(place, metric, points, inverse, fwd, back)
    received = lax.all_to_all(out, "span", 0, 0, tiled=True)

    local = wall_local.T.reshape(1, 2 * wall_count)
    element = wall_element.T.reshape(1, 2 * wall_count) - plane * adjoint.shape[3]
    partial_sum = wall_sums(received, local, element)
    gradient = partial_sum
    for k in range(1, plane_count):
        gradient = gradient + lax.ppermute(
            partial_sum, "plane", [(i, (i + k) % plane_count) for i in range(plane_count)]
        )
    weighted = wall_weight * gradient
    square = jnp.sum(weighted * weighted)
    squares = lax.all_to_all(
        jnp.broadcast_to(square, (span_count, 1, 128)), "span", 0, 0, tiled=True
    )
    total = jnp.sum(squares[:, 0, 0])
    share_width = wall_count // plane_count
    share = lax.dynamic_slice_in_dim(weighted, plane * share_width, share_width, 1)
    inverse_rms = lax.rsqrt(total / (adjoint.shape[1] * span_count * wall_count) + 1e-06)
    return (unpack(received), share * inverse_rms)


def solution(mesh):
    placed = (
        P(None, "span", None, "plane"),
        P(None, None, "span", None, "plane"),
        P(),
        P(None, "plane"),
        P("span", None, None),
        P(),
        P(),
        P("span", None),
    )
    return jax.shard_map(
        on_device,
        mesh=mesh,
        in_specs=placed,
        out_specs=(P(None, "span", None, "plane"), P("span", "plane")),
        check_vma=False,
    )
```

```python
import jax
import jax.numpy as jnp
import numpy as np
from jax import lax
from jax.experimental import pallas as pl
from jax.experimental.pallas import tpu as pltpu
from jax.sharding import PartitionSpec as P

P_SIZE = 8
Q = 81
QP = 88
NSTEP = 3
HIGHEST = lax.Precision.HIGHEST
F32 = jnp.float32
VMEM_BYTES = 56 * 1024 * 1024
LEVELS = 32767.0
SCALE_LANE = 250


def chebyshev_matrix(degree):
    points = np.arange(degree + 1)
    abscissa = np.cos(np.pi * points / degree)
    signed = np.where((points == 0) | (points == degree), 2.0, 1.0) * (-1.0) ** points
    spacing = abscissa[:, None] - abscissa[None, :] + np.eye(degree + 1)
    matrix = signed[:, None] / signed[None, :] / spacing
    return matrix - np.eye(degree + 1) * np.sum(matrix, axis=1)[:, None]


def fourier_table(length):
    row_index = np.arange(length)[:, None]
    column = np.arange(length)[None, :]
    wavenumber = (row_index + 1) // 2
    phase_angle = 2.0 * np.pi * wavenumber * column / length
    parity = row_index % 2
    base_rows = np.where(
        row_index == 0, 1.0, np.where(parity == 1, np.cos(phase_angle), np.sin(phase_angle))
    )
    row_scale = np.where(
        (row_index == 0) | (row_index == length - 1), 1.0 / np.sqrt(length), np.sqrt(2.0 / length)
    )
    return base_rows * row_scale


def lane_order():
    chips = np.arange(32)
    pieces = []
    for part, shift in ((chips, 0), (chips, 3), (chips, 1), (chips[:16], 2), (chips[16:], 2)):
        for core in range(2):
            pieces.append((part, np.full(part.shape, core), np.full(part.shape, shift)))
    return [np.concatenate([p[k] for p in pieces]).astype(np.int32) for k in range(3)]


def in_two(array):
    high = array.astype(jnp.bfloat16)
    return high, (array - high.astype(F32)).astype(jnp.bfloat16)


def split_table(table):
    high = table.astype(jnp.bfloat16)
    return high, (table - high.astype(np.float64)).astype(jnp.bfloat16)


def transforms(core, plane):
    zl = np.arange(256)
    z_of = 4 * (zl % 64) + zl // 64
    high, low = split_table(fourier_table(256)[:, z_of])
    chip, lane_core, shift = (jnp.asarray(v) for v in lane_order())
    span_of = 2 * chip + lane_core + core * (1 - 2 * lane_core)
    order = 4 * span_of + (plane + shift) % 4
    pick = jnp.where(order[:, None] == jnp.arange(256)[None, :], 1.0, 0.0).astype(jnp.bfloat16)
    both = jnp.asarray(np.concatenate([high, low], axis=1))
    back = jnp.dot(pick, both, preferred_element_type=F32).astype(jnp.bfloat16)
    high, low = back[:, :256], back[:, 256:]
    return (
        jnp.concatenate([high.T, high.T, low.T], axis=0),
        jnp.concatenate([high, high, low], axis=0),
    )


def slope_table():
    d = chebyshev_matrix(P_SIZE)
    eye = np.eye(P_SIZE + 1)
    both = np.zeros((2 * QP, QP), np.float32)
    both[:Q, :Q] = np.kron(d, eye)
    both[QP : QP + Q, :Q] = np.kron(eye, d)
    return jnp.asarray(np.concatenate(split_table(both), axis=0))


def vmem_spec():
    return pl.BlockSpec(memory_space=pltpu.VMEM)


def smem_spec():
    return pl.BlockSpec(memory_space=pltpu.SMEM)


def params():
    return pltpu.CompilerParams(vmem_limit_bytes=VMEM_BYTES)


def pair_up(low, high):
    return (high.astype(jnp.int32) << 16) | (low.astype(jnp.int32) & 0xFFFF)


def scale_code(largest):
    return jnp.floor(jnp.log2(jnp.maximum(largest, 1e-30)) * 2.0**16) + 2.0


def scale_of(code):
    return jnp.exp2(code * 2.0**-16)


def low_of(pair):
    return ((pair << 16) >> 16).astype(F32)


def high_of(pair):
    return (pair >> 16).astype(F32)


def pack_inverse_kernel(h_ref, o_ref, w_ref, f_ref):
    h = h_ref[...]
    largest = jnp.max(jnp.abs(h), axis=1, keepdims=True)
    code = jnp.floor(largest * 2.0**30) + 1.0
    upper = jnp.floor(code * 2.0**-15)
    lower = code - upper * 2.0**15
    w_ref[...] = jnp.zeros_like(w_ref)
    w_ref[0:Q, 0:Q] = jnp.round(h * (LEVELS / (code * 2.0**-30)))
    w_ref[0:Q, Q : Q + 1] = upper
    w_ref[0:Q, Q + 1 : Q + 2] = lower
    turned = w_ref[...].T
    w_ref[...] = turned
    f_ref[...] = jnp.zeros_like(f_ref)
    for r in range(Q):
        line, lane = divmod(r * QP, 128)
        first = min(Q, 128 - lane)
        f_ref[line, lane : lane + first] = w_ref[r, 0:first]
        if first < Q:
            f_ref[line + 1, 0 : Q - first] = w_ref[r, first:Q]
    f_ref[56, 0:Q] = w_ref[Q, 0:Q]
    f_ref[57, 0:Q] = w_ref[Q + 1, 0:Q]
    o_ref[...] = jnp.broadcast_to(pair_up(f_ref[0:32, :], f_ref[32:64, :])[None], o_ref.shape)


def pack_inverse(matrix, targets):
    return pl.pallas_call(
        pack_inverse_kernel,
        out_shape=jax.ShapeDtypeStruct((targets, 32, 128), jnp.int32),
        in_specs=[vmem_spec()],
        out_specs=vmem_spec(),
        scratch_shapes=[pltpu.VMEM((128, 128), F32), pltpu.VMEM((64, 128), F32)],
        compiler_params=params(),
    )(matrix)


def pack_points_kernel(step_ref, adj_ref, c0_ref, c1_ref, c2_ref, o_ref, t_ref):
    stored = (c0_ref, c1_ref, c2_ref)
    lane = lax.broadcasted_iota(jnp.int32, (64, 256), 1)
    for z in range(4):
        for g in range(3):
            t_ref[g, z, 3 * Q : 256, :] = jnp.zeros((256 - 3 * Q, 128), F32)
            for i in range(3):
                if g == 0:
                    block = adj_ref[i, z]
                else:
                    block = stored[i][0, g - 1, z].astype(F32)
                t_ref[g, z, i * Q : (i + 1) * Q, :] = block
            block = t_ref[g, z]
            largest = jnp.max(jnp.max(jnp.abs(block), axis=0, keepdims=True), axis=1, keepdims=True)
            code = jnp.floor(largest * 2.0**27) + 1.0
            turned = jnp.round(block * (LEVELS / (code * 2.0**-27))).T
            pair = pair_up(turned[0:64, :], turned[64:128, :])
            pair = jnp.where(lane == SCALE_LANE, code.astype(jnp.int32), pair)
            if g == 0:
                o_ref[:, z * 2, 0:256] = pair
            elif g == 1:
                o_ref[:, z * 2, 256:384] = pair[:, 0:128]
                o_ref[:, z * 2 + 1, 0:128] = pair[:, 128:256]
            else:
                o_ref[:, z * 2 + 1, 128:384] = pair


def pack_points(adjoint, checkpoints, checkpoint_step):
    def slot(k):
        return pl.BlockSpec((1, 2, 4, Q, 128), lambda i, st: (st[k], 0, 0, 0, 0))

    return pl.pallas_call(
        pack_points_kernel,
        out_shape=jax.ShapeDtypeStruct((64, 8, 384), jnp.int32),
        grid_spec=pltpu.PrefetchScalarGridSpec(
            num_scalar_prefetch=1,
            grid=(1,),
            in_specs=[
                pl.BlockSpec((3, 4, Q, 128), lambda i, st: (0, 0, 0, 0)),
                slot(0),
                slot(1),
                slot(2),
            ],
            out_specs=pl.BlockSpec((64, 8, 384), lambda i, st: (0, 0, 0)),
            scratch_shapes=[pltpu.VMEM((3, 4, 256, 128), F32)],
        ),
        compiler_params=params(),
    )(checkpoint_step, adjoint, checkpoints, checkpoints, checkpoints)


def transform(array, table_ref):
    high, low = in_two(array)
    return jnp.dot(
        jnp.concatenate([high, low, high], axis=1), table_ref[...], preferred_element_type=F32
    )


def steps_kernel(
    place_ref, metric_ref, r_ref, own_ref, own2_ref, left_ref, left2_ref, right_ref, right2_ref,
    oa_ref, oa2_ref, ob_ref, ob2_ref, fwd_ref, back_ref, both_ref,
    out_ref,
    ht, rows, x, v, coef, solved, wall, spread, turn,
):
    chip = place_ref[0]
    lanes = (
        (own_ref, own2_ref, left_ref, left2_ref),
        (right_ref, right2_ref, oa_ref, oa2_ref, ob_ref, ob2_ref),
    )

    def turn_inverse(k, carry):
        row = pl.multiple_of(k * 128, 128)
        for half in range(2):
            pair = jnp.concatenate([ref[:, k, :] for ref in lanes[half]], axis=0).T
            ht[half, pl.ds(row, 128), :] = low_of(pair)
            ht[half, pl.ds(row + 4096, 128), :] = high_of(pair)
        return carry

    lax.fori_loop(0, 32, turn_inverse, 0)
    for half in range(2):
        rows[half] = (
            ht[half, 7168 : 7168 + QP, :] * 2.0**15 + ht[half, 7296 : 7296 + QP, :]
        ) * (2.0**-30 / LEVELS)

    x[...] = jnp.zeros_like(x)
    v[...] = jnp.zeros_like(v)
    for g in range(3):
        stack = []
        for z in range(4):
            if g == 0:
                stack.append(r_ref[:, z * 2, 0:256])
            elif g == 1:
                stack.append(
                    jnp.concatenate(
                        [r_ref[:, z * 2, 256:384], r_ref[:, z * 2 + 1, 0:128]], axis=1
                    )
                )
            else:
                stack.append(r_ref[:, z * 2 + 1, 128:384])
        pair = jnp.concatenate(stack, axis=0).T
        unit = pair[SCALE_LANE : SCALE_LANE + 1, :].astype(F32) * (2.0**-27 / LEVELS)
        for e in range(2):
            spread[...] = (low_of(pair) if e == 0 else high_of(pair)) * unit
            for i in range(3):
                part = spread[i * Q : (i + 1) * Q, :]
                if g == 0:
                    x[e * 3 + i, 0:Q, :] = part
                else:
                    v[(g - 1), e, i, 0:Q, :] = part

    for step in range(NSTEP):
        for e in range(2):
            m0 = metric_ref[0, chip + 64 * e]
            m1 = metric_ref[1, chip + 64 * e]
            for c in range(3):
                field = x[e * 3 + c]
                high, low = in_two(field)
                large = jnp.dot(both_ref[...], high, preferred_element_type=F32)
                small = jnp.dot(both_ref[0 : 2 * QP, :], low, preferred_element_type=F32)
                slopes = large[0 : 2 * QP] + (large[2 * QP : 4 * QP] + small)
                x[e * 3 + c] = (
                    field
                    + v[0, e, step] * (m0 * slopes[0:QP])
                    + v[1, e, step] * (m1 * slopes[QP : 2 * QP])
                )
        modes = transform(x[...].reshape(6 * QP, 256), fwd_ref)
        coef[0] = modes[:, 0:128]
        coef[1] = modes[:, 128:256]
        for half in range(2):
            for e in range(2):

                def column(r, sums, half=half, e=e):
                    h = ht[half, pl.ds(pl.multiple_of(r * QP, 8), QP), :]
                    return tuple(
                        sums[c] + h * coef[half, pl.ds((e * 3 + c) * QP + r, 1), :] for c in range(3)
                    )

                zero = jnp.zeros((QP, 128), F32)
                sums = lax.fori_loop(0, Q, column, (zero, zero, zero), unroll=27)
                for c in range(3):
                    solved[e * 3 + c, :, half * 128 : (half + 1) * 128] = sums[c] * rows[half]
        planes = transform(solved[...].reshape(6 * QP, 256), back_ref)
        x[...] = planes.reshape(6, QP, 256)
        for e in range(2):
            product = x[e * 3 + 1] * v[1, e, step]
            if step == 0:
                wall[e] = product
            else:
                wall[e] = wall[e] + product

    def levels(array):
        largest = jnp.max(jnp.max(jnp.abs(array), axis=0), axis=0, keepdims=True)
        code = scale_code(largest)
        return code.astype(jnp.int32), LEVELS / scale_of(code)

    code, unit = levels(wall[...])
    turn[0:QP, :] = pair_up(jnp.round(wall[0] * unit), jnp.round(wall[1] * unit))
    turn[QP:128, :] = jnp.broadcast_to(code, (128 - QP, 256))
    turned = turn[0:128, :].T
    for z in range(4):
        out_ref[:, z, 256:384] = turned[z * 64 : (z + 1) * 64, :]
    code, unit = levels(x[...])
    for c in range(3):
        turn[c * Q : (c + 1) * Q, :] = pair_up(
            jnp.round(x[c, 0:Q, :] * unit), jnp.round(x[c + 3, 0:Q, :] * unit)
        )
    turn[3 * Q : 256, :] = jnp.broadcast_to(code, (256 - 3 * Q, 256))
    turned = turn[...].T
    for z in range(4):
        out_ref[:, z, 0:256] = turned[z * 64 : (z + 1) * 64, :]


def steps(place, metric, points, inverse, fwd, back):
    return pl.pallas_call(
        steps_kernel,
        out_shape=jax.ShapeDtypeStruct((64, 4, 384), jnp.int32),
        in_specs=[smem_spec(), smem_spec()] + [vmem_spec()] * (len(inverse) + 4),
        out_specs=vmem_spec(),
        scratch_shapes=[
            pltpu.VMEM((2, 64 * 128, 128), F32),
            pltpu.VMEM((2, QP, 128), F32),
            pltpu.VMEM((6, QP, 256), F32),
            pltpu.VMEM((2, 2, 3, QP, 256), F32),
            pltpu.VMEM((2, 6 * QP, 128), F32),
            pltpu.VMEM((6, QP, 256), F32),
            pltpu.VMEM((2, QP, 256), F32),
            pltpu.VMEM((256, 256), F32),
            pltpu.VMEM((256, 256), jnp.int32),
        ],
        compiler_params=params(),
    )(place, metric, points, *inverse, fwd, back, slope_table())


def wall_kernel(r_ref, local_ref, element_ref, o_ref):
    points = local_ref.shape[1]
    mode = lax.broadcasted_iota(jnp.int32, (128, points), 0)
    pick = jnp.where(mode == local_ref[...], 1.0, 0.0).astype(jnp.bfloat16)
    here = mode == element_ref[...]
    for z in range(4):
        pair = r_ref[:, z, :]
        unit = scale_of(pair[:, QP : QP + 1].astype(F32)) * (1.0 / LEVELS)
        field = jnp.concatenate([low_of(pair) * unit, high_of(pair) * unit], axis=0)
        high, low = in_two(field)
        values = jnp.dot(low, pick, preferred_element_type=F32) + jnp.dot(
            high, pick, preferred_element_type=F32
        )
        total = jnp.sum(jnp.where(here, values, 0.0), axis=0, keepdims=True)
        o_ref[z : z + 1, :] = total[:, 0 : points // 2] + total[:, points // 2 :]


def wall_sums(received, local, element):
    return pl.pallas_call(
        wall_kernel,
        out_shape=jax.ShapeDtypeStruct((4, local.shape[1] // 2), F32),
        grid=(1,),
        in_specs=[
            pl.BlockSpec((64, 4, 128), lambda i: (0, 0, 2)),
            pl.BlockSpec(local.shape, lambda i: (0, 0)),
            pl.BlockSpec(element.shape, lambda i: (0, 0)),
        ],
        out_specs=pl.BlockSpec((4, local.shape[1] // 2), lambda i: (0, 0)),
        compiler_params=params(),
    )(received, local, element)


def weigh_kernel(weight_ref, p0_ref, p1_ref, p2_ref, p3_ref, weighted_ref, square_ref):
    weighted = weight_ref[...] * ((p0_ref[...] + p1_ref[...]) + (p2_ref[...] + p3_ref[...]))
    weighted_ref[...] = weighted
    square = jnp.sum(jnp.sum(weighted * weighted, axis=0, keepdims=True), axis=1, keepdims=True)
    square_ref[...] = jnp.broadcast_to(square.reshape(1, 1, 1), square_ref.shape)


def weigh(weight, parts, targets):
    return pl.pallas_call(
        weigh_kernel,
        out_shape=(
            jax.ShapeDtypeStruct(weight.shape, F32),
            jax.ShapeDtypeStruct((targets, 1, 128), F32),
        ),
        in_specs=[vmem_spec()] * 5,
        out_specs=(vmem_spec(), vmem_spec()),
        compiler_params=params(),
    )(weight, *parts)


def unpack_kernel(r_ref, o_ref, t_ref):
    for z in range(4):
        pair = r_ref[:, z, :].T
        unit = scale_of(pair[SCALE_LANE : SCALE_LANE + 1, :].astype(F32)) * (1.0 / LEVELS)
        t_ref[z] = jnp.concatenate([low_of(pair) * unit, high_of(pair) * unit], axis=1)
        for c in range(3):
            o_ref[c, z] = t_ref[z, c * Q : (c + 1) * Q, :]


def unpack(received):
    return pl.pallas_call(
        unpack_kernel,
        out_shape=jax.ShapeDtypeStruct((3, 4, Q, 128), F32),
        grid=(1,),
        in_specs=[pl.BlockSpec((64, 4, 256), lambda i: (0, 0, 0))],
        out_specs=pl.BlockSpec((3, 4, Q, 128), lambda i: (0, 0, 0, 0)),
        scratch_shapes=[pltpu.VMEM((4, 256, 128), F32)],
        compiler_params=params(),
    )(received)


def on_device(
    adjoint,
    checkpoints,
    checkpoint_step,
    metric,
    helmholtz_inverse,
    wall_element,
    wall_local,
    wall_weight,
):
    span = lax.axis_index("span")
    plane = lax.axis_index("plane")
    span_count = lax.axis_size("span")
    plane_count = lax.axis_size("plane")
    wall_count = wall_element.shape[0]
    core = span % 2
    place = jnp.stack([span, core]).astype(jnp.int32)
    fwd, back = transforms(core, plane)

    def around(block, step):
        return lax.ppermute(
            block, "plane", [(i, (i + step) % plane_count) for i in range(plane_count)]
        )

    def across(block):
        return lax.ppermute(block, "span", [(i, i ^ 1) for i in range(span_count)])

    matrix = lax.dynamic_index_in_dim(helmholtz_inverse, plane, 0, keepdims=False)
    same_core = [list(range(c, span_count, 2)) for c in range(2)]
    own = lax.all_to_all(
        pack_inverse(matrix, span_count // 2), "span", 0, 0, tiled=True, axis_index_groups=same_core
    )
    local = wall_local.T.reshape(1, 2 * wall_count)
    element = wall_element.T.reshape(1, 2 * wall_count) - plane * adjoint.shape[3]
    sent = pack_points(adjoint, checkpoints, checkpoint_step)
    own, sent, local, element = lax.optimization_barrier((own, sent, local, element))
    left = around(own, 1)
    right = around(own, 3)
    oa = around(left[:16], 1)
    ob = around(right[16:], 3)
    inverse = []
    for piece in (own, left, right, oa, ob):
        inverse += [piece, across(piece)]
    points = lax.all_to_all(sent, "span", 0, 0, tiled=True)
    out = steps(place, metric, points, inverse, fwd, back)
    received = lax.all_to_all(out, "span", 0, 0, tiled=True)

    partial_sum = wall_sums(received, local, element)
    parts = [partial_sum] + [around(partial_sum, k) for k in range(1, plane_count)]
    weighted, square = weigh(wall_weight, parts, span_count)
    squares = lax.all_to_all(square, "span", 0, 0, tiled=True)
    total = jnp.sum(squares[:, 0, 0])
    share_width = wall_count // plane_count
    share = lax.dynamic_slice_in_dim(weighted, plane * share_width, share_width, 1)
    inverse_rms = lax.rsqrt(total / (adjoint.shape[1] * span_count * wall_count) + 1e-06)
    return (unpack(received), share * inverse_rms)


def solution(mesh):
    placed = (
        P(None, "span", None, "plane"),
        P(None, None, "span", None, "plane"),
        P(),
        P(None, "plane"),
        P("span", None, None),
        P(),
        P(),
        P("span", None),
    )
    return jax.shard_map(
        on_device,
        mesh=mesh,
        in_specs=placed,
        out_specs=(P(None, "span", None, "plane"), P("span", "plane")),
        check_vma=False,
    )
```

```python
import functools

import jax
import jax.numpy as jnp
import numpy as np
from jax import lax
from jax.experimental import pallas as pl
from jax.experimental.pallas import tpu as pltpu
from jax.sharding import PartitionSpec as P

P_SIZE = 8
Q = 81
QP = 88
NSTEP = 3
HIGHEST = lax.Precision.HIGHEST
F32 = jnp.float32
VMEM_BYTES = 56 * 1024 * 1024
LEVELS = 32767.0
SCALE_LANE = 250
LINES = 58


def chebyshev_matrix(degree):
    points = np.arange(degree + 1)
    abscissa = np.cos(np.pi * points / degree)
    signed = np.where((points == 0) | (points == degree), 2.0, 1.0) * (-1.0) ** points
    spacing = abscissa[:, None] - abscissa[None, :] + np.eye(degree + 1)
    matrix = signed[:, None] / signed[None, :] / spacing
    return matrix - np.eye(degree + 1) * np.sum(matrix, axis=1)[:, None]


def fourier_table(length):
    row_index = np.arange(length)[:, None]
    column = np.arange(length)[None, :]
    wavenumber = (row_index + 1) // 2
    phase_angle = 2.0 * np.pi * wavenumber * column / length
    parity = row_index % 2
    base_rows = np.where(
        row_index == 0, 1.0, np.where(parity == 1, np.cos(phase_angle), np.sin(phase_angle))
    )
    row_scale = np.where(
        (row_index == 0) | (row_index == length - 1), 1.0 / np.sqrt(length), np.sqrt(2.0 / length)
    )
    return base_rows * row_scale


def lane_order():
    chips = np.arange(32)
    pieces = []
    for part, shift in ((chips, 0), (chips, 3), (chips, 1), (chips[:16], 2), (chips[16:], 2)):
        for core in range(2):
            pieces.append((part, np.full(part.shape, core), np.full(part.shape, shift)))
    return [np.concatenate([p[k] for p in pieces]).astype(np.int32) for k in range(3)]


def in_two(array):
    high = array.astype(jnp.bfloat16)
    return high, (array - high.astype(F32)).astype(jnp.bfloat16)


def split_table(table):
    high = table.astype(jnp.bfloat16)
    return high, (table - high.astype(np.float64)).astype(jnp.bfloat16)


def transforms(core, plane):
    zl = np.arange(256)
    z_of = 4 * (zl % 64) + zl // 64
    high, low = split_table(fourier_table(256)[:, z_of])
    chip, lane_core, shift = (jnp.asarray(v) for v in lane_order())
    span_of = 2 * chip + lane_core + core * (1 - 2 * lane_core)
    order = 4 * span_of + (plane + shift) % 4
    pick = jnp.where(order[:, None] == jnp.arange(256)[None, :], 1.0, 0.0).astype(jnp.bfloat16)
    both = jnp.asarray(np.concatenate([high, low], axis=1))
    back = jnp.dot(pick, both, preferred_element_type=F32).astype(jnp.bfloat16)
    high, low = back[:, :256], back[:, 256:]
    return (
        jnp.concatenate([high.T, high.T, low.T], axis=0),
        jnp.concatenate([high, high, low], axis=0),
    )


def slope_table():
    d = chebyshev_matrix(P_SIZE)
    eye = np.eye(P_SIZE + 1)
    both = np.zeros((2 * QP, QP), np.float32)
    both[:Q, :Q] = np.kron(d, eye)
    both[QP : QP + Q, :Q] = np.kron(eye, d)
    return jnp.asarray(np.concatenate(split_table(both), axis=0))


def vmem_spec():
    return pl.BlockSpec(memory_space=pltpu.VMEM)


def smem_spec():
    return pl.BlockSpec(memory_space=pltpu.SMEM)


def params():
    return pltpu.CompilerParams(vmem_limit_bytes=VMEM_BYTES)


def pair_up(low, high):
    return (high.astype(jnp.int32) << 16) | (low.astype(jnp.int32) & 0xFFFF)


def scale_code(largest):
    return jnp.floor(jnp.log2(jnp.maximum(largest, 1e-30)) * 2.0**16) + 2.0


def scale_of(code):
    return jnp.exp2(code * 2.0**-16)


def low_of(pair):
    return ((pair << 16) >> 16).astype(F32)


def high_of(pair):
    return (pair >> 16).astype(F32)


def pack_inverse_kernel(h_ref, o_ref, w_ref, f_ref):
    h = h_ref[...]
    largest = jnp.max(jnp.abs(h), axis=1, keepdims=True)
    code = jnp.floor(largest * 2.0**30) + 1.0
    upper = jnp.floor(code * 2.0**-15)
    lower = code - upper * 2.0**15
    w_ref[...] = jnp.zeros_like(w_ref)
    w_ref[0:Q, 0:Q] = jnp.round(h * (LEVELS / (code * 2.0**-30)))
    w_ref[0:Q, Q : Q + 1] = upper
    w_ref[0:Q, Q + 1 : Q + 2] = lower
    turned = w_ref[...].T
    w_ref[...] = turned
    f_ref[...] = jnp.zeros_like(f_ref)
    for k in range(16):
        line, lane = divmod(k * QP, 128)
        count = (Q - k + 15) // 16
        block = w_ref[pl.ds(k, count, stride=16), :]
        if lane:
            block = jnp.roll(block, lane, axis=1)
        place = lax.broadcasted_iota(jnp.int32, (count, 128), 1)
        here = pl.ds(line, count, stride=11)
        f_ref[here, :] = f_ref[here, :] + jnp.where(place >= lane, block, 0.0)
        if lane + Q > 128:
            after = pl.ds(line + 1, count, stride=11)
            f_ref[after, :] = f_ref[after, :] + jnp.where(place < lane, block, 0.0)
    f_ref[56, 0:Q] = w_ref[Q, 0:Q]
    f_ref[57, 0:Q] = w_ref[Q + 1, 0:Q]
    o_ref[...] = jnp.broadcast_to(pair_up(f_ref[0:32, :], f_ref[32:64, :])[None], o_ref.shape)


def pack_inverse(matrix, targets):
    return pl.pallas_call(
        pack_inverse_kernel,
        out_shape=jax.ShapeDtypeStruct((targets, 32, 128), jnp.int32),
        in_specs=[vmem_spec()],
        out_specs=vmem_spec(),
        scratch_shapes=[pltpu.VMEM((128, 128), F32), pltpu.VMEM((64, 128), F32)],
        compiler_params=params(),
    )(matrix)


def pack_points_kernel(step_ref, adj_ref, c0_ref, c1_ref, c2_ref, o_ref, t_ref):
    stored = (c0_ref, c1_ref, c2_ref)
    lane = lax.broadcasted_iota(jnp.int32, (64, 256), 1)
    for z in range(4):
        for g in range(3):
            t_ref[g, z, 3 * Q : 256, :] = jnp.zeros((256 - 3 * Q, 128), F32)
            for i in range(3):
                if g == 0:
                    block = adj_ref[i, z]
                else:
                    block = stored[i][0, g - 1, z].astype(F32)
                t_ref[g, z, i * Q : (i + 1) * Q, :] = block
            block = t_ref[g, z]
            largest = jnp.max(jnp.max(jnp.abs(block), axis=0, keepdims=True), axis=1, keepdims=True)
            code = jnp.floor(largest * 2.0**27) + 1.0
            turned = jnp.round(block * (LEVELS / (code * 2.0**-27))).T
            pair = pair_up(turned[0:64, :], turned[64:128, :])
            pair = jnp.where(lane == SCALE_LANE, code.astype(jnp.int32), pair)
            if g == 0:
                o_ref[:, z * 2, 0:256] = pair
            elif g == 1:
                o_ref[:, z * 2, 256:384] = pair[:, 0:128]
                o_ref[:, z * 2 + 1, 0:128] = pair[:, 128:256]
            else:
                o_ref[:, z * 2 + 1, 128:384] = pair


def pack_points(adjoint, checkpoints, checkpoint_step):
    def slot(k):
        return pl.BlockSpec((1, 2, 4, Q, 128), lambda i, st: (st[k], 0, 0, 0, 0))

    return pl.pallas_call(
        pack_points_kernel,
        out_shape=jax.ShapeDtypeStruct((64, 8, 384), jnp.int32),
        grid_spec=pltpu.PrefetchScalarGridSpec(
            num_scalar_prefetch=1,
            grid=(1,),
            in_specs=[
                pl.BlockSpec((3, 4, Q, 128), lambda i, st: (0, 0, 0, 0)),
                slot(0),
                slot(1),
                slot(2),
            ],
            out_specs=pl.BlockSpec((64, 8, 384), lambda i, st: (0, 0, 0)),
            scratch_shapes=[pltpu.VMEM((3, 4, 256, 128), F32)],
        ),
        compiler_params=params(),
    )(checkpoint_step, adjoint, checkpoints, checkpoints, checkpoints)


def transform(array, table_ref):
    high, low = in_two(array)
    return jnp.dot(
        jnp.concatenate([high, low, high], axis=1), table_ref[...], preferred_element_type=F32
    )


def turn_pieces(pieces, write):
    def lines(k, both):
        pair = jnp.concatenate([ref[:, k, :] for ref in pieces], axis=0).T
        write(pl.multiple_of(k * 128, 128), low_of(pair))
        if both:
            write(pl.multiple_of(k * 128 + 4096, 128), high_of(pair))

    def both_halves(k, carry):
        lines(k, True)
        return carry

    def low_half(k, carry):
        lines(k, False)
        return carry

    lax.fori_loop(0, LINES - 32, both_halves, 0)
    lax.fori_loop(LINES - 32, 32, low_half, 0)


def turn_kernel(own_ref, own2_ref, o_ref):
    def write(row, block):
        o_ref[pl.ds(row, 128), 0:64] = block

    turn_pieces((own_ref, own2_ref), write)


def turn_own(own, own2):
    return pl.pallas_call(
        turn_kernel,
        out_shape=jax.ShapeDtypeStruct((LINES * 128, 128), F32),
        in_specs=[vmem_spec()] * 2,
        out_specs=vmem_spec(),
        compiler_params=params(),
    )(own, own2)


def advance(place_ref, metric_ref, x, v, step, both_ref, fwd_ref, coef):
    chip = place_ref[0]
    for e in range(2):
        m0 = metric_ref[0, chip + 64 * e]
        m1 = metric_ref[1, chip + 64 * e]
        for c in range(3):
            field = x[e * 3 + c]
            high, low = in_two(field)
            large = jnp.dot(both_ref[...], high, preferred_element_type=F32)
            small = jnp.dot(both_ref[0 : 2 * QP, :], low, preferred_element_type=F32)
            slopes = large[0 : 2 * QP] + (large[2 * QP : 4 * QP] + small)
            x[e * 3 + c] = (
                field
                + v[0, e, step] * (m0 * slopes[0:QP])
                + v[1, e, step] * (m1 * slopes[QP : 2 * QP])
            )
    modes = transform(x[...].reshape(6 * QP, 256), fwd_ref)
    coef[0] = modes[:, 0:128]
    coef[1] = modes[:, 128:256]


def first_kernel(place_ref, metric_ref, r_ref, fwd_ref, both_ref, coef, v, x, spread):
    x[...] = jnp.zeros_like(x)
    v[...] = jnp.zeros_like(v)
    for g in range(3):
        stack = []
        for z in range(4):
            if g == 0:
                stack.append(r_ref[:, z * 2, 0:256])
            elif g == 1:
                stack.append(
                    jnp.concatenate(
                        [r_ref[:, z * 2, 256:384], r_ref[:, z * 2 + 1, 0:128]], axis=1
                    )
                )
            else:
                stack.append(r_ref[:, z * 2 + 1, 128:384])
        pair = jnp.concatenate(stack, axis=0).T
        unit = pair[SCALE_LANE : SCALE_LANE + 1, :].astype(F32) * (2.0**-27 / LEVELS)
        for e in range(2):
            spread[...] = (low_of(pair) if e == 0 else high_of(pair)) * unit
            for i in range(3):
                part = spread[i * Q : (i + 1) * Q, :]
                if g == 0:
                    x[e * 3 + i, 0:Q, :] = part
                else:
                    v[(g - 1), e, i, 0:Q, :] = part
    advance(place_ref, metric_ref, x, v, 0, both_ref, fwd_ref, coef)


def first_modes(place, metric, points, fwd, both):
    return pl.pallas_call(
        first_kernel,
        out_shape=(
            jax.ShapeDtypeStruct((2, 6 * QP, 128), F32),
            jax.ShapeDtypeStruct((2, 2, 3, QP, 256), F32),
        ),
        in_specs=[smem_spec(), smem_spec()] + [vmem_spec()] * 3,
        out_specs=(vmem_spec(), vmem_spec()),
        scratch_shapes=[pltpu.VMEM((6, QP, 256), F32), pltpu.VMEM((256, 256), F32)],
        compiler_params=params(),
    )(place, metric, points, fwd, both)


def steps_kernel(
    place_ref, metric_ref, turned_ref, left_ref, left2_ref, right_ref, right2_ref, oa_ref, oa2_ref, ob_ref, ob2_ref,
    first_ref, v, fwd_ref, back_ref, both_ref,
    out_ref,
    ht, rows, x, coef, solved, wall, turn, sem,
):
    load = pltpu.make_async_copy(turned_ref, ht.at[0], sem)
    load.start()

    def write(row, block):
        ht[1, pl.ds(row, 128), :] = block

    turn_pieces((right_ref, right2_ref, oa_ref, oa2_ref, ob_ref, ob2_ref), write)
    load.wait()

    def write_left(row, block):
        ht[0, pl.ds(row, 128), 64:128] = block

    turn_pieces((left_ref, left2_ref), write_left)
    for half in range(2):
        rows[half] = (
            ht[half, 7168 : 7168 + QP, :] * 2.0**15 + ht[half, 7296 : 7296 + QP, :]
        ) * (2.0**-30 / LEVELS)

    for step in range(NSTEP):
        if step > 0:
            advance(place_ref, metric_ref, x, v, step, both_ref, fwd_ref, coef)
        modes = coef if step > 0 else first_ref
        for half in range(2):
            for e in range(2):

                def column(r, sums, half=half, e=e, modes=modes):
                    h = ht[half, pl.ds(pl.multiple_of(r * QP, 8), QP), :]
                    return tuple(
                        sums[c] + h * modes[half, pl.ds((e * 3 + c) * QP + r, 1), :]
                        for c in range(3)
                    )

                zero = jnp.zeros((QP, 128), F32)
                sums = lax.fori_loop(0, Q, column, (zero, zero, zero), unroll=27)
                for c in range(3):
                    solved[e * 3 + c, :, half * 128 : (half + 1) * 128] = sums[c] * rows[half]
        planes = transform(solved[...].reshape(6 * QP, 256), back_ref)
        x[...] = planes.reshape(6, QP, 256)
        for e in range(2):
            product = x[e * 3 + 1] * v[1, e, step]
            if step == 0:
                wall[e] = product
            else:
                wall[e] = wall[e] + product

    def levels(array):
        largest = jnp.max(jnp.max(jnp.abs(array), axis=0), axis=0, keepdims=True)
        code = scale_code(largest)
        return code.astype(jnp.int32), LEVELS / scale_of(code)

    code, unit = levels(wall[...])
    turn[0:QP, :] = pair_up(jnp.round(wall[0] * unit), jnp.round(wall[1] * unit))
    turn[QP:128, :] = jnp.broadcast_to(code, (128 - QP, 256))
    turned = turn[0:128, :].T
    for z in range(4):
        out_ref[:, z, 256:384] = turned[z * 64 : (z + 1) * 64, :]
    code, unit = levels(x[...])
    for c in range(3):
        turn[c * Q : (c + 1) * Q, :] = pair_up(
            jnp.round(x[c, 0:Q, :] * unit), jnp.round(x[c + 3, 0:Q, :] * unit)
        )
    turn[3 * Q : 256, :] = jnp.broadcast_to(code, (256 - 3 * Q, 256))
    turned = turn[...].T
    for z in range(4):
        out_ref[:, z, 0:256] = turned[z * 64 : (z + 1) * 64, :]


def steps(place, metric, turned, pieces, first, velocity, fwd, back, both):
    return pl.pallas_call(
        steps_kernel,
        out_shape=jax.ShapeDtypeStruct((64, 4, 384), jnp.int32),
        in_specs=[smem_spec(), smem_spec(), pl.BlockSpec(memory_space=pl.ANY)]
        + [vmem_spec()] * (len(pieces) + 5),
        out_specs=vmem_spec(),
        scratch_shapes=[
            pltpu.VMEM((2, LINES * 128, 128), F32),
            pltpu.VMEM((2, QP, 128), F32),
            pltpu.VMEM((6, QP, 256), F32),
            pltpu.VMEM((2, 6 * QP, 128), F32),
            pltpu.VMEM((6, QP, 256), F32),
            pltpu.VMEM((2, QP, 256), F32),
            pltpu.VMEM((256, 256), jnp.int32),
            pltpu.SemaphoreType.DMA,
        ],
        compiler_params=params(),
    )(place, metric, turned, *pieces, first, velocity, fwd, back, both)


def wall_kernel(r_ref, local_ref, element_ref, o_ref):
    points = local_ref.shape[1]
    mode = lax.broadcasted_iota(jnp.int32, (128, points), 0)
    pick = jnp.where(mode == local_ref[...], 1.0, 0.0).astype(jnp.bfloat16)
    here = mode == element_ref[...]
    for z in range(4):
        pair = r_ref[:, z, :]
        unit = scale_of(pair[:, QP : QP + 1].astype(F32)) * (1.0 / LEVELS)
        field = jnp.concatenate([low_of(pair) * unit, high_of(pair) * unit], axis=0)
        high, low = in_two(field)
        values = jnp.dot(low, pick, preferred_element_type=F32) + jnp.dot(
            high, pick, preferred_element_type=F32
        )
        total = jnp.sum(jnp.where(here, values, 0.0), axis=0, keepdims=True)
        o_ref[z : z + 1, :] = total[:, 0 : points // 2] + total[:, points // 2 :]


def wall_sums(received, local, element):
    return pl.pallas_call(
        wall_kernel,
        out_shape=jax.ShapeDtypeStruct((4, local.shape[1] // 2), F32),
        grid=(1,),
        in_specs=[
            pl.BlockSpec((64, 4, 128), lambda i: (0, 0, 2)),
            pl.BlockSpec(local.shape, lambda i: (0, 0)),
            pl.BlockSpec(element.shape, lambda i: (0, 0)),
        ],
        out_specs=pl.BlockSpec((4, local.shape[1] // 2), lambda i: (0, 0)),
        compiler_params=params(),
    )(received, local, element)


def weigh_kernel(weight_ref, p0_ref, p1_ref, p2_ref, p3_ref, weighted_ref, square_ref):
    weighted = weight_ref[...] * ((p0_ref[...] + p1_ref[...]) + (p2_ref[...] + p3_ref[...]))
    weighted_ref[...] = weighted
    square = jnp.sum(jnp.sum(weighted * weighted, axis=0, keepdims=True), axis=1, keepdims=True)
    square_ref[...] = jnp.broadcast_to(square.reshape(1, 1, 1), square_ref.shape)


def weigh(weight, parts, targets):
    return pl.pallas_call(
        weigh_kernel,
        out_shape=(
            jax.ShapeDtypeStruct(weight.shape, F32),
            jax.ShapeDtypeStruct((targets, 1, 128), F32),
        ),
        in_specs=[vmem_spec()] * 5,
        out_specs=(vmem_spec(), vmem_spec()),
        compiler_params=params(),
    )(weight, *parts)


def share_kernel(plane_ref, weighted_ref, squares_ref, o_ref, *, entries):
    width = o_ref.shape[1]
    total = jnp.sum(squares_ref[:, 0, :], axis=0, keepdims=True)[:, 0:1]
    start = pl.multiple_of(plane_ref[0] * width, 128)
    o_ref[...] = weighted_ref[:, pl.ds(start, width)] * lax.rsqrt(total * (1.0 / entries) + 1e-06)


def share(plane, weighted, squares, width, entries):
    return pl.pallas_call(
        functools.partial(share_kernel, entries=entries),
        out_shape=jax.ShapeDtypeStruct((weighted.shape[0], width), F32),
        in_specs=[smem_spec(), vmem_spec(), vmem_spec()],
        out_specs=vmem_spec(),
        compiler_params=params(),
    )(plane, weighted, squares)


def unpack_kernel(r_ref, o_ref, t_ref):
    for z in range(4):
        pair = r_ref[:, z, :].T
        unit = scale_of(pair[SCALE_LANE : SCALE_LANE + 1, :].astype(F32)) * (1.0 / LEVELS)
        t_ref[z] = jnp.concatenate([low_of(pair) * unit, high_of(pair) * unit], axis=1)
        for c in range(3):
            o_ref[c, z] = t_ref[z, c * Q : (c + 1) * Q, :]


def unpack(received):
    return pl.pallas_call(
        unpack_kernel,
        out_shape=jax.ShapeDtypeStruct((3, 4, Q, 128), F32),
        grid=(1,),
        in_specs=[pl.BlockSpec((64, 4, 256), lambda i: (0, 0, 0))],
        out_specs=pl.BlockSpec((3, 4, Q, 128), lambda i: (0, 0, 0, 0)),
        scratch_shapes=[pltpu.VMEM((4, 256, 128), F32)],
        compiler_params=params(),
    )(received)


def on_device(
    adjoint,
    checkpoints,
    checkpoint_step,
    metric,
    helmholtz_inverse,
    wall_element,
    wall_local,
    wall_weight,
):
    span = lax.axis_index("span")
    plane = lax.axis_index("plane")
    span_count = lax.axis_size("span")
    plane_count = lax.axis_size("plane")
    wall_count = wall_element.shape[0]
    core = span % 2
    place = jnp.stack([span, core]).astype(jnp.int32)
    fwd, back = transforms(core, plane)

    def around(block, step):
        return lax.ppermute(
            block, "plane", [(i, (i + step) % plane_count) for i in range(plane_count)]
        )

    def across(block):
        return lax.ppermute(block, "span", [(i, i ^ 1) for i in range(span_count)])

    matrix = lax.dynamic_index_in_dim(helmholtz_inverse, plane, 0, keepdims=False)
    same_core = [list(range(c, span_count, 2)) for c in range(2)]
    own = lax.all_to_all(
        pack_inverse(matrix, span_count // 2), "span", 0, 0, tiled=True, axis_index_groups=same_core
    )
    local = wall_local.T.reshape(1, 2 * wall_count)
    element = wall_element.T.reshape(1, 2 * wall_count) - plane * adjoint.shape[3]
    sent = pack_points(adjoint, checkpoints, checkpoint_step)
    own, sent, local, element = lax.optimization_barrier((own, sent, local, element))
    own2 = across(own)
    left = around(own, 1)
    right = around(own, 3)
    points = lax.all_to_all(sent, "span", 0, 0, tiled=True)
    turned = turn_own(own, own2)
    left, right, turned = lax.optimization_barrier((left, right, turned))
    oa = around(left[:16], 1)
    ob = around(right[16:], 3)
    both = slope_table()
    first, velocity = first_modes(place, metric, points, fwd, both)
    pieces = []
    for piece in (left, right):
        pieces += [piece, across(piece)]
    oa, ob, first = lax.optimization_barrier((oa, ob, first))
    for piece in (oa, ob):
        pieces += [piece, across(piece)]
    out = steps(place, metric, turned, pieces, first, velocity, fwd, back, both)
    received = lax.all_to_all(out, "span", 0, 0, tiled=True)

    partial_sum = wall_sums(received, local, element)
    parts = [partial_sum] + [around(partial_sum, k) for k in range(1, plane_count)]
    weighted, square = weigh(wall_weight, parts, span_count)
    squares = lax.all_to_all(square, "span", 0, 0, tiled=True)
    gradient = share(
        plane.reshape(1).astype(jnp.int32),
        weighted,
        squares,
        wall_count // plane_count,
        adjoint.shape[1] * span_count * wall_count,
    )
    return (unpack(received), gradient)


def solution(mesh):
    placed = (
        P(None, "span", None, "plane"),
        P(None, None, "span", None, "plane"),
        P(),
        P(None, "plane"),
        P("span", None, None),
        P(),
        P(),
        P("span", None),
    )
    return jax.shard_map(
        on_device,
        mesh=mesh,
        in_specs=placed,
        out_specs=(P(None, "span", None, "plane"), P("span", "plane")),
        check_vma=False,
    )
```

```python
import functools

import jax
import jax.numpy as jnp
import numpy as np
from jax import lax
from jax.experimental import pallas as pl
from jax.experimental.pallas import tpu as pltpu
from jax.sharding import PartitionSpec as P

P_SIZE = 8
Q = 81
QP = 88
NSTEP = 3
HIGHEST = lax.Precision.HIGHEST
F32 = jnp.float32
VMEM_BYTES = 56 * 1024 * 1024
LEVELS = 32767.0
SCALE_LANE = 250
LINES = 56


def chebyshev_matrix(degree):
    points = np.arange(degree + 1)
    abscissa = np.cos(np.pi * points / degree)
    signed = np.where((points == 0) | (points == degree), 2.0, 1.0) * (-1.0) ** points
    spacing = abscissa[:, None] - abscissa[None, :] + np.eye(degree + 1)
    matrix = signed[:, None] / signed[None, :] / spacing
    return matrix - np.eye(degree + 1) * np.sum(matrix, axis=1)[:, None]


def fourier_table(length):
    row_index = np.arange(length)[:, None]
    column = np.arange(length)[None, :]
    wavenumber = (row_index + 1) // 2
    phase_angle = 2.0 * np.pi * wavenumber * column / length
    parity = row_index % 2
    base_rows = np.where(
        row_index == 0, 1.0, np.where(parity == 1, np.cos(phase_angle), np.sin(phase_angle))
    )
    row_scale = np.where(
        (row_index == 0) | (row_index == length - 1), 1.0 / np.sqrt(length), np.sqrt(2.0 / length)
    )
    return base_rows * row_scale


def lane_order():
    chips = np.arange(32)
    pieces = []
    for shift in (0, 3, 1, 2):
        for core in range(2):
            pieces.append((chips, np.full(chips.shape, core), np.full(chips.shape, shift)))
    return [np.concatenate([p[k] for p in pieces]).astype(np.int32) for k in range(3)]


def in_two(array):
    high = array.astype(jnp.bfloat16)
    return high, (array - high.astype(F32)).astype(jnp.bfloat16)


def split_table(table):
    high = table.astype(jnp.bfloat16)
    return high, (table - high.astype(np.float64)).astype(jnp.bfloat16)


def transforms(core, plane):
    zl = np.arange(256)
    z_of = 4 * (zl % 64) + zl // 64
    high, low = split_table(fourier_table(256)[:, z_of])
    chip, lane_core, shift = (jnp.asarray(v) for v in lane_order())
    span_of = 2 * chip + lane_core + core * (1 - 2 * lane_core)
    order = 4 * span_of + (plane + shift) % 4
    pick = jnp.where(order[:, None] == jnp.arange(256)[None, :], 1.0, 0.0).astype(jnp.bfloat16)
    both = jnp.asarray(np.concatenate([high, low], axis=1))
    back = jnp.dot(pick, both, preferred_element_type=F32).astype(jnp.bfloat16)
    high, low = back[:, :256], back[:, 256:]
    return (
        jnp.concatenate([high.T, high.T, low.T], axis=0),
        jnp.concatenate([high, high, low], axis=0),
    )


def slope_table():
    d = chebyshev_matrix(P_SIZE)
    eye = np.eye(P_SIZE + 1)
    both = np.zeros((2 * QP, QP), np.float32)
    both[:Q, :Q] = np.kron(d, eye)
    both[QP : QP + Q, :Q] = np.kron(eye, d)
    return jnp.asarray(np.concatenate(split_table(both), axis=0))


def vmem_spec():
    return pl.BlockSpec(memory_space=pltpu.VMEM)


def smem_spec():
    return pl.BlockSpec(memory_space=pltpu.SMEM)


def params():
    return pltpu.CompilerParams(vmem_limit_bytes=VMEM_BYTES)


def pair_up(low, high):
    return (high.astype(jnp.int32) << 16) | (low.astype(jnp.int32) & 0xFFFF)


def scale_code(largest):
    return jnp.floor(jnp.log2(jnp.maximum(largest, 1e-30)) * 2.0**16) + 2.0


def scale_of(code):
    return jnp.exp2(code * 2.0**-16)


def low_of(pair):
    return ((pair << 16) >> 16).astype(F32)


def high_of(pair):
    return (pair >> 16).astype(F32)


def pack_inverse_kernel(h_ref, o_ref, w_ref, f_ref):
    h = h_ref[...]
    largest = jnp.max(jnp.abs(h), axis=1, keepdims=True)
    code = jnp.floor(largest * 2.0**30) + 1.0
    upper = jnp.floor(code * 2.0**-15)
    lower = code - upper * 2.0**15
    w_ref[...] = jnp.zeros_like(w_ref)
    w_ref[0:Q, 0:Q] = jnp.round(h * (LEVELS / (code * 2.0**-30)))
    turned = w_ref[...].T
    w_ref[...] = turned
    w_ref[0:Q, Q : Q + 1] = upper
    w_ref[0:Q, Q + 1 : Q + 2] = lower
    f_ref[...] = jnp.zeros_like(f_ref)
    for k in range(16):
        line, lane = divmod(k * QP, 128)
        count = (Q - k + 15) // 16
        block = w_ref[pl.ds(k, count, stride=16), :]
        if lane:
            block = jnp.roll(block, lane, axis=1)
        place = lax.broadcasted_iota(jnp.int32, (count, 128), 1)
        here = pl.ds(line, count, stride=11)
        f_ref[here, :] = f_ref[here, :] + jnp.where(place >= lane, block, 0.0)
        if lane + QP > 128:
            after = pl.ds(line + 1, count, stride=11)
            f_ref[after, :] = f_ref[after, :] + jnp.where(place < lane, block, 0.0)
    pair = pair_up(f_ref[0:32, :], f_ref[LINES // 2 : LINES // 2 + 32, :])
    o_ref[...] = jnp.broadcast_to(pair[None], o_ref.shape)


def pack_inverse(matrix, targets):
    return pl.pallas_call(
        pack_inverse_kernel,
        out_shape=jax.ShapeDtypeStruct((targets, 32, 128), jnp.int32),
        in_specs=[vmem_spec()],
        out_specs=vmem_spec(),
        scratch_shapes=[pltpu.VMEM((128, 128), F32), pltpu.VMEM((64, 128), F32)],
        compiler_params=params(),
    )(matrix)


def turn_kernel(own_ref, o_ref):
    for g in range(LINES // 8):
        lines = [own_ref[:, 4 * g + b, :] for b in range(4)]
        o_ref[g * 128 : (g + 1) * 128, :] = jnp.concatenate(lines, axis=0).T


def turn_own(own):
    return pl.pallas_call(
        turn_kernel,
        out_shape=jax.ShapeDtypeStruct((LINES // 8 * 128, 128), jnp.int32),
        in_specs=[vmem_spec()],
        out_specs=vmem_spec(),
        compiler_params=params(),
    )(own)


def pack_points_kernel(step_ref, adj_ref, c0_ref, c1_ref, c2_ref, o_ref, t_ref):
    stored = (c0_ref, c1_ref, c2_ref)
    lane = lax.broadcasted_iota(jnp.int32, (64, 256), 1)
    for z in range(4):
        for g in range(3):
            t_ref[g, z, 3 * Q : 256, :] = jnp.zeros((256 - 3 * Q, 128), F32)
            for i in range(3):
                if g == 0:
                    block = adj_ref[i, z]
                else:
                    block = stored[i][0, g - 1, z].astype(F32)
                t_ref[g, z, i * Q : (i + 1) * Q, :] = block
            block = t_ref[g, z]
            largest = jnp.max(jnp.max(jnp.abs(block), axis=0, keepdims=True), axis=1, keepdims=True)
            code = jnp.floor(largest * 2.0**27) + 1.0
            turned = jnp.round(block * (LEVELS / (code * 2.0**-27))).T
            pair = pair_up(turned[0:64, :], turned[64:128, :])
            pair = jnp.where(lane == SCALE_LANE, code.astype(jnp.int32), pair)
            if g == 0:
                o_ref[:, z * 2, 0:256] = pair
            elif g == 1:
                o_ref[:, z * 2, 256:384] = pair[:, 0:128]
                o_ref[:, z * 2 + 1, 0:128] = pair[:, 128:256]
            else:
                o_ref[:, z * 2 + 1, 128:384] = pair


def pack_points(adjoint, checkpoints, checkpoint_step):
    def slot(k):
        return pl.BlockSpec((1, 2, 4, Q, 128), lambda i, st: (st[k], 0, 0, 0, 0))

    return pl.pallas_call(
        pack_points_kernel,
        out_shape=jax.ShapeDtypeStruct((64, 8, 384), jnp.int32),
        grid_spec=pltpu.PrefetchScalarGridSpec(
            num_scalar_prefetch=1,
            grid=(1,),
            in_specs=[
                pl.BlockSpec((3, 4, Q, 128), lambda i, st: (0, 0, 0, 0)),
                slot(0),
                slot(1),
                slot(2),
            ],
            out_specs=pl.BlockSpec((64, 8, 384), lambda i, st: (0, 0, 0)),
            scratch_shapes=[pltpu.VMEM((3, 4, 256, 128), F32)],
        ),
        compiler_params=params(),
    )(checkpoint_step, adjoint, checkpoints, checkpoints, checkpoints)


def transform(array, table_ref):
    high, low = in_two(array)
    return jnp.dot(
        jnp.concatenate([high, low, high], axis=1), table_ref[...], preferred_element_type=F32
    )


def regroup(blocks):
    lane = lax.broadcasted_iota(jnp.int32, blocks[0].shape, 1)

    def exchange(a, b, keep, width):
        return jnp.where(keep, a, pltpu.roll(b, width, 1)), jnp.where(
            keep, pltpu.roll(a, 128 - width, 1), b
        )

    low = lane < 64
    p0, p2 = exchange(blocks[0], blocks[2], low, 64)
    p1, p3 = exchange(blocks[1], blocks[3], low, 64)
    even = (lane & 32) == 0
    p0, p1 = exchange(p0, p1, even, 32)
    p2, p3 = exchange(p2, p3, even, 32)
    return p0, p1, p2, p3


def spread_pieces(pieces, first, last, ht, half):
    def rows(k, carry):
        blocks = regroup([ref[pl.ds(pl.multiple_of((k - f) * 32, 32), 32), :] for ref, f in pieces])
        start = (k >> 2) * 512 + (k & 3) * 32
        for b in range(4):
            row = pl.multiple_of(start + b * 128, 32)
            ht[half, pl.ds(row, 32), :] = low_of(blocks[b])
            row = pl.multiple_of(start + b * 128 + LINES * 64, 32)
            ht[half, pl.ds(row, 32), :] = high_of(blocks[b])
        return carry

    lax.fori_loop(first, last, rows, 0, unroll=2)


def advance(place_ref, metric_ref, x, v, step, both_ref, fwd_ref, coef):
    chip = place_ref[0]
    for e in range(2):
        m0 = metric_ref[0, chip + 64 * e]
        m1 = metric_ref[1, chip + 64 * e]
        for c in range(3):
            field = x[e * 3 + c]
            high, low = in_two(field)
            large = jnp.dot(both_ref[...], high, preferred_element_type=F32)
            small = jnp.dot(both_ref[0 : 2 * QP, :], low, preferred_element_type=F32)
            slopes = large[0 : 2 * QP] + (large[2 * QP : 4 * QP] + small)
            x[e * 3 + c] = (
                field
                + v[0, e, step] * (m0 * slopes[0:QP])
                + v[1, e, step] * (m1 * slopes[QP : 2 * QP])
            )
    modes = transform(x[...].reshape(6 * QP, 256), fwd_ref)
    coef[0] = modes[:, 0:128]
    coef[1] = modes[:, 128:256]


def first_kernel(place_ref, metric_ref, r_ref, fwd_ref, both_ref, coef, v, x, spread):
    x[...] = jnp.zeros_like(x)
    v[...] = jnp.zeros_like(v)
    for g in range(3):
        stack = []
        for z in range(4):
            if g == 0:
                stack.append(r_ref[:, z * 2, 0:256])
            elif g == 1:
                stack.append(
                    jnp.concatenate(
                        [r_ref[:, z * 2, 256:384], r_ref[:, z * 2 + 1, 0:128]], axis=1
                    )
                )
            else:
                stack.append(r_ref[:, z * 2 + 1, 128:384])
        pair = jnp.concatenate(stack, axis=0).T
        unit = pair[SCALE_LANE : SCALE_LANE + 1, :].astype(F32) * (2.0**-27 / LEVELS)
        for e in range(2):
            spread[...] = (low_of(pair) if e == 0 else high_of(pair)) * unit
            for i in range(3):
                part = spread[i * Q : (i + 1) * Q, :]
                if g == 0:
                    x[e * 3 + i, 0:Q, :] = part
                else:
                    v[(g - 1), e, i, 0:Q, :] = part
    advance(place_ref, metric_ref, x, v, 0, both_ref, fwd_ref, coef)


def first_modes(place, metric, points, fwd, both):
    return pl.pallas_call(
        first_kernel,
        out_shape=(
            jax.ShapeDtypeStruct((2, 6 * QP, 128), F32),
            jax.ShapeDtypeStruct((2, 2, 3, QP, 256), F32),
        ),
        in_specs=[smem_spec(), smem_spec()] + [vmem_spec()] * 3,
        out_specs=(vmem_spec(), vmem_spec()),
        scratch_shapes=[pltpu.VMEM((6, QP, 256), F32), pltpu.VMEM((256, 256), F32)],
        compiler_params=params(),
    )(place, metric, points, fwd, both)


def steps_kernel(
    place_ref, metric_ref, own_ref, own2_ref, left_ref, left2_ref, right_ref, right2_ref, oa_ref, oa2_ref, ob_ref, ob2_ref,
    first_ref, v, fwd_ref, back_ref, both_ref,
    out_ref,
    ht, rows, x, coef, solved, wall, turn,
):
    spread_pieces([(r, 0) for r in (own_ref, own2_ref, left_ref, left2_ref)], 0, 28, ht, 0)
    for first, last, oref, oref2 in ((0, 14, oa_ref, oa2_ref), (14, 28, ob_ref, ob2_ref)):
        spread_pieces(
            [(right_ref, 0), (right2_ref, 0), (oref, first), (oref2, first)], first, last, ht, 1
        )
    for half in range(2):
        rows[half] = jnp.zeros((QP, 128), F32)
        rows[half, 0:Q, :] = (
            ht[half, pl.ds(Q, Q, stride=QP), :] * 2.0**15
            + ht[half, pl.ds(Q + 1, Q, stride=QP), :]
        ) * (2.0**-30 / LEVELS)

    for step in range(NSTEP):
        if step > 0:
            advance(place_ref, metric_ref, x, v, step, both_ref, fwd_ref, coef)
        modes = coef if step > 0 else first_ref
        for half in range(2):
            for e in range(2):

                def column(r, sums, half=half, e=e, modes=modes):
                    h = ht[half, pl.ds(pl.multiple_of(r * QP, 8), QP), :]
                    return tuple(
                        sums[c] + h * modes[half, pl.ds((e * 3 + c) * QP + r, 1), :]
                        for c in range(3)
                    )

                zero = jnp.zeros((QP, 128), F32)
                sums = lax.fori_loop(0, Q, column, (zero, zero, zero), unroll=27)
                for c in range(3):
                    solved[e * 3 + c, :, half * 128 : (half + 1) * 128] = sums[c] * rows[half]
        planes = transform(solved[...].reshape(6 * QP, 256), back_ref)
        x[...] = planes.reshape(6, QP, 256)
        for e in range(2):
            product = x[e * 3 + 1] * v[1, e, step]
            if step == 0:
                wall[e] = product
            else:
                wall[e] = wall[e] + product

    def levels(array):
        largest = jnp.max(jnp.max(jnp.abs(array), axis=0), axis=0, keepdims=True)
        code = scale_code(largest)
        return code.astype(jnp.int32), LEVELS / scale_of(code)

    code, unit = levels(wall[...])
    turn[0:QP, :] = pair_up(jnp.round(wall[0] * unit), jnp.round(wall[1] * unit))
    turn[QP:128, :] = jnp.broadcast_to(code, (128 - QP, 256))
    turned = turn[0:128, :].T
    for z in range(4):
        out_ref[:, z, 256:384] = turned[z * 64 : (z + 1) * 64, :]
    code, unit = levels(x[...])
    for c in range(3):
        turn[c * Q : (c + 1) * Q, :] = pair_up(
            jnp.round(x[c, 0:Q, :] * unit), jnp.round(x[c + 3, 0:Q, :] * unit)
        )
    turn[3 * Q : 256, :] = jnp.broadcast_to(code, (256 - 3 * Q, 256))
    turned = turn[...].T
    for z in range(4):
        out_ref[:, z, 0:256] = turned[z * 64 : (z + 1) * 64, :]


def steps(place, metric, pieces, first, velocity, fwd, back, both):
    return pl.pallas_call(
        steps_kernel,
        out_shape=jax.ShapeDtypeStruct((64, 4, 384), jnp.int32),
        in_specs=[smem_spec(), smem_spec()] + [vmem_spec()] * (len(pieces) + 5),
        out_specs=vmem_spec(),
        scratch_shapes=[
            pltpu.VMEM((2, LINES * 128, 128), F32),
            pltpu.VMEM((2, QP, 128), F32),
            pltpu.VMEM((6, QP, 256), F32),
            pltpu.VMEM((2, 6 * QP, 128), F32),
            pltpu.VMEM((6, QP, 256), F32),
            pltpu.VMEM((2, QP, 256), F32),
            pltpu.VMEM((256, 256), jnp.int32),
        ],
        compiler_params=params(),
    )(place, metric, *pieces, first, velocity, fwd, back, both)


def wall_kernel(r_ref, local_ref, element_ref, o_ref):
    points = local_ref.shape[1]
    mode = lax.broadcasted_iota(jnp.int32, (128, points), 0)
    pick = jnp.where(mode == local_ref[...], 1.0, 0.0).astype(jnp.bfloat16)
    here = mode == element_ref[...]
    for z in range(4):
        pair = r_ref[:, z, :]
        unit = scale_of(pair[:, QP : QP + 1].astype(F32)) * (1.0 / LEVELS)
        field = jnp.concatenate([low_of(pair) * unit, high_of(pair) * unit], axis=0)
        high, low = in_two(field)
        values = jnp.dot(low, pick, preferred_element_type=F32) + jnp.dot(
            high, pick, preferred_element_type=F32
        )
        total = jnp.sum(jnp.where(here, values, 0.0), axis=0, keepdims=True)
        o_ref[z : z + 1, :] = total[:, 0 : points // 2] + total[:, points // 2 :]


def wall_sums(received, local, element):
    return pl.pallas_call(
        wall_kernel,
        out_shape=jax.ShapeDtypeStruct((4, local.shape[1] // 2), F32),
        grid=(1,),
        in_specs=[
            pl.BlockSpec((64, 4, 128), lambda i: (0, 0, 2)),
            pl.BlockSpec(local.shape, lambda i: (0, 0)),
            pl.BlockSpec(element.shape, lambda i: (0, 0)),
        ],
        out_specs=pl.BlockSpec((4, local.shape[1] // 2), lambda i: (0, 0)),
        compiler_params=params(),
    )(received, local, element)


def weigh_kernel(weight_ref, p0_ref, p1_ref, p2_ref, p3_ref, weighted_ref, square_ref):
    weighted = weight_ref[...] * ((p0_ref[...] + p1_ref[...]) + (p2_ref[...] + p3_ref[...]))
    weighted_ref[...] = weighted
    square = jnp.sum(jnp.sum(weighted * weighted, axis=0, keepdims=True), axis=1, keepdims=True)
    square_ref[...] = jnp.broadcast_to(square.reshape(1, 1, 1), square_ref.shape)


def weigh(weight, parts, targets):
    return pl.pallas_call(
        weigh_kernel,
        out_shape=(
            jax.ShapeDtypeStruct(weight.shape, F32),
            jax.ShapeDtypeStruct((targets, 1, 128), F32),
        ),
        in_specs=[vmem_spec()] * 5,
        out_specs=(vmem_spec(), vmem_spec()),
        compiler_params=params(),
    )(weight, *parts)


def share_kernel(plane_ref, weighted_ref, squares_ref, o_ref, *, entries):
    width = o_ref.shape[1]
    total = jnp.sum(squares_ref[:, 0, :], axis=0, keepdims=True)[:, 0:1]
    start = pl.multiple_of(plane_ref[0] * width, 128)
    o_ref[...] = weighted_ref[:, pl.ds(start, width)] * lax.rsqrt(total * (1.0 / entries) + 1e-06)


def share(plane, weighted, squares, width, entries):
    return pl.pallas_call(
        functools.partial(share_kernel, entries=entries),
        out_shape=jax.ShapeDtypeStruct((weighted.shape[0], width), F32),
        in_specs=[smem_spec(), vmem_spec(), vmem_spec()],
        out_specs=vmem_spec(),
        compiler_params=params(),
    )(plane, weighted, squares)


def unpack_kernel(r_ref, o_ref, t_ref):
    for z in range(4):
        pair = r_ref[:, z, :].T
        unit = scale_of(pair[SCALE_LANE : SCALE_LANE + 1, :].astype(F32)) * (1.0 / LEVELS)
        t_ref[z] = jnp.concatenate([low_of(pair) * unit, high_of(pair) * unit], axis=1)
        for c in range(3):
            o_ref[c, z] = t_ref[z, c * Q : (c + 1) * Q, :]


def unpack(received):
    return pl.pallas_call(
        unpack_kernel,
        out_shape=jax.ShapeDtypeStruct((3, 4, Q, 128), F32),
        grid=(1,),
        in_specs=[pl.BlockSpec((64, 4, 256), lambda i: (0, 0, 0))],
        out_specs=pl.BlockSpec((3, 4, Q, 128), lambda i: (0, 0, 0, 0)),
        scratch_shapes=[pltpu.VMEM((4, 256, 128), F32)],
        compiler_params=params(),
    )(received)


def on_device(
    adjoint,
    checkpoints,
    checkpoint_step,
    metric,
    helmholtz_inverse,
    wall_element,
    wall_local,
    wall_weight,
):
    span = lax.axis_index("span")
    plane = lax.axis_index("plane")
    span_count = lax.axis_size("span")
    plane_count = lax.axis_size("plane")
    wall_count = wall_element.shape[0]
    core = span % 2
    place = jnp.stack([span, core]).astype(jnp.int32)
    fwd, back = transforms(core, plane)

    def around(block, step):
        return lax.ppermute(
            block, "plane", [(i, (i + step) % plane_count) for i in range(plane_count)]
        )

    def across(block):
        return lax.ppermute(block, "span", [(i, i ^ 1) for i in range(span_count)])

    matrix = lax.dynamic_index_in_dim(helmholtz_inverse, plane, 0, keepdims=False)
    same_core = [list(range(c, span_count, 2)) for c in range(2)]
    own = lax.all_to_all(
        pack_inverse(matrix, span_count // 2), "span", 0, 0, tiled=True, axis_index_groups=same_core
    )
    local = wall_local.T.reshape(1, 2 * wall_count)
    element = wall_element.T.reshape(1, 2 * wall_count) - plane * adjoint.shape[3]
    sent = pack_points(adjoint, checkpoints, checkpoint_step)
    own, sent, local, element = lax.optimization_barrier((own, sent, local, element))
    own = turn_own(own)
    left = around(own, 1)
    right = around(own, 3)
    points = lax.all_to_all(sent, "span", 0, 0, tiled=True)
    oa = around(left[:448], 1)
    ob = around(right[448:], 3)
    both = slope_table()
    first, velocity = first_modes(place, metric, points, fwd, both)
    pieces = []
    for piece in (own, left, right):
        pieces += [piece, across(piece)]
    oa, ob, first = lax.optimization_barrier((oa, ob, first))
    for piece in (oa, ob):
        pieces += [piece, across(piece)]
    out = steps(place, metric, pieces, first, velocity, fwd, back, both)
    received = lax.all_to_all(out, "span", 0, 0, tiled=True)

    partial_sum = wall_sums(received, local, element)
    parts = [partial_sum] + [around(partial_sum, k) for k in range(1, plane_count)]
    weighted, square = weigh(wall_weight, parts, span_count)
    squares = lax.all_to_all(square, "span", 0, 0, tiled=True)
    gradient = share(
        plane.reshape(1).astype(jnp.int32),
        weighted,
        squares,
        wall_count // plane_count,
        adjoint.shape[1] * span_count * wall_count,
    )
    return (unpack(received), gradient)


def solution(mesh):
    placed = (
        P(None, "span", None, "plane"),
        P(None, None, "span", None, "plane"),
        P(),
        P(None, "plane"),
        P("span", None, None),
        P(),
        P(),
        P("span", None),
    )
    return jax.shard_map(
        on_device,
        mesh=mesh,
        in_specs=placed,
        out_specs=(P(None, "span", None, "plane"), P("span", "plane")),
        check_vma=False,
    )
```

```python
import functools

import jax
import jax.numpy as jnp
import numpy as np
from jax import lax
from jax.experimental import pallas as pl
from jax.experimental.pallas import tpu as pltpu
from jax.sharding import PartitionSpec as P

P_SIZE = 8
Q = 81
QP = 88
NSTEP = 3
HIGHEST = lax.Precision.HIGHEST
F32 = jnp.float32
VMEM_BYTES = 56 * 1024 * 1024
LEVELS = 32767.0
SCALE_LANE = 250
LINES = 56


def chebyshev_matrix(degree):
    points = np.arange(degree + 1)
    abscissa = np.cos(np.pi * points / degree)
    signed = np.where((points == 0) | (points == degree), 2.0, 1.0) * (-1.0) ** points
    spacing = abscissa[:, None] - abscissa[None, :] + np.eye(degree + 1)
    matrix = signed[:, None] / signed[None, :] / spacing
    return matrix - np.eye(degree + 1) * np.sum(matrix, axis=1)[:, None]


def fourier_table(length):
    row_index = np.arange(length)[:, None]
    column = np.arange(length)[None, :]
    wavenumber = (row_index + 1) // 2
    phase_angle = 2.0 * np.pi * wavenumber * column / length
    parity = row_index % 2
    base_rows = np.where(
        row_index == 0, 1.0, np.where(parity == 1, np.cos(phase_angle), np.sin(phase_angle))
    )
    row_scale = np.where(
        (row_index == 0) | (row_index == length - 1), 1.0 / np.sqrt(length), np.sqrt(2.0 / length)
    )
    return base_rows * row_scale


def lane_order():
    chips = np.arange(32)
    pieces = []
    for shift in (0, 3, 1, 2):
        for core in range(2):
            pieces.append((chips, np.full(chips.shape, core), np.full(chips.shape, shift)))
    return [np.concatenate([p[k] for p in pieces]).astype(np.int32) for k in range(3)]


def in_two(array):
    high = array.astype(jnp.bfloat16)
    return high, (array - high.astype(F32)).astype(jnp.bfloat16)


def split_table(table):
    high = table.astype(jnp.bfloat16)
    return high, (table - high.astype(np.float64)).astype(jnp.bfloat16)


def transforms(core, plane):
    zl = np.arange(256)
    z_of = 4 * (zl % 64) + zl // 64
    high, low = split_table(fourier_table(256)[:, z_of])
    chip, lane_core, shift = (jnp.asarray(v) for v in lane_order())
    span_of = 2 * chip + lane_core + core * (1 - 2 * lane_core)
    order = 4 * span_of + (plane + shift) % 4
    pick = jnp.where(order[:, None] == jnp.arange(256)[None, :], 1.0, 0.0).astype(jnp.bfloat16)
    both = jnp.asarray(np.concatenate([high, low], axis=1))
    back = jnp.dot(pick, both, preferred_element_type=F32).astype(jnp.bfloat16)
    high, low = back[:, :256], back[:, 256:]
    return (
        jnp.concatenate([high.T, high.T, low.T], axis=0),
        jnp.concatenate([high, high, low], axis=0),
    )


def slope_table():
    d = chebyshev_matrix(P_SIZE)
    eye = np.eye(P_SIZE + 1)
    both = np.zeros((2 * QP, QP), np.float32)
    both[:Q, :Q] = np.kron(d, eye)
    both[QP : QP + Q, :Q] = np.kron(eye, d)
    return jnp.asarray(np.concatenate(split_table(both), axis=0))


def vmem_spec():
    return pl.BlockSpec(memory_space=pltpu.VMEM)


def smem_spec():
    return pl.BlockSpec(memory_space=pltpu.SMEM)


def params():
    return pltpu.CompilerParams(vmem_limit_bytes=VMEM_BYTES)


def pair_up(low, high):
    return (high.astype(jnp.int32) << 16) | (low.astype(jnp.int32) & 0xFFFF)


def scale_code(largest):
    return jnp.floor(jnp.log2(jnp.maximum(largest, 1e-30)) * 2.0**16) + 2.0


def scale_of(code):
    return jnp.exp2(code * 2.0**-16)


def low_of(pair):
    return ((pair << 16) >> 16).astype(F32)


def high_of(pair):
    return (pair >> 16).astype(F32)


def pack_inverse_kernel(h_ref, o_ref, w_ref, f_ref):
    h = h_ref[...]
    largest = jnp.max(jnp.abs(h), axis=1, keepdims=True)
    code = jnp.floor(largest * 2.0**30) + 1.0
    upper = jnp.floor(code * 2.0**-15)
    lower = code - upper * 2.0**15
    w_ref[...] = jnp.zeros_like(w_ref)
    w_ref[0:Q, 0:Q] = jnp.round(h * (LEVELS / (code * 2.0**-30)))
    turned = w_ref[...].T
    w_ref[...] = turned
    w_ref[0:Q, Q : Q + 1] = upper
    w_ref[0:Q, Q + 1 : Q + 2] = lower
    f_ref[...] = jnp.zeros_like(f_ref)
    for k in range(16):
        line, lane = divmod(k * QP, 128)
        count = (Q - k + 15) // 16
        block = w_ref[pl.ds(k, count, stride=16), :]
        if lane:
            block = jnp.roll(block, lane, axis=1)
        place = lax.broadcasted_iota(jnp.int32, (count, 128), 1)
        here = pl.ds(line, count, stride=11)
        f_ref[here, :] = f_ref[here, :] + jnp.where(place >= lane, block, 0.0)
        if lane + QP > 128:
            after = pl.ds(line + 1, count, stride=11)
            f_ref[after, :] = f_ref[after, :] + jnp.where(place < lane, block, 0.0)
    pair = pair_up(f_ref[0:32, :], f_ref[LINES // 2 : LINES // 2 + 32, :])
    o_ref[...] = jnp.broadcast_to(pair[None], o_ref.shape)


def pack_inverse(matrix, targets):
    return pl.pallas_call(
        pack_inverse_kernel,
        out_shape=jax.ShapeDtypeStruct((targets, 32, 128), jnp.int32),
        in_specs=[vmem_spec()],
        out_specs=vmem_spec(),
        scratch_shapes=[pltpu.VMEM((128, 128), F32), pltpu.VMEM((64, 128), F32)],
        compiler_params=params(),
    )(matrix)


def turn_kernel(own_ref, o_ref):
    for g in range(LINES // 8):
        lines = [own_ref[:, 4 * g + b, :] for b in range(4)]
        o_ref[g * 128 : (g + 1) * 128, :] = jnp.concatenate(lines, axis=0).T


def turn_own(own):
    return pl.pallas_call(
        turn_kernel,
        out_shape=jax.ShapeDtypeStruct((LINES // 8 * 128, 128), jnp.int32),
        in_specs=[vmem_spec()],
        out_specs=vmem_spec(),
        compiler_params=params(),
    )(own)


def pack_points_kernel(step_ref, adj_ref, c0_ref, c1_ref, c2_ref, o_ref, t_ref):
    stored = (c0_ref, c1_ref, c2_ref)
    lane = lax.broadcasted_iota(jnp.int32, (64, 256), 1)
    for z in range(4):
        for g in range(3):
            t_ref[g, z, 3 * Q : 256, :] = jnp.zeros((256 - 3 * Q, 128), F32)
            for i in range(3):
                if g == 0:
                    block = adj_ref[i, z]
                else:
                    block = stored[i][0, g - 1, z].astype(F32)
                t_ref[g, z, i * Q : (i + 1) * Q, :] = block
            block = t_ref[g, z]
            largest = jnp.max(jnp.max(jnp.abs(block), axis=0, keepdims=True), axis=1, keepdims=True)
            code = jnp.floor(largest * 2.0**27) + 1.0
            turned = jnp.round(block * (LEVELS / (code * 2.0**-27))).T
            pair = pair_up(turned[0:64, :], turned[64:128, :])
            pair = jnp.where(lane == SCALE_LANE, code.astype(jnp.int32), pair)
            if g == 0:
                o_ref[:, z * 2, 0:256] = pair
            elif g == 1:
                o_ref[:, z * 2, 256:384] = pair[:, 0:128]
                o_ref[:, z * 2 + 1, 0:128] = pair[:, 128:256]
            else:
                o_ref[:, z * 2 + 1, 128:384] = pair


def pack_points(adjoint, checkpoints, checkpoint_step):
    def slot(k):
        return pl.BlockSpec((1, 2, 4, Q, 128), lambda i, st: (st[k], 0, 0, 0, 0))

    return pl.pallas_call(
        pack_points_kernel,
        out_shape=jax.ShapeDtypeStruct((64, 8, 384), jnp.int32),
        grid_spec=pltpu.PrefetchScalarGridSpec(
            num_scalar_prefetch=1,
            grid=(1,),
            in_specs=[
                pl.BlockSpec((3, 4, Q, 128), lambda i, st: (0, 0, 0, 0)),
                slot(0),
                slot(1),
                slot(2),
            ],
            out_specs=pl.BlockSpec((64, 8, 384), lambda i, st: (0, 0, 0)),
            scratch_shapes=[pltpu.VMEM((3, 4, 256, 128), F32)],
        ),
        compiler_params=params(),
    )(checkpoint_step, adjoint, checkpoints, checkpoints, checkpoints)


def transform(array, table_ref):
    high, low = in_two(array)
    return jnp.dot(
        jnp.concatenate([high, low, high], axis=1), table_ref[...], preferred_element_type=F32
    )


def regroup(blocks):
    lane = lax.broadcasted_iota(jnp.int32, blocks[0].shape, 1)

    def exchange(a, b, keep, width):
        return jnp.where(keep, a, pltpu.roll(b, width, 1)), jnp.where(
            keep, pltpu.roll(a, 128 - width, 1), b
        )

    low = lane < 64
    p0, p2 = exchange(blocks[0], blocks[2], low, 64)
    p1, p3 = exchange(blocks[1], blocks[3], low, 64)
    even = (lane & 32) == 0
    p0, p1 = exchange(p0, p1, even, 32)
    p2, p3 = exchange(p2, p3, even, 32)
    return p0, p1, p2, p3


def spread_rows(pieces, k, ht):
    blocks = regroup([ref[pl.ds(pl.multiple_of((k - f) * 32, 32), 32), :] for ref, f in pieces])
    start = (k >> 2) * 512 + (k & 3) * 32
    for b in range(4):
        row = pl.multiple_of(start + b * 128, 32)
        ht[pl.ds(row, 32), :] = low_of(blocks[b])
        row = pl.multiple_of(start + b * 128 + LINES * 64, 32)
        ht[pl.ds(row, 32), :] = high_of(blocks[b])


def row_scales(ht, rows):
    rows[...] = jnp.zeros_like(rows)
    rows[0:Q, :] = (
        ht[pl.ds(Q, Q, stride=QP), :] * 2.0**15 + ht[pl.ds(Q + 1, Q, stride=QP), :]
    ) * (2.0**-30 / LEVELS)


def advance(place_ref, metric_ref, x, v, step, both_ref, fwd_ref, coef):
    chip = place_ref[0]
    for e in range(2):
        m0 = metric_ref[0, chip + 64 * e]
        m1 = metric_ref[1, chip + 64 * e]
        for c in range(3):
            field = x[e * 3 + c]
            high, low = in_two(field)
            large = jnp.dot(both_ref[...], high, preferred_element_type=F32)
            small = jnp.dot(both_ref[0 : 2 * QP, :], low, preferred_element_type=F32)
            slopes = large[0 : 2 * QP] + (large[2 * QP : 4 * QP] + small)
            x[e * 3 + c] = (
                field
                + v[0, e, step] * (m0 * slopes[0:QP])
                + v[1, e, step] * (m1 * slopes[QP : 2 * QP])
            )
    modes = transform(x[...].reshape(6 * QP, 256), fwd_ref)
    coef[0] = modes[:, 0:128]
    coef[1] = modes[:, 128:256]


def first_kernel(place_ref, metric_ref, r_ref, fwd_ref, both_ref, coef, v, x, spread):
    x[...] = jnp.zeros_like(x)
    v[...] = jnp.zeros_like(v)
    for g in range(3):
        stack = []
        for z in range(4):
            if g == 0:
                stack.append(r_ref[:, z * 2, 0:256])
            elif g == 1:
                stack.append(
                    jnp.concatenate(
                        [r_ref[:, z * 2, 256:384], r_ref[:, z * 2 + 1, 0:128]], axis=1
                    )
                )
            else:
                stack.append(r_ref[:, z * 2 + 1, 128:384])
        pair = jnp.concatenate(stack, axis=0).T
        unit = pair[SCALE_LANE : SCALE_LANE + 1, :].astype(F32) * (2.0**-27 / LEVELS)
        for e in range(2):
            spread[...] = (low_of(pair) if e == 0 else high_of(pair)) * unit
            for i in range(3):
                part = spread[i * Q : (i + 1) * Q, :]
                if g == 0:
                    x[e * 3 + i, 0:Q, :] = part
                else:
                    v[(g - 1), e, i, 0:Q, :] = part
    advance(place_ref, metric_ref, x, v, 0, both_ref, fwd_ref, coef)


def first_modes(place, metric, points, fwd, both):
    return pl.pallas_call(
        first_kernel,
        out_shape=(
            jax.ShapeDtypeStruct((2, 6 * QP, 128), F32),
            jax.ShapeDtypeStruct((2, 2, 3, QP, 256), F32),
        ),
        in_specs=[smem_spec(), smem_spec()] + [vmem_spec()] * 3,
        out_specs=(vmem_spec(), vmem_spec()),
        scratch_shapes=[pltpu.VMEM((6, QP, 256), F32), pltpu.VMEM((256, 256), F32)],
        compiler_params=params(),
    )(place, metric, points, fwd, both)


def steps_kernel(
    place_ref, metric_ref, own_ref, own2_ref, left_ref, left2_ref, right_ref, right2_ref, oa_ref, oa2_ref, ob_ref, ob2_ref,
    first_ref, v, fwd_ref, back_ref, both_ref,
    out_ref,
    ht0, ht1, rows0, rows1, x, coef, solved, wall, turn,
):
    halves = (ht0, ht1)
    scales = (rows0, rows1)

    def spread_first(k, carry):
        spread_rows([(r, 0) for r in (own_ref, own2_ref, left_ref, left2_ref)], k, ht0)
        return carry

    def spread_second(e, k):
        far = (oa_ref, oa2_ref) if e == 0 else (ob_ref, ob2_ref)
        spread_rows([(right_ref, 0), (right2_ref, 0), (far[0], 14 * e), (far[1], 14 * e)], k, ht1)

    lax.fori_loop(0, 28, spread_first, 0, unroll=2)
    row_scales(ht0, rows0)

    for step in range(NSTEP):
        if step > 0:
            advance(place_ref, metric_ref, x, v, step, both_ref, fwd_ref, coef)
        modes = coef if step > 0 else first_ref
        for half in range(2):
            for e in range(2):

                def columns(i, sums, half=half, e=e, modes=modes, step=step):
                    for t in range(27):
                        if step == 0 and half == 0 and t % 5 == 0 and t < 25:
                            spread_second(e, jnp.minimum(5 * i + t // 5, 13) + 14 * e)
                        r = i * 27 + t
                        h = halves[half][pl.ds(pl.multiple_of(r * QP, 8), QP), :]
                        sums = tuple(
                            sums[c] + h * modes[half, pl.ds((e * 3 + c) * QP + r, 1), :]
                            for c in range(3)
                        )
                    return sums

                zero = jnp.zeros((QP, 128), F32)
                sums = lax.fori_loop(0, Q // 27, columns, (zero, zero, zero))
                for c in range(3):
                    solved[e * 3 + c, :, half * 128 : (half + 1) * 128] = (
                        sums[c] * scales[half][...]
                    )
            if step == 0 and half == 0:
                row_scales(ht1, rows1)
        planes = transform(solved[...].reshape(6 * QP, 256), back_ref)
        x[...] = planes.reshape(6, QP, 256)
        for e in range(2):
            product = x[e * 3 + 1] * v[1, e, step]
            if step == 0:
                wall[e] = product
            else:
                wall[e] = wall[e] + product

    def levels(array):
        largest = jnp.max(jnp.max(jnp.abs(array), axis=0), axis=0, keepdims=True)
        code = scale_code(largest)
        return code.astype(jnp.int32), LEVELS / scale_of(code)

    code, unit = levels(wall[...])
    turn[0:QP, :] = pair_up(jnp.round(wall[0] * unit), jnp.round(wall[1] * unit))
    turn[QP:128, :] = jnp.broadcast_to(code, (128 - QP, 256))
    turned = turn[0:128, :].T
    for z in range(4):
        out_ref[:, z, 256:384] = turned[z * 64 : (z + 1) * 64, :]
    code, unit = levels(x[...])
    for c in range(3):
        turn[c * Q : (c + 1) * Q, :] = pair_up(
            jnp.round(x[c, 0:Q, :] * unit), jnp.round(x[c + 3, 0:Q, :] * unit)
        )
    turn[3 * Q : 256, :] = jnp.broadcast_to(code, (256 - 3 * Q, 256))
    turned = turn[...].T
    for z in range(4):
        out_ref[:, z, 0:256] = turned[z * 64 : (z + 1) * 64, :]


def steps(place, metric, pieces, first, velocity, fwd, back, both):
    return pl.pallas_call(
        steps_kernel,
        out_shape=jax.ShapeDtypeStruct((64, 4, 384), jnp.int32),
        in_specs=[smem_spec(), smem_spec()] + [vmem_spec()] * (len(pieces) + 5),
        out_specs=vmem_spec(),
        scratch_shapes=[
            pltpu.VMEM((LINES * 128, 128), F32),
            pltpu.VMEM((LINES * 128, 128), F32),
            pltpu.VMEM((QP, 128), F32),
            pltpu.VMEM((QP, 128), F32),
            pltpu.VMEM((6, QP, 256), F32),
            pltpu.VMEM((2, 6 * QP, 128), F32),
            pltpu.VMEM((6, QP, 256), F32),
            pltpu.VMEM((2, QP, 256), F32),
            pltpu.VMEM((256, 256), jnp.int32),
        ],
        compiler_params=params(),
    )(place, metric, *pieces, first, velocity, fwd, back, both)


def wall_kernel(r_ref, local_ref, element_ref, o_ref):
    points = local_ref.shape[1]
    mode = lax.broadcasted_iota(jnp.int32, (128, points), 0)
    pick = jnp.where(mode == local_ref[...], 1.0, 0.0).astype(jnp.bfloat16)
    pick = jnp.concatenate([pick, pick], axis=0)
    here = mode == element_ref[...]
    for z in range(4):
        pair = r_ref[:, z, :]
        unit = scale_of(pair[:, QP : QP + 1].astype(F32)) * (1.0 / LEVELS)
        field = jnp.concatenate([low_of(pair) * unit, high_of(pair) * unit], axis=0)
        high, low = in_two(field)
        values = jnp.dot(
            jnp.concatenate([low, high], axis=1), pick, preferred_element_type=F32
        )
        total = jnp.sum(jnp.where(here, values, 0.0), axis=0, keepdims=True)
        o_ref[z : z + 1, :] = total[:, 0 : points // 2] + total[:, points // 2 :]


def wall_sums(received, local, element):
    return pl.pallas_call(
        wall_kernel,
        out_shape=jax.ShapeDtypeStruct((4, local.shape[1] // 2), F32),
        grid=(1,),
        in_specs=[
            pl.BlockSpec((64, 4, 128), lambda i: (0, 0, 2)),
            pl.BlockSpec(local.shape, lambda i: (0, 0)),
            pl.BlockSpec(element.shape, lambda i: (0, 0)),
        ],
        out_specs=pl.BlockSpec((4, local.shape[1] // 2), lambda i: (0, 0)),
        compiler_params=params(),
    )(received, local, element)


def weigh_kernel(weight_ref, p0_ref, p1_ref, p2_ref, p3_ref, weighted_ref, square_ref):
    weighted = weight_ref[...] * ((p0_ref[...] + p1_ref[...]) + (p2_ref[...] + p3_ref[...]))
    weighted_ref[...] = weighted
    square = jnp.sum(jnp.sum(weighted * weighted, axis=0, keepdims=True), axis=1, keepdims=True)
    square_ref[...] = jnp.broadcast_to(square.reshape(1, 1, 1), square_ref.shape)


def weigh(weight, parts, targets):
    return pl.pallas_call(
        weigh_kernel,
        out_shape=(
            jax.ShapeDtypeStruct(weight.shape, F32),
            jax.ShapeDtypeStruct((targets, 1, 128), F32),
        ),
        in_specs=[vmem_spec()] * 5,
        out_specs=(vmem_spec(), vmem_spec()),
        compiler_params=params(),
    )(weight, *parts)


def share_kernel(plane_ref, weighted_ref, squares_ref, o_ref, *, entries):
    width = o_ref.shape[1]
    total = jnp.sum(squares_ref[:, 0, :], axis=0, keepdims=True)[:, 0:1]
    start = pl.multiple_of(plane_ref[0] * width, 128)
    o_ref[...] = weighted_ref[:, pl.ds(start, width)] * lax.rsqrt(total * (1.0 / entries) + 1e-06)


def share(plane, weighted, squares, width, entries):
    return pl.pallas_call(
        functools.partial(share_kernel, entries=entries),
        out_shape=jax.ShapeDtypeStruct((weighted.shape[0], width), F32),
        in_specs=[smem_spec(), vmem_spec(), vmem_spec()],
        out_specs=vmem_spec(),
        compiler_params=params(),
    )(plane, weighted, squares)


def unpack_kernel(r_ref, o_ref, t_ref):
    for z in range(4):
        pair = r_ref[:, z, :].T
        unit = scale_of(pair[SCALE_LANE : SCALE_LANE + 1, :].astype(F32)) * (1.0 / LEVELS)
        t_ref[z] = jnp.concatenate([low_of(pair) * unit, high_of(pair) * unit], axis=1)
        for c in range(3):
            o_ref[c, z] = t_ref[z, c * Q : (c + 1) * Q, :]


def unpack(received):
    return pl.pallas_call(
        unpack_kernel,
        out_shape=jax.ShapeDtypeStruct((3, 4, Q, 128), F32),
        grid=(1,),
        in_specs=[pl.BlockSpec((64, 4, 256), lambda i: (0, 0, 0))],
        out_specs=pl.BlockSpec((3, 4, Q, 128), lambda i: (0, 0, 0, 0)),
        scratch_shapes=[pltpu.VMEM((4, 256, 128), F32)],
        compiler_params=params(),
    )(received)


def on_device(
    adjoint,
    checkpoints,
    checkpoint_step,
    metric,
    helmholtz_inverse,
    wall_element,
    wall_local,
    wall_weight,
):
    span = lax.axis_index("span")
    plane = lax.axis_index("plane")
    span_count = lax.axis_size("span")
    plane_count = lax.axis_size("plane")
    wall_count = wall_element.shape[0]
    core = span % 2
    place = jnp.stack([span, core]).astype(jnp.int32)
    fwd, back = transforms(core, plane)

    def around(block, step):
        return lax.ppermute(
            block, "plane", [(i, (i + step) % plane_count) for i in range(plane_count)]
        )

    def across(block):
        return lax.ppermute(block, "span", [(i, i ^ 1) for i in range(span_count)])

    matrix = lax.dynamic_index_in_dim(helmholtz_inverse, plane, 0, keepdims=False)
    same_core = [list(range(c, span_count, 2)) for c in range(2)]
    own = lax.all_to_all(
        pack_inverse(matrix, span_count // 2), "span", 0, 0, tiled=True, axis_index_groups=same_core
    )
    local = wall_local.T.reshape(1, 2 * wall_count)
    element = wall_element.T.reshape(1, 2 * wall_count) - plane * adjoint.shape[3]
    sent = pack_points(adjoint, checkpoints, checkpoint_step)
    own, sent, local, element, place, fwd, back = lax.optimization_barrier(
        (own, sent, local, element, place, fwd, back)
    )
    own = turn_own(own)
    left = around(own, 1)
    right = around(own, 3)
    points = lax.all_to_all(sent, "span", 0, 0, tiled=True)
    oa = around(left[:448], 1)
    ob = around(right[448:], 3)
    both = slope_table()
    first, velocity = first_modes(place, metric, points, fwd, both)
    pieces = []
    for piece in (own, left, right):
        pieces += [piece, across(piece)]
    for piece in (oa, ob):
        pieces += [piece, across(piece)]
    out = steps(place, metric, pieces, first, velocity, fwd, back, both)
    received = lax.all_to_all(out, "span", 0, 0, tiled=True)

    partial_sum = wall_sums(received, local, element)
    parts = [partial_sum] + [around(partial_sum, k) for k in range(1, plane_count)]
    weighted, square = weigh(wall_weight, parts, span_count)
    squares = lax.all_to_all(square, "span", 0, 0, tiled=True)
    gradient = share(
        plane.reshape(1).astype(jnp.int32),
        weighted,
        squares,
        wall_count // plane_count,
        adjoint.shape[1] * span_count * wall_count,
    )
    return (unpack(received), gradient)


def solution(mesh):
    placed = (
        P(None, "span", None, "plane"),
        P(None, None, "span", None, "plane"),
        P(),
        P(None, "plane"),
        P("span", None, None),
        P(),
        P(),
        P("span", None),
    )
    return jax.shard_map(
        on_device,
        mesh=mesh,
        in_specs=placed,
        out_specs=(P(None, "span", None, "plane"), P("span", "plane")),
        check_vma=False,
    )
```

```python
import functools

import jax
import jax.numpy as jnp
import numpy as np
from jax import lax
from jax.experimental import pallas as pl
from jax.experimental.pallas import tpu as pltpu
from jax.sharding import PartitionSpec as P

P_SIZE = 8
Q = 81
QP = 88
NSTEP = 3
HIGHEST = lax.Precision.HIGHEST
F32 = jnp.float32
VMEM_BYTES = 56 * 1024 * 1024
LEVELS = 32767.0
SCALE_LANE = 250
LINES = 56


def chebyshev_matrix(degree):
    points = np.arange(degree + 1)
    abscissa = np.cos(np.pi * points / degree)
    signed = np.where((points == 0) | (points == degree), 2.0, 1.0) * (-1.0) ** points
    spacing = abscissa[:, None] - abscissa[None, :] + np.eye(degree + 1)
    matrix = signed[:, None] / signed[None, :] / spacing
    return matrix - np.eye(degree + 1) * np.sum(matrix, axis=1)[:, None]


def fourier_table(length):
    row_index = np.arange(length)[:, None]
    column = np.arange(length)[None, :]
    wavenumber = (row_index + 1) // 2
    phase_angle = 2.0 * np.pi * wavenumber * column / length
    parity = row_index % 2
    base_rows = np.where(
        row_index == 0, 1.0, np.where(parity == 1, np.cos(phase_angle), np.sin(phase_angle))
    )
    row_scale = np.where(
        (row_index == 0) | (row_index == length - 1), 1.0 / np.sqrt(length), np.sqrt(2.0 / length)
    )
    return base_rows * row_scale


def lane_order():
    chips = np.arange(32)
    pieces = []
    for shift in (0, 3, 1, 2):
        for core in range(2):
            pieces.append((chips, np.full(chips.shape, core), np.full(chips.shape, shift)))
    return [np.concatenate([p[k] for p in pieces]).astype(np.int32) for k in range(3)]


def in_two(array):
    high = array.astype(jnp.bfloat16)
    return high, (array - high.astype(F32)).astype(jnp.bfloat16)


def split_table(table):
    high = table.astype(jnp.bfloat16)
    return high, (table - high.astype(np.float64)).astype(jnp.bfloat16)


def transforms(core, plane):
    zl = np.arange(256)
    z_of = 4 * (zl % 64) + zl // 64
    high, low = split_table(fourier_table(256)[:, z_of])
    chip, lane_core, shift = (jnp.asarray(v) for v in lane_order())
    span_of = 2 * chip + lane_core + core * (1 - 2 * lane_core)
    order = 4 * span_of + (plane + shift) % 4
    pick = jnp.where(order[:, None] == jnp.arange(256)[None, :], 1.0, 0.0).astype(jnp.bfloat16)
    both = jnp.asarray(np.concatenate([high, low], axis=1))
    back = jnp.dot(pick, both, preferred_element_type=F32).astype(jnp.bfloat16)
    high, low = back[:, :256], back[:, 256:]
    return (
        jnp.concatenate([high.T, high.T, low.T], axis=0),
        jnp.concatenate([high, high, low], axis=0),
    )


def slope_table():
    d = chebyshev_matrix(P_SIZE)
    eye = np.eye(P_SIZE + 1)
    both = np.zeros((2 * QP, QP), np.float32)
    both[:Q, :Q] = np.kron(d, eye)
    both[QP : QP + Q, :Q] = np.kron(eye, d)
    return jnp.asarray(np.concatenate(split_table(both), axis=0))


def vmem_spec():
    return pl.BlockSpec(memory_space=pltpu.VMEM)


def smem_spec():
    return pl.BlockSpec(memory_space=pltpu.SMEM)


def params():
    return pltpu.CompilerParams(vmem_limit_bytes=VMEM_BYTES)


def pair_up(low, high):
    return (high.astype(jnp.int32) << 16) | (low.astype(jnp.int32) & 0xFFFF)


def scale_code(largest):
    return jnp.floor(jnp.log2(jnp.maximum(largest, 1e-30)) * 2.0**16) + 2.0


def scale_of(code):
    return jnp.exp2(code * 2.0**-16)


def low_of(pair):
    return ((pair << 16) >> 16).astype(F32)


def high_of(pair):
    return (pair >> 16).astype(F32)


def pack_inverse_kernel(h_ref, o_ref, w_ref, f_ref):
    h = h_ref[...]
    largest = jnp.max(jnp.abs(h), axis=1, keepdims=True)
    code = jnp.floor(largest * 2.0**30) + 1.0
    upper = jnp.floor(code * 2.0**-15)
    lower = code - upper * 2.0**15
    w_ref[...] = jnp.zeros_like(w_ref)
    w_ref[0:Q, 0:Q] = jnp.round(h * (LEVELS / (code * 2.0**-30)))
    turned = w_ref[...].T
    w_ref[...] = turned
    w_ref[0:Q, Q : Q + 1] = upper
    w_ref[0:Q, Q + 1 : Q + 2] = lower
    f_ref[...] = jnp.zeros_like(f_ref)
    for k in range(16):
        line, lane = divmod(k * QP, 128)
        count = (Q - k + 15) // 16
        block = w_ref[pl.ds(k, count, stride=16), :]
        if lane:
            block = jnp.roll(block, lane, axis=1)
        place = lax.broadcasted_iota(jnp.int32, (count, 128), 1)
        here = pl.ds(line, count, stride=11)
        f_ref[here, :] = f_ref[here, :] + jnp.where(place >= lane, block, 0.0)
        if lane + QP > 128:
            after = pl.ds(line + 1, count, stride=11)
            f_ref[after, :] = f_ref[after, :] + jnp.where(place < lane, block, 0.0)
    pair = pair_up(f_ref[0:32, :], f_ref[LINES // 2 : LINES // 2 + 32, :])
    o_ref[...] = jnp.broadcast_to(pair[None], o_ref.shape)


def pack_inverse(matrix, targets):
    return pl.pallas_call(
        pack_inverse_kernel,
        out_shape=jax.ShapeDtypeStruct((targets, 32, 128), jnp.int32),
        in_specs=[vmem_spec()],
        out_specs=vmem_spec(),
        scratch_shapes=[pltpu.VMEM((128, 128), F32), pltpu.VMEM((64, 128), F32)],
        compiler_params=params(),
    )(matrix)


def turn_kernel(own_ref, o_ref):
    for g in range(LINES // 8):
        lines = [own_ref[:, 4 * g + b, :] for b in range(4)]
        o_ref[g * 128 : (g + 1) * 128, :] = jnp.concatenate(lines, axis=0).T


def turn_own(own):
    return pl.pallas_call(
        turn_kernel,
        out_shape=jax.ShapeDtypeStruct((LINES // 8 * 128, 128), jnp.int32),
        in_specs=[vmem_spec()],
        out_specs=vmem_spec(),
        compiler_params=params(),
    )(own)


def pack_points_kernel(step_ref, adj_ref, c0_ref, c1_ref, c2_ref, o_ref, t_ref):
    stored = (c0_ref, c1_ref, c2_ref)
    lane = lax.broadcasted_iota(jnp.int32, (64, 256), 1)
    for z in range(4):
        for g in range(3):
            t_ref[g, z, 3 * Q : 256, :] = jnp.zeros((256 - 3 * Q, 128), F32)
            for i in range(3):
                if g == 0:
                    block = adj_ref[i, z]
                else:
                    block = stored[i][0, g - 1, z].astype(F32)
                t_ref[g, z, i * Q : (i + 1) * Q, :] = block
            block = t_ref[g, z]
            largest = jnp.max(jnp.max(jnp.abs(block), axis=0, keepdims=True), axis=1, keepdims=True)
            code = jnp.floor(largest * 2.0**27) + 1.0
            turned = jnp.round(block * (LEVELS / (code * 2.0**-27))).T
            pair = pair_up(turned[0:64, :], turned[64:128, :])
            pair = jnp.where(lane == SCALE_LANE, code.astype(jnp.int32), pair)
            if g == 0:
                o_ref[:, z * 2, 0:256] = pair
            elif g == 1:
                o_ref[:, z * 2, 256:384] = pair[:, 0:128]
                o_ref[:, z * 2 + 1, 0:128] = pair[:, 128:256]
            else:
                o_ref[:, z * 2 + 1, 128:384] = pair


def pack_points(adjoint, checkpoints, checkpoint_step):
    def slot(k):
        return pl.BlockSpec((1, 2, 4, Q, 128), lambda i, st: (st[k], 0, 0, 0, 0))

    return pl.pallas_call(
        pack_points_kernel,
        out_shape=jax.ShapeDtypeStruct((64, 8, 384), jnp.int32),
        grid_spec=pltpu.PrefetchScalarGridSpec(
            num_scalar_prefetch=1,
            grid=(1,),
            in_specs=[
                pl.BlockSpec((3, 4, Q, 128), lambda i, st: (0, 0, 0, 0)),
                slot(0),
                slot(1),
                slot(2),
            ],
            out_specs=pl.BlockSpec((64, 8, 384), lambda i, st: (0, 0, 0)),
            scratch_shapes=[pltpu.VMEM((3, 4, 256, 128), F32)],
        ),
        compiler_params=params(),
    )(checkpoint_step, adjoint, checkpoints, checkpoints, checkpoints)


def transform(array, table_ref):
    high, low = in_two(array)
    return jnp.dot(
        jnp.concatenate([high, low, high], axis=1), table_ref[...], preferred_element_type=F32
    )


def regroup(blocks):
    lane = lax.broadcasted_iota(jnp.int32, blocks[0].shape, 1)

    def exchange(a, b, keep, width):
        return jnp.where(keep, a, pltpu.roll(b, width, 1)), jnp.where(
            keep, pltpu.roll(a, 128 - width, 1), b
        )

    low = lane < 64
    p0, p2 = exchange(blocks[0], blocks[2], low, 64)
    p1, p3 = exchange(blocks[1], blocks[3], low, 64)
    even = (lane & 32) == 0
    p0, p1 = exchange(p0, p1, even, 32)
    p2, p3 = exchange(p2, p3, even, 32)
    return p0, p1, p2, p3


def spread_rows(pieces, k, ht):
    blocks = regroup([ref[pl.ds(pl.multiple_of((k - f) * 32, 32), 32), :] for ref, f in pieces])
    start = (k >> 2) * 512 + (k & 3) * 32
    for b in range(4):
        row = pl.multiple_of(start + b * 128, 32)
        ht[pl.ds(row, 32), :] = low_of(blocks[b])
        row = pl.multiple_of(start + b * 128 + LINES * 64, 32)
        ht[pl.ds(row, 32), :] = high_of(blocks[b])


def row_scales(ht, rows):
    rows[...] = jnp.zeros_like(rows)
    rows[0:Q, :] = (
        ht[pl.ds(Q, Q, stride=QP), :] * 2.0**15 + ht[pl.ds(Q + 1, Q, stride=QP), :]
    ) * (2.0**-30 / LEVELS)


def regroup_kernel(own_ref, own2_ref, left_ref, left2_ref, o_ref):
    def spread(k, carry):
        spread_rows([(r, 0) for r in (own_ref, own2_ref, left_ref, left2_ref)], k, o_ref)
        return carry

    lax.fori_loop(0, 28, spread, 0, unroll=7)


def regroup_half(pieces):
    return pl.pallas_call(
        regroup_kernel,
        out_shape=jax.ShapeDtypeStruct((LINES * 128, 128), F32),
        in_specs=[vmem_spec()] * 4,
        out_specs=vmem_spec(),
        compiler_params=params(),
    )(*pieces)


def advance(place_ref, metric_ref, x, v, step, both_ref, fwd_ref, coef):
    chip = place_ref[0]
    for e in range(2):
        m0 = metric_ref[0, chip + 64 * e]
        m1 = metric_ref[1, chip + 64 * e]
        for c in range(3):
            field = x[e * 3 + c]
            high, low = in_two(field)
            large = jnp.dot(both_ref[...], high, preferred_element_type=F32)
            small = jnp.dot(both_ref[0 : 2 * QP, :], low, preferred_element_type=F32)
            slopes = large[0 : 2 * QP] + (large[2 * QP : 4 * QP] + small)
            x[e * 3 + c] = (
                field
                + v[0, e, step] * (m0 * slopes[0:QP])
                + v[1, e, step] * (m1 * slopes[QP : 2 * QP])
            )
    modes = transform(x[...].reshape(6 * QP, 256), fwd_ref)
    coef[0] = modes[:, 0:128]
    coef[1] = modes[:, 128:256]


def first_kernel(place_ref, metric_ref, r_ref, fwd_ref, both_ref, coef, v, x, spread):
    x[...] = jnp.zeros_like(x)
    v[...] = jnp.zeros_like(v)
    for g in range(3):
        stack = []
        for z in range(4):
            if g == 0:
                stack.append(r_ref[:, z * 2, 0:256])
            elif g == 1:
                stack.append(
                    jnp.concatenate(
                        [r_ref[:, z * 2, 256:384], r_ref[:, z * 2 + 1, 0:128]], axis=1
                    )
                )
            else:
                stack.append(r_ref[:, z * 2 + 1, 128:384])
        pair = jnp.concatenate(stack, axis=0).T
        unit = pair[SCALE_LANE : SCALE_LANE + 1, :].astype(F32) * (2.0**-27 / LEVELS)
        for e in range(2):
            spread[...] = (low_of(pair) if e == 0 else high_of(pair)) * unit
            for i in range(3):
                part = spread[i * Q : (i + 1) * Q, :]
                if g == 0:
                    x[e * 3 + i, 0:Q, :] = part
                else:
                    v[(g - 1), e, i, 0:Q, :] = part
    advance(place_ref, metric_ref, x, v, 0, both_ref, fwd_ref, coef)


def first_modes(place, metric, points, fwd, both):
    return pl.pallas_call(
        first_kernel,
        out_shape=(
            jax.ShapeDtypeStruct((2, 6 * QP, 128), F32),
            jax.ShapeDtypeStruct((2, 2, 3, QP, 256), F32),
        ),
        in_specs=[smem_spec(), smem_spec()] + [vmem_spec()] * 3,
        out_specs=(vmem_spec(), vmem_spec()),
        scratch_shapes=[pltpu.VMEM((6, QP, 256), F32), pltpu.VMEM((256, 256), F32)],
        compiler_params=params(),
    )(place, metric, points, fwd, both)


def steps_kernel(
    place_ref, metric_ref, regrouped_ref, right_ref, right2_ref, oa_ref, oa2_ref, ob_ref, ob2_ref,
    first_ref, v, fwd_ref, back_ref, both_ref,
    out_ref,
    ht0, ht1, rows0, rows1, x, coef, solved, wall, turn, sem,
):
    load = pltpu.make_async_copy(regrouped_ref, ht0, sem)
    load.start()
    halves = (ht0, ht1)
    scales = (rows0, rows1)
    for first, far in ((0, (oa_ref, oa2_ref)), (14, (ob_ref, ob2_ref))):

        def spread(k, carry, first=first, far=far):
            near = [(right_ref, 0), (right2_ref, 0)]
            spread_rows(near + [(ref, first) for ref in far], k, ht1)
            return carry

        lax.fori_loop(first, first + 14, spread, 0, unroll=7)
    load.wait()
    row_scales(ht0, rows0)
    row_scales(ht1, rows1)

    for step in range(NSTEP):
        if step > 0:
            advance(place_ref, metric_ref, x, v, step, both_ref, fwd_ref, coef)
        modes = coef if step > 0 else first_ref
        for half in range(2):
            for e in range(2):

                def columns(i, sums, half=half, e=e, modes=modes):
                    for t in range(27):
                        r = i * 27 + t
                        h = halves[half][pl.ds(pl.multiple_of(r * QP, 8), QP), :]
                        sums = tuple(
                            sums[c] + h * modes[half, pl.ds((e * 3 + c) * QP + r, 1), :]
                            for c in range(3)
                        )
                    return sums

                zero = jnp.zeros((QP, 128), F32)
                sums = lax.fori_loop(0, Q // 27, columns, (zero, zero, zero))
                for c in range(3):
                    solved[e * 3 + c, :, half * 128 : (half + 1) * 128] = (
                        sums[c] * scales[half][...]
                    )
        planes = transform(solved[...].reshape(6 * QP, 256), back_ref)
        x[...] = planes.reshape(6, QP, 256)
        for e in range(2):
            product = x[e * 3 + 1] * v[1, e, step]
            if step == 0:
                wall[e] = product
            else:
                wall[e] = wall[e] + product

    def levels(array):
        largest = jnp.max(jnp.max(jnp.abs(array), axis=0), axis=0, keepdims=True)
        code = scale_code(largest)
        return code.astype(jnp.int32), LEVELS / scale_of(code)

    code, unit = levels(wall[...])
    turn[0:QP, :] = pair_up(jnp.round(wall[0] * unit), jnp.round(wall[1] * unit))
    turn[QP:128, :] = jnp.broadcast_to(code, (128 - QP, 256))
    turned = turn[0:128, :].T
    for z in range(4):
        out_ref[:, z, 256:384] = turned[z * 64 : (z + 1) * 64, :]
    code, unit = levels(x[...])
    for c in range(3):
        turn[c * Q : (c + 1) * Q, :] = pair_up(
            jnp.round(x[c, 0:Q, :] * unit), jnp.round(x[c + 3, 0:Q, :] * unit)
        )
    turn[3 * Q : 256, :] = jnp.broadcast_to(code, (256 - 3 * Q, 256))
    turned = turn[...].T
    for z in range(4):
        out_ref[:, z, 0:256] = turned[z * 64 : (z + 1) * 64, :]


def steps(place, metric, regrouped, pieces, first, velocity, fwd, back, both):
    return pl.pallas_call(
        steps_kernel,
        out_shape=jax.ShapeDtypeStruct((64, 4, 384), jnp.int32),
        in_specs=[smem_spec(), smem_spec(), pl.BlockSpec(memory_space=pl.ANY)]
        + [vmem_spec()] * (len(pieces) + 5),
        out_specs=vmem_spec(),
        scratch_shapes=[
            pltpu.VMEM((LINES * 128, 128), F32),
            pltpu.VMEM((LINES * 128, 128), F32),
            pltpu.VMEM((QP, 128), F32),
            pltpu.VMEM((QP, 128), F32),
            pltpu.VMEM((6, QP, 256), F32),
            pltpu.VMEM((2, 6 * QP, 128), F32),
            pltpu.VMEM((6, QP, 256), F32),
            pltpu.VMEM((2, QP, 256), F32),
            pltpu.VMEM((256, 256), jnp.int32),
            pltpu.SemaphoreType.DMA,
        ],
        compiler_params=params(),
    )(place, metric, regrouped, *pieces, first, velocity, fwd, back, both)


def wall_kernel(r_ref, local_ref, element_ref, o_ref):
    points = local_ref.shape[1]
    mode = lax.broadcasted_iota(jnp.int32, (128, points), 0)
    pick = jnp.where(mode == local_ref[...], 1.0, 0.0).astype(jnp.bfloat16)
    pick = jnp.concatenate([pick, pick], axis=0)
    here = mode == element_ref[...]
    for z in range(4):
        pair = r_ref[:, z, :]
        unit = scale_of(pair[:, QP : QP + 1].astype(F32)) * (1.0 / LEVELS)
        field = jnp.concatenate([low_of(pair) * unit, high_of(pair) * unit], axis=0)
        high, low = in_two(field)
        values = jnp.dot(
            jnp.concatenate([low, high], axis=1), pick, preferred_element_type=F32
        )
        total = jnp.sum(jnp.where(here, values, 0.0), axis=0, keepdims=True)
        o_ref[z : z + 1, :] = total[:, 0 : points // 2] + total[:, points // 2 :]


def wall_sums(received, local, element):
    return pl.pallas_call(
        wall_kernel,
        out_shape=jax.ShapeDtypeStruct((4, local.shape[1] // 2), F32),
        grid=(1,),
        in_specs=[
            pl.BlockSpec((64, 4, 128), lambda i: (0, 0, 2)),
            pl.BlockSpec(local.shape, lambda i: (0, 0)),
            pl.BlockSpec(element.shape, lambda i: (0, 0)),
        ],
        out_specs=pl.BlockSpec((4, local.shape[1] // 2), lambda i: (0, 0)),
        compiler_params=params(),
    )(received, local, element)


def weigh_kernel(weight_ref, p0_ref, p1_ref, p2_ref, p3_ref, weighted_ref, square_ref):
    weighted = weight_ref[...] * ((p0_ref[...] + p1_ref[...]) + (p2_ref[...] + p3_ref[...]))
    weighted_ref[...] = weighted
    square = jnp.sum(jnp.sum(weighted * weighted, axis=0, keepdims=True), axis=1, keepdims=True)
    square_ref[...] = jnp.broadcast_to(square.reshape(1, 1, 1), square_ref.shape)


def weigh(weight, parts, targets):
    return pl.pallas_call(
        weigh_kernel,
        out_shape=(
            jax.ShapeDtypeStruct(weight.shape, F32),
            jax.ShapeDtypeStruct((targets, 1, 128), F32),
        ),
        in_specs=[vmem_spec()] * 5,
        out_specs=(vmem_spec(), vmem_spec()),
        compiler_params=params(),
    )(weight, *parts)


def share_kernel(plane_ref, weighted_ref, squares_ref, o_ref, *, entries):
    width = o_ref.shape[1]
    total = jnp.sum(squares_ref[:, 0, :], axis=0, keepdims=True)[:, 0:1]
    start = pl.multiple_of(plane_ref[0] * width, 128)
    o_ref[...] = weighted_ref[:, pl.ds(start, width)] * lax.rsqrt(total * (1.0 / entries) + 1e-06)


def share(plane, weighted, squares, width, entries):
    return pl.pallas_call(
        functools.partial(share_kernel, entries=entries),
        out_shape=jax.ShapeDtypeStruct((weighted.shape[0], width), F32),
        in_specs=[smem_spec(), vmem_spec(), vmem_spec()],
        out_specs=vmem_spec(),
        compiler_params=params(),
    )(plane, weighted, squares)


def unpack_kernel(r_ref, o_ref, t_ref):
    for z in range(4):
        pair = r_ref[:, z, :].T
        unit = scale_of(pair[SCALE_LANE : SCALE_LANE + 1, :].astype(F32)) * (1.0 / LEVELS)
        t_ref[z] = jnp.concatenate([low_of(pair) * unit, high_of(pair) * unit], axis=1)
        for c in range(3):
            o_ref[c, z] = t_ref[z, c * Q : (c + 1) * Q, :]


def unpack(received):
    return pl.pallas_call(
        unpack_kernel,
        out_shape=jax.ShapeDtypeStruct((3, 4, Q, 128), F32),
        grid=(1,),
        in_specs=[pl.BlockSpec((64, 4, 256), lambda i: (0, 0, 0))],
        out_specs=pl.BlockSpec((3, 4, Q, 128), lambda i: (0, 0, 0, 0)),
        scratch_shapes=[pltpu.VMEM((4, 256, 128), F32)],
        compiler_params=params(),
    )(received)


def on_device(
    adjoint,
    checkpoints,
    checkpoint_step,
    metric,
    helmholtz_inverse,
    wall_element,
    wall_local,
    wall_weight,
):
    span = lax.axis_index("span")
    plane = lax.axis_index("plane")
    span_count = lax.axis_size("span")
    plane_count = lax.axis_size("plane")
    wall_count = wall_element.shape[0]
    core = span % 2
    place = jnp.stack([span, core]).astype(jnp.int32)
    fwd, back = transforms(core, plane)

    def around(block, step):
        return lax.ppermute(
            block, "plane", [(i, (i + step) % plane_count) for i in range(plane_count)]
        )

    def across(block):
        return lax.ppermute(block, "span", [(i, i ^ 1) for i in range(span_count)])

    matrix = lax.dynamic_index_in_dim(helmholtz_inverse, plane, 0, keepdims=False)
    same_core = [list(range(c, span_count, 2)) for c in range(2)]
    own = lax.all_to_all(
        pack_inverse(matrix, span_count // 2), "span", 0, 0, tiled=True, axis_index_groups=same_core
    )
    local = wall_local.T.reshape(1, 2 * wall_count)
    element = wall_element.T.reshape(1, 2 * wall_count) - plane * adjoint.shape[3]
    sent = pack_points(adjoint, checkpoints, checkpoint_step)
    own, sent, local, element, place, fwd, back = lax.optimization_barrier(
        (own, sent, local, element, place, fwd, back)
    )
    own = turn_own(own)
    left = around(own, 1)
    right = around(own, 3)
    points = lax.all_to_all(sent, "span", 0, 0, tiled=True)
    oa = around(left[:448], 1)
    ob = around(right[448:], 3)
    both = slope_table()
    first, velocity = first_modes(place, metric, points, fwd, both)
    regrouped = regroup_half((own, across(own), left, across(left)))
    pieces = [right, across(right)]
    oa, ob, regrouped = lax.optimization_barrier((oa, ob, regrouped))
    for piece in (oa, ob):
        pieces += [piece, across(piece)]
    out = steps(place, metric, regrouped, pieces, first, velocity, fwd, back, both)
    received = lax.all_to_all(out, "span", 0, 0, tiled=True)

    partial_sum = wall_sums(received, local, element)
    parts = [partial_sum] + [around(partial_sum, k) for k in range(1, plane_count)]
    weighted, square = weigh(wall_weight, parts, span_count)
    squares = lax.all_to_all(square, "span", 0, 0, tiled=True)
    gradient = share(
        plane.reshape(1).astype(jnp.int32),
        weighted,
        squares,
        wall_count // plane_count,
        adjoint.shape[1] * span_count * wall_count,
    )
    return (unpack(received), gradient)


def solution(mesh):
    placed = (
        P(None, "span", None, "plane"),
        P(None, None, "span", None, "plane"),
        P(),
        P(None, "plane"),
        P("span", None, None),
        P(),
        P(),
        P("span", None),
    )
    return jax.shard_map(
        on_device,
        mesh=mesh,
        in_specs=placed,
        out_specs=(P(None, "span", None, "plane"), P("span", "plane")),
        check_vma=False,
    )
```

```python
import functools

import jax
import jax.numpy as jnp
import numpy as np
from jax import lax
from jax.experimental import pallas as pl
from jax.experimental.pallas import tpu as pltpu
from jax.sharding import PartitionSpec as P

P_SIZE = 8
Q = 81
QP = 88
NSTEP = 3
HIGHEST = lax.Precision.HIGHEST
F32 = jnp.float32
VMEM_BYTES = 12 * 1024 * 1024
LEVELS = 32767.0
SCALE_LANE = 250
LINES = 56


def chebyshev_matrix(degree):
    points = np.arange(degree + 1)
    abscissa = np.cos(np.pi * points / degree)
    signed = np.where((points == 0) | (points == degree), 2.0, 1.0) * (-1.0) ** points
    spacing = abscissa[:, None] - abscissa[None, :] + np.eye(degree + 1)
    matrix = signed[:, None] / signed[None, :] / spacing
    return matrix - np.eye(degree + 1) * np.sum(matrix, axis=1)[:, None]


def fourier_table(length):
    row_index = np.arange(length)[:, None]
    column = np.arange(length)[None, :]
    wavenumber = (row_index + 1) // 2
    phase_angle = 2.0 * np.pi * wavenumber * column / length
    parity = row_index % 2
    base_rows = np.where(
        row_index == 0, 1.0, np.where(parity == 1, np.cos(phase_angle), np.sin(phase_angle))
    )
    row_scale = np.where(
        (row_index == 0) | (row_index == length - 1), 1.0 / np.sqrt(length), np.sqrt(2.0 / length)
    )
    return base_rows * row_scale


def lane_order():
    chips = np.arange(32)
    pieces = []
    for shift in (0, 3, 1, 2):
        for core in range(2):
            pieces.append((chips, np.full(chips.shape, core), np.full(chips.shape, shift)))
    return [np.concatenate([p[k] for p in pieces]).astype(np.int32) for k in range(3)]


def in_two(array):
    high = array.astype(jnp.bfloat16)
    return high, (array - high.astype(F32)).astype(jnp.bfloat16)


def split_table(table):
    high = table.astype(jnp.bfloat16)
    return high, (table - high.astype(np.float64)).astype(jnp.bfloat16)


def transforms(core, plane):
    zl = np.arange(256)
    z_of = 4 * (zl % 64) + zl // 64
    high, low = split_table(fourier_table(256)[:, z_of])
    chip, lane_core, shift = (jnp.asarray(v) for v in lane_order())
    span_of = 2 * chip + lane_core + core * (1 - 2 * lane_core)
    order = 4 * span_of + (plane + shift) % 4
    index = jnp.arange(256)
    pick = jnp.where(order[:, None] == index[None, :], 1.0, 0.0).astype(jnp.bfloat16)
    pick_turned = jnp.where(index[:, None] == order[None, :], 1.0, 0.0).astype(jnp.bfloat16)
    both = jnp.asarray(np.concatenate([high, low], axis=1))
    back = jnp.dot(pick, both, preferred_element_type=F32).astype(jnp.bfloat16)
    both = jnp.asarray(np.ascontiguousarray(np.concatenate([high, high, low], axis=1).T))
    fwd = jnp.dot(both, pick_turned, preferred_element_type=F32).astype(jnp.bfloat16)
    return fwd, jnp.concatenate([back[:, :256], back[:, :256], back[:, 256:]], axis=0)


def slope_table():
    d = chebyshev_matrix(P_SIZE)
    eye = np.eye(P_SIZE + 1)
    both = np.zeros((2 * QP, QP), np.float32)
    both[:Q, :Q] = np.kron(d, eye)
    both[QP : QP + Q, :Q] = np.kron(eye, d)
    return jnp.asarray(np.concatenate(split_table(both), axis=0))


def vmem_spec():
    return pl.BlockSpec(memory_space=pltpu.VMEM)


def smem_spec():
    return pl.BlockSpec(memory_space=pltpu.SMEM)


def params(size=VMEM_BYTES):
    return pltpu.CompilerParams(vmem_limit_bytes=size)


def pair_up(low, high):
    return (high.astype(jnp.int32) << 16) | (low.astype(jnp.int32) & 0xFFFF)


def scale_code(largest):
    return jnp.floor(jnp.log2(jnp.maximum(largest, 1e-30)) * 2.0**16) + 2.0


def scale_of(code):
    return jnp.exp2(code * 2.0**-16)


def low_of(pair):
    return ((pair << 16) >> 16).astype(F32)


def high_of(pair):
    return (pair >> 16).astype(F32)


def pack_inverse_kernel(plane_ref, h_ref, o_ref, w_ref, f_ref):
    h = h_ref[:, 0, :]
    for k in range(1, h_ref.shape[1]):
        h = jnp.where(plane_ref[0] == k, h_ref[:, k, :], h)
    largest = jnp.max(jnp.abs(h), axis=1, keepdims=True)
    code = jnp.floor(largest * 2.0**30) + 1.0
    upper = jnp.floor(code * 2.0**-15)
    lower = code - upper * 2.0**15
    w_ref[...] = jnp.zeros_like(w_ref)
    w_ref[0:Q, 0:Q] = jnp.round(h * (LEVELS / (code * 2.0**-30)))
    turned = w_ref[...].T
    w_ref[...] = turned
    w_ref[0:Q, Q : Q + 1] = upper
    w_ref[0:Q, Q + 1 : Q + 2] = lower
    f_ref[...] = jnp.zeros_like(f_ref)
    for k in range(16):
        line, lane = divmod(k * QP, 128)
        count = (Q - k + 15) // 16
        block = w_ref[pl.ds(k, count, stride=16), :]
        if lane:
            block = jnp.roll(block, lane, axis=1)
        place = lax.broadcasted_iota(jnp.int32, (count, 128), 1)
        here = pl.ds(line, count, stride=11)
        f_ref[here, :] = f_ref[here, :] + jnp.where(place >= lane, block, 0.0)
        if lane + QP > 128:
            after = pl.ds(line + 1, count, stride=11)
            f_ref[after, :] = f_ref[after, :] + jnp.where(place < lane, block, 0.0)
    pair = pair_up(f_ref[0:32, :], f_ref[LINES // 2 : LINES // 2 + 32, :])
    o_ref[...] = jnp.broadcast_to(pair[None], o_ref.shape)


def pack_inverse(plane, inverse, targets):
    return pl.pallas_call(
        pack_inverse_kernel,
        out_shape=jax.ShapeDtypeStruct((targets, 32, 128), jnp.int32),
        in_specs=[smem_spec(), vmem_spec()],
        out_specs=vmem_spec(),
        scratch_shapes=[pltpu.VMEM((128, 128), F32), pltpu.VMEM((64, 128), F32)],
        compiler_params=params(),
    )(plane, inverse.transpose(1, 0, 2))


def turn_kernel(own_ref, o_ref):
    for g in range(LINES // 8):
        lines = [own_ref[:, 4 * g + b, :] for b in range(4)]
        o_ref[g * 128 : (g + 1) * 128, :] = jnp.concatenate(lines, axis=0).T


def turn_own(own):
    return pl.pallas_call(
        turn_kernel,
        out_shape=jax.ShapeDtypeStruct((LINES // 8 * 128, 128), jnp.int32),
        in_specs=[vmem_spec()],
        out_specs=vmem_spec(),
        compiler_params=params(),
    )(own)


def pack_points_kernel(step_ref, adj_ref, c0_ref, c1_ref, c2_ref, o_ref, t_ref):
    stored = (c0_ref, c1_ref, c2_ref)
    lane = lax.broadcasted_iota(jnp.int32, (64, 256), 1)
    for z in range(4):
        for g in range(3):
            t_ref[g, z, 3 * Q : 256, :] = jnp.zeros((256 - 3 * Q, 128), F32)
            for i in range(3):
                if g == 0:
                    block = adj_ref[i, z]
                else:
                    block = stored[i][0, g - 1, z].astype(F32)
                t_ref[g, z, i * Q : (i + 1) * Q, :] = block
            block = t_ref[g, z]
            largest = jnp.max(jnp.max(jnp.abs(block), axis=0, keepdims=True), axis=1, keepdims=True)
            code = jnp.floor(largest * 2.0**27) + 1.0
            turned = jnp.round(block * (LEVELS / (code * 2.0**-27))).T
            pair = pair_up(turned[0:64, :], turned[64:128, :])
            pair = jnp.where(lane == SCALE_LANE, code.astype(jnp.int32), pair)
            if g == 0:
                o_ref[:, z * 2, 0:256] = pair
            elif g == 1:
                o_ref[:, z * 2, 256:384] = pair[:, 0:128]
                o_ref[:, z * 2 + 1, 0:128] = pair[:, 128:256]
            else:
                o_ref[:, z * 2 + 1, 128:384] = pair


def pack_points(adjoint, checkpoints, checkpoint_step):
    def slot(k):
        return pl.BlockSpec((1, 2, 4, Q, 128), lambda i, st: (st[k], 0, 0, 0, 0))

    return pl.pallas_call(
        pack_points_kernel,
        out_shape=jax.ShapeDtypeStruct((64, 8, 384), jnp.int32),
        grid_spec=pltpu.PrefetchScalarGridSpec(
            num_scalar_prefetch=1,
            grid=(1,),
            in_specs=[
                pl.BlockSpec((3, 4, Q, 128), lambda i, st: (0, 0, 0, 0)),
                slot(0),
                slot(1),
                slot(2),
            ],
            out_specs=pl.BlockSpec((64, 8, 384), lambda i, st: (0, 0, 0)),
            scratch_shapes=[pltpu.VMEM((3, 4, 256, 128), F32)],
        ),
        compiler_params=params(),
    )(checkpoint_step, adjoint, checkpoints, checkpoints, checkpoints)


def transform(array, table_ref):
    high, low = in_two(array)
    return jnp.dot(
        jnp.concatenate([high, low, high], axis=1), table_ref[...], preferred_element_type=F32
    )


def regroup(blocks):
    lane = lax.broadcasted_iota(jnp.int32, blocks[0].shape, 1)

    def exchange(a, b, keep, width):
        return jnp.where(keep, a, pltpu.roll(b, width, 1)), jnp.where(
            keep, pltpu.roll(a, 128 - width, 1), b
        )

    low = lane < 64
    p0, p2 = exchange(blocks[0], blocks[2], low, 64)
    p1, p3 = exchange(blocks[1], blocks[3], low, 64)
    even = (lane & 32) == 0
    p0, p1 = exchange(p0, p1, even, 32)
    p2, p3 = exchange(p2, p3, even, 32)
    return p0, p1, p2, p3


def spread_rows(pieces, k, ht):
    blocks = regroup([ref[pl.ds(pl.multiple_of((k - f) * 32, 32), 32), :] for ref, f in pieces])
    start = (k >> 2) * 512 + (k & 3) * 32
    for b in range(4):
        row = pl.multiple_of(start + b * 128, 32)
        ht[pl.ds(row, 32), :] = low_of(blocks[b])
        row = pl.multiple_of(start + b * 128 + LINES * 64, 32)
        ht[pl.ds(row, 32), :] = high_of(blocks[b])


def row_scales(ht, rows):
    rows[...] = jnp.zeros_like(rows)
    rows[0:Q, :] = (
        ht[pl.ds(Q, Q, stride=QP), :] * 2.0**15 + ht[pl.ds(Q + 1, Q, stride=QP), :]
    ) * (2.0**-30 / LEVELS)


def regroup_kernel(own_ref, own2_ref, left_ref, left2_ref, o_ref, ht, sems):
    copies = []
    for g in range(LINES // 8):
        for k in range(4 * g, 4 * g + 4):
            spread_rows([(r, 0) for r in (own_ref, own2_ref, left_ref, left2_ref)], k, ht)
        for part in range(2):
            block = pl.ds(g * 512 + part * LINES * 64, 512)
            copy = pltpu.make_async_copy(ht.at[block, :], o_ref.at[block, :], sems.at[g, part])
            copy.start()
            copies.append(copy)
    for copy in copies:
        copy.wait()


def regroup_half(pieces):
    return pl.pallas_call(
        regroup_kernel,
        out_shape=pltpu.HBM((LINES * 128, 128), F32),
        in_specs=[vmem_spec()] * 4,
        out_specs=pl.BlockSpec(memory_space=pltpu.HBM),
        scratch_shapes=[
            pltpu.VMEM((LINES * 128, 128), F32),
            pltpu.SemaphoreType.DMA((LINES // 8, 2)),
        ],
        compiler_params=params(),
    )(*pieces)


def advance(place_ref, metric_ref, x, v, step, both_ref, fwd_ref, coef):
    chip = place_ref[0]
    for e in range(2):
        m0 = metric_ref[0, chip + 64 * e]
        m1 = metric_ref[1, chip + 64 * e]
        for c in range(3):
            field = x[e * 3 + c]
            high, low = in_two(field)
            large = jnp.dot(both_ref[...], high, preferred_element_type=F32)
            small = jnp.dot(both_ref[0 : 2 * QP, :], low, preferred_element_type=F32)
            slopes = large[0 : 2 * QP] + (large[2 * QP : 4 * QP] + small)
            x[e * 3 + c] = (
                field
                + v[0, e, step] * (m0 * slopes[0:QP])
                + v[1, e, step] * (m1 * slopes[QP : 2 * QP])
            )
    modes = transform(x[...].reshape(6 * QP, 256), fwd_ref)
    coef[0] = modes[:, 0:128]
    coef[1] = modes[:, 128:256]


def first_kernel(place_ref, metric_ref, r_ref, fwd_ref, both_ref, coef, v, x, spread):
    x[...] = jnp.zeros_like(x)
    v[...] = jnp.zeros_like(v)
    for g in range(3):
        stack = []
        for z in range(4):
            if g == 0:
                stack.append(r_ref[:, z * 2, 0:256])
            elif g == 1:
                stack.append(
                    jnp.concatenate(
                        [r_ref[:, z * 2, 256:384], r_ref[:, z * 2 + 1, 0:128]], axis=1
                    )
                )
            else:
                stack.append(r_ref[:, z * 2 + 1, 128:384])
        pair = jnp.concatenate(stack, axis=0).T
        unit = pair[SCALE_LANE : SCALE_LANE + 1, :].astype(F32) * (2.0**-27 / LEVELS)
        for e in range(2):
            spread[...] = (low_of(pair) if e == 0 else high_of(pair)) * unit
            for i in range(3):
                part = spread[i * Q : (i + 1) * Q, :]
                if g == 0:
                    x[e * 3 + i, 0:Q, :] = part
                else:
                    v[(g - 1), e, i, 0:Q, :] = part
    advance(place_ref, metric_ref, x, v, 0, both_ref, fwd_ref, coef)


def first_modes(place, metric, points, fwd, both):
    return pl.pallas_call(
        first_kernel,
        out_shape=(
            jax.ShapeDtypeStruct((2, 6 * QP, 128), F32),
            jax.ShapeDtypeStruct((2, 2, 3, QP, 256), F32),
        ),
        in_specs=[smem_spec(), smem_spec()] + [vmem_spec()] * 3,
        out_specs=(vmem_spec(), vmem_spec()),
        scratch_shapes=[pltpu.VMEM((6, QP, 256), F32), pltpu.VMEM((256, 256), F32)],
        compiler_params=params(),
    )(place, metric, points, fwd, both)


def steps_kernel(
    place_ref, metric_ref, regrouped_ref, right_ref, right2_ref, oa_ref, oa2_ref, ob_ref, ob2_ref,
    first_ref, v, fwd_ref, back_ref, both_ref,
    out_ref,
    ht0, ht1, rows0, rows1, x, coef, solved, wall, turn, sem,
):
    load = pltpu.make_async_copy(regrouped_ref, ht0, sem)
    load.start()
    halves = (ht0, ht1)
    scales = (rows0, rows1)
    for first, far in ((0, (oa_ref, oa2_ref)), (14, (ob_ref, ob2_ref))):

        def spread(k, carry, first=first, far=far):
            near = [(right_ref, 0), (right2_ref, 0)]
            spread_rows(near + [(ref, first) for ref in far], k, ht1)
            return carry

        lax.fori_loop(first, first + 14, spread, 0, unroll=7)
    load.wait()
    row_scales(ht0, rows0)
    row_scales(ht1, rows1)

    for step in range(NSTEP):
        if step > 0:
            advance(place_ref, metric_ref, x, v, step, both_ref, fwd_ref, coef)
        modes = coef if step > 0 else first_ref
        for half in range(2):
            for e in range(2):

                def columns(i, sums, half=half, e=e, modes=modes):
                    for t in range(27):
                        r = i * 27 + t
                        h = halves[half][pl.ds(pl.multiple_of(r * QP, 8), QP), :]
                        sums = tuple(
                            sums[c] + h * modes[half, pl.ds((e * 3 + c) * QP + r, 1), :]
                            for c in range(3)
                        )
                    return sums

                zero = jnp.zeros((QP, 128), F32)
                sums = lax.fori_loop(0, Q // 27, columns, (zero, zero, zero))
                for c in range(3):
                    solved[e * 3 + c, :, half * 128 : (half + 1) * 128] = (
                        sums[c] * scales[half][...]
                    )
        planes = transform(solved[...].reshape(6 * QP, 256), back_ref)
        x[...] = planes.reshape(6, QP, 256)
        for e in range(2):
            product = x[e * 3 + 1] * v[1, e, step]
            if step == 0:
                wall[e] = product
            else:
                wall[e] = wall[e] + product

    def levels(array):
        largest = jnp.max(jnp.max(jnp.abs(array), axis=0), axis=0, keepdims=True)
        code = scale_code(largest)
        return code.astype(jnp.int32), LEVELS / scale_of(code)

    code, unit = levels(wall[...])
    turn[0:QP, :] = pair_up(jnp.round(wall[0] * unit), jnp.round(wall[1] * unit))
    turn[QP:128, :] = jnp.broadcast_to(code, (128 - QP, 256))
    turned = turn[0:128, :].T
    for z in range(4):
        out_ref[:, z, 256:384] = turned[z * 64 : (z + 1) * 64, :]
    code, unit = levels(x[...])
    for c in range(3):
        turn[c * Q : (c + 1) * Q, :] = pair_up(
            jnp.round(x[c, 0:Q, :] * unit), jnp.round(x[c + 3, 0:Q, :] * unit)
        )
    turn[3 * Q : 256, :] = jnp.broadcast_to(code, (256 - 3 * Q, 256))
    turned = turn[...].T
    for z in range(4):
        out_ref[:, z, 0:256] = turned[z * 64 : (z + 1) * 64, :]


def steps(place, metric, regrouped, pieces, first, velocity, fwd, back, both):
    return pl.pallas_call(
        steps_kernel,
        out_shape=jax.ShapeDtypeStruct((64, 4, 384), jnp.int32),
        in_specs=[smem_spec(), smem_spec(), pl.BlockSpec(memory_space=pltpu.HBM)]
        + [vmem_spec()] * (len(pieces) + 5),
        out_specs=vmem_spec(),
        scratch_shapes=[
            pltpu.VMEM((LINES * 128, 128), F32),
            pltpu.VMEM((LINES * 128, 128), F32),
            pltpu.VMEM((QP, 128), F32),
            pltpu.VMEM((QP, 128), F32),
            pltpu.VMEM((6, QP, 256), F32),
            pltpu.VMEM((2, 6 * QP, 128), F32),
            pltpu.VMEM((6, QP, 256), F32),
            pltpu.VMEM((2, QP, 256), F32),
            pltpu.VMEM((256, 256), jnp.int32),
            pltpu.SemaphoreType.DMA,
        ],
        compiler_params=params(2 * VMEM_BYTES),
    )(place, metric, regrouped, *pieces, first, velocity, fwd, back, both)


def wall_kernel(r_ref, local_ref, element_ref, o_ref):
    points = local_ref.shape[1]
    mode = lax.broadcasted_iota(jnp.int32, (128, points), 0)
    pick = jnp.where(mode == local_ref[...], 1.0, 0.0).astype(jnp.bfloat16)
    pick = jnp.concatenate([pick, pick], axis=0)
    here = mode == element_ref[...]
    for z in range(4):
        pair = r_ref[:, z, :]
        unit = scale_of(pair[:, QP : QP + 1].astype(F32)) * (1.0 / LEVELS)
        field = jnp.concatenate([low_of(pair) * unit, high_of(pair) * unit], axis=0)
        high, low = in_two(field)
        values = jnp.dot(
            jnp.concatenate([low, high], axis=1), pick, preferred_element_type=F32
        )
        total = jnp.sum(jnp.where(here, values, 0.0), axis=0, keepdims=True)
        o_ref[z : z + 1, :] = total[:, 0 : points // 2] + total[:, points // 2 :]


def wall_sums(received, local, element):
    return pl.pallas_call(
        wall_kernel,
        out_shape=jax.ShapeDtypeStruct((4, local.shape[1] // 2), F32),
        grid=(1,),
        in_specs=[
            pl.BlockSpec((64, 4, 128), lambda i: (0, 0, 2)),
            pl.BlockSpec(local.shape, lambda i: (0, 0)),
            pl.BlockSpec(element.shape, lambda i: (0, 0)),
        ],
        out_specs=pl.BlockSpec((4, local.shape[1] // 2), lambda i: (0, 0)),
        compiler_params=params(),
    )(received, local, element)


def weigh_kernel(weight_ref, p0_ref, p1_ref, p2_ref, p3_ref, weighted_ref, square_ref):
    weighted = weight_ref[...] * ((p0_ref[...] + p1_ref[...]) + (p2_ref[...] + p3_ref[...]))
    weighted_ref[...] = weighted
    square = jnp.sum(jnp.sum(weighted * weighted, axis=0, keepdims=True), axis=1, keepdims=True)
    square_ref[...] = jnp.broadcast_to(square.reshape(1, 1, 1), square_ref.shape)


def weigh(weight, parts, targets):
    return pl.pallas_call(
        weigh_kernel,
        out_shape=(
            jax.ShapeDtypeStruct(weight.shape, F32),
            jax.ShapeDtypeStruct((targets, 1, 128), F32),
        ),
        in_specs=[vmem_spec()] * 5,
        out_specs=(vmem_spec(), vmem_spec()),
        compiler_params=params(),
    )(weight, *parts)


def share_kernel(plane_ref, weighted_ref, squares_ref, o_ref, *, entries):
    width = o_ref.shape[1]
    total = jnp.sum(squares_ref[:, 0, :], axis=0, keepdims=True)[:, 0:1]
    start = pl.multiple_of(plane_ref[0] * width, 128)
    o_ref[...] = weighted_ref[:, pl.ds(start, width)] * lax.rsqrt(total * (1.0 / entries) + 1e-06)


def share(plane, weighted, squares, width, entries):
    return pl.pallas_call(
        functools.partial(share_kernel, entries=entries),
        out_shape=jax.ShapeDtypeStruct((weighted.shape[0], width), F32),
        in_specs=[smem_spec(), vmem_spec(), vmem_spec()],
        out_specs=vmem_spec(),
        compiler_params=params(),
    )(plane, weighted, squares)


def unpack_kernel(r_ref, o_ref, t_ref):
    for z in range(4):
        pair = r_ref[:, z, :].T
        unit = scale_of(pair[SCALE_LANE : SCALE_LANE + 1, :].astype(F32)) * (1.0 / LEVELS)
        t_ref[z] = jnp.concatenate([low_of(pair) * unit, high_of(pair) * unit], axis=1)
        for c in range(3):
            o_ref[c, z] = t_ref[z, c * Q : (c + 1) * Q, :]


def unpack(received):
    return pl.pallas_call(
        unpack_kernel,
        out_shape=jax.ShapeDtypeStruct((3, 4, Q, 128), F32),
        grid=(1,),
        in_specs=[pl.BlockSpec((64, 4, 256), lambda i: (0, 0, 0))],
        out_specs=pl.BlockSpec((3, 4, Q, 128), lambda i: (0, 0, 0, 0)),
        scratch_shapes=[pltpu.VMEM((4, 256, 128), F32)],
        compiler_params=params(),
    )(received)


def on_device(
    adjoint,
    checkpoints,
    checkpoint_step,
    metric,
    helmholtz_inverse,
    wall_element,
    wall_local,
    wall_weight,
):
    span = lax.axis_index("span")
    plane = lax.axis_index("plane")
    span_count = lax.axis_size("span")
    plane_count = lax.axis_size("plane")
    wall_count = wall_element.shape[0]
    core = span % 2
    place = jnp.stack([span, core]).astype(jnp.int32)
    fwd, back = transforms(core, plane)

    def around(block, step):
        return lax.ppermute(
            block, "plane", [(i, (i + step) % plane_count) for i in range(plane_count)]
        )

    def across(block):
        return lax.ppermute(block, "span", [(i, i ^ 1) for i in range(span_count)])

    which = plane.reshape(1).astype(jnp.int32)
    same_core = [list(range(c, span_count, 2)) for c in range(2)]
    own = lax.all_to_all(
        pack_inverse(which, helmholtz_inverse, span_count // 2), "span", 0, 0, tiled=True, axis_index_groups=same_core
    )
    local = wall_local.T.reshape(1, 2 * wall_count)
    element = wall_element.T.reshape(1, 2 * wall_count) - plane * adjoint.shape[3]
    sent = pack_points(adjoint, checkpoints, checkpoint_step)
    own, sent, local, element, place, fwd, back = lax.optimization_barrier(
        (own, sent, local, element, place, fwd, back)
    )
    own = turn_own(own)
    left = around(own, 1)
    right = around(own, 3)
    points = lax.all_to_all(sent, "span", 0, 0, tiled=True)
    oa = around(left[:448], 1)
    ob = around(right[448:], 3)
    both = slope_table()
    first, velocity = first_modes(place, metric, points, fwd, both)
    regrouped = regroup_half((own, across(own), left, across(left)))
    pieces = [right, across(right)]
    oa, ob, regrouped = lax.optimization_barrier((oa, ob, regrouped))
    for piece in (oa, ob):
        pieces += [piece, across(piece)]
    regrouped = pltpu.with_memory_space_constraint(regrouped, pltpu.HBM)
    out = steps(place, metric, regrouped, pieces, first, velocity, fwd, back, both)
    received = lax.all_to_all(out, "span", 0, 0, tiled=True)

    partial_sum = wall_sums(received, local, element)
    parts = [partial_sum] + [around(partial_sum, k) for k in range(1, plane_count)]
    weighted, square = weigh(wall_weight, parts, span_count)
    squares = lax.all_to_all(square, "span", 0, 0, tiled=True)
    gradient = share(
        which,
        weighted,
        squares,
        wall_count // plane_count,
        adjoint.shape[1] * span_count * wall_count,
    )
    return (unpack(received), gradient)


def solution(mesh):
    placed = (
        P(None, "span", None, "plane"),
        P(None, None, "span", None, "plane"),
        P(),
        P(None, "plane"),
        P("span", None, None),
        P(),
        P(),
        P("span", None),
    )
    return jax.shard_map(
        on_device,
        mesh=mesh,
        in_specs=placed,
        out_specs=(P(None, "span", None, "plane"), P("span", "plane")),
        check_vma=False,
    )
```

```python
import functools

import jax
import jax.numpy as jnp
import numpy as np
from jax import lax
from jax.experimental import pallas as pl
from jax.experimental.pallas import tpu as pltpu
from jax.sharding import PartitionSpec as P

P_SIZE = 8
Q = 81
QP = 88
NSTEP = 3
HIGHEST = lax.Precision.HIGHEST
F32 = jnp.float32
VMEM_BYTES = 12 * 1024 * 1024
LEVELS = 32767.0
SCALE_LANE = 250
LINES = 56


def chebyshev_matrix(degree):
    points = np.arange(degree + 1)
    abscissa = np.cos(np.pi * points / degree)
    signed = np.where((points == 0) | (points == degree), 2.0, 1.0) * (-1.0) ** points
    spacing = abscissa[:, None] - abscissa[None, :] + np.eye(degree + 1)
    matrix = signed[:, None] / signed[None, :] / spacing
    return matrix - np.eye(degree + 1) * np.sum(matrix, axis=1)[:, None]


def fourier_table(length):
    row_index = np.arange(length)[:, None]
    column = np.arange(length)[None, :]
    wavenumber = (row_index + 1) // 2
    phase_angle = 2.0 * np.pi * wavenumber * column / length
    parity = row_index % 2
    base_rows = np.where(
        row_index == 0, 1.0, np.where(parity == 1, np.cos(phase_angle), np.sin(phase_angle))
    )
    row_scale = np.where(
        (row_index == 0) | (row_index == length - 1), 1.0 / np.sqrt(length), np.sqrt(2.0 / length)
    )
    return base_rows * row_scale


def lane_order():
    chips = np.arange(32)
    pieces = []
    for shift in (0, 3, 1, 2):
        for core in range(2):
            pieces.append((chips, np.full(chips.shape, core), np.full(chips.shape, shift)))
    return [np.concatenate([p[k] for p in pieces]).astype(np.int32) for k in range(3)]


def in_two(array):
    high = array.astype(jnp.bfloat16)
    return high, (array - high.astype(F32)).astype(jnp.bfloat16)


def split_table(table):
    high = table.astype(jnp.bfloat16)
    return high, (table - high.astype(np.float64)).astype(jnp.bfloat16)


def transforms(core, plane):
    zl = np.arange(256)
    z_of = 4 * (zl % 64) + zl // 64
    high, low = split_table(fourier_table(256)[:, z_of])
    chip, lane_core, shift = (jnp.asarray(v) for v in lane_order())
    span_of = 2 * chip + lane_core + core * (1 - 2 * lane_core)
    order = 4 * span_of + (plane + shift) % 4
    index = jnp.arange(256)
    pick = jnp.where(order[:, None] == index[None, :], 1.0, 0.0).astype(jnp.bfloat16)
    pick_turned = jnp.where(index[:, None] == order[None, :], 1.0, 0.0).astype(jnp.bfloat16)
    both = jnp.asarray(np.concatenate([high, low], axis=1))
    back = jnp.dot(pick, both, preferred_element_type=F32).astype(jnp.bfloat16)
    both = jnp.asarray(np.ascontiguousarray(np.concatenate([high, high, low], axis=1).T))
    fwd = jnp.dot(both, pick_turned, preferred_element_type=F32).astype(jnp.bfloat16)
    return fwd, jnp.concatenate([back[:, :256], back[:, :256], back[:, 256:]], axis=0)


def slope_table():
    d = chebyshev_matrix(P_SIZE)
    eye = np.eye(P_SIZE + 1)
    both = np.zeros((2 * QP, QP), np.float32)
    both[:Q, :Q] = np.kron(d, eye)
    both[QP : QP + Q, :Q] = np.kron(eye, d)
    return jnp.asarray(np.concatenate(split_table(both), axis=0))


def vmem_spec():
    return pl.BlockSpec(memory_space=pltpu.VMEM)


def smem_spec():
    return pl.BlockSpec(memory_space=pltpu.SMEM)


def params(size=VMEM_BYTES):
    return pltpu.CompilerParams(vmem_limit_bytes=size)


def pair_up(low, high):
    return (high.astype(jnp.int32) << 16) | (low.astype(jnp.int32) & 0xFFFF)


def scale_code(largest):
    return jnp.floor(jnp.log2(jnp.maximum(largest, 1e-30)) * 2.0**16) + 2.0


def scale_of(code):
    return jnp.exp2(code * 2.0**-16)


def low_of(pair):
    return ((pair << 16) >> 16).astype(F32)


def high_of(pair):
    return (pair >> 16).astype(F32)


def pack_inverse_kernel(plane_ref, h_ref, o_ref, w_ref, f_ref):
    h = h_ref[:, 0, :]
    for k in range(1, h_ref.shape[1]):
        h = jnp.where(plane_ref[0] == k, h_ref[:, k, :], h)
    largest = jnp.max(jnp.abs(h), axis=1, keepdims=True)
    code = jnp.floor(largest * 2.0**30) + 1.0
    upper = jnp.floor(code * 2.0**-15)
    lower = code - upper * 2.0**15
    w_ref[...] = jnp.zeros_like(w_ref)
    w_ref[0:Q, 0:Q] = jnp.round(h * (LEVELS / (code * 2.0**-30)))
    turned = w_ref[...].T
    w_ref[...] = turned
    w_ref[0:Q, Q : Q + 1] = upper
    w_ref[0:Q, Q + 1 : Q + 2] = lower
    f_ref[...] = jnp.zeros_like(f_ref)
    for k in range(16):
        line, lane = divmod(k * QP, 128)
        count = (Q - k + 15) // 16
        block = w_ref[pl.ds(k, count, stride=16), :]
        if lane:
            block = jnp.roll(block, lane, axis=1)
        place = lax.broadcasted_iota(jnp.int32, (count, 128), 1)
        here = pl.ds(line, count, stride=11)
        f_ref[here, :] = f_ref[here, :] + jnp.where(place >= lane, block, 0.0)
        if lane + QP > 128:
            after = pl.ds(line + 1, count, stride=11)
            f_ref[after, :] = f_ref[after, :] + jnp.where(place < lane, block, 0.0)
    pair = pair_up(f_ref[0:32, :], f_ref[LINES // 2 : LINES // 2 + 32, :])
    o_ref[...] = jnp.broadcast_to(pair[None], o_ref.shape)


def pack_inverse(plane, inverse, targets):
    return pl.pallas_call(
        pack_inverse_kernel,
        out_shape=jax.ShapeDtypeStruct((targets, 32, 128), jnp.int32),
        in_specs=[smem_spec(), vmem_spec()],
        out_specs=vmem_spec(),
        scratch_shapes=[pltpu.VMEM((128, 128), F32), pltpu.VMEM((64, 128), F32)],
        compiler_params=params(),
    )(plane, inverse.transpose(1, 0, 2))


def turn_kernel(own_ref, o_ref):
    for k in range(LINES // 2):
        o_ref[k] = own_ref[:, k, :]


def turn_own(own):
    return pl.pallas_call(
        turn_kernel,
        out_shape=jax.ShapeDtypeStruct((LINES // 2, 32, 128), jnp.int32),
        in_specs=[vmem_spec()],
        out_specs=vmem_spec(),
        compiler_params=params(),
    )(own)


def pack_points_kernel(step_ref, adj_ref, c0_ref, c1_ref, c2_ref, o_ref, t_ref):
    stored = (c0_ref, c1_ref, c2_ref)
    lane = lax.broadcasted_iota(jnp.int32, (64, 256), 1)
    for z in range(4):
        for g in range(3):
            t_ref[g, z, 3 * Q : 256, :] = jnp.zeros((256 - 3 * Q, 128), F32)
            for i in range(3):
                if g == 0:
                    block = adj_ref[i, z]
                else:
                    block = stored[i][0, g - 1, z].astype(F32)
                t_ref[g, z, i * Q : (i + 1) * Q, :] = block
            block = t_ref[g, z]
            largest = jnp.max(jnp.max(jnp.abs(block), axis=0, keepdims=True), axis=1, keepdims=True)
            code = jnp.floor(largest * 2.0**27) + 1.0
            turned = jnp.round(block * (LEVELS / (code * 2.0**-27))).T
            pair = pair_up(turned[0:64, :], turned[64:128, :])
            pair = jnp.where(lane == SCALE_LANE, code.astype(jnp.int32), pair)
            if g == 0:
                o_ref[:, z * 2, 0:256] = pair
            elif g == 1:
                o_ref[:, z * 2, 256:384] = pair[:, 0:128]
                o_ref[:, z * 2 + 1, 0:128] = pair[:, 128:256]
            else:
                o_ref[:, z * 2 + 1, 128:384] = pair


def pack_points(adjoint, checkpoints, checkpoint_step):
    def slot(k):
        return pl.BlockSpec((1, 2, 4, Q, 128), lambda i, st: (st[k], 0, 0, 0, 0))

    return pl.pallas_call(
        pack_points_kernel,
        out_shape=jax.ShapeDtypeStruct((64, 8, 384), jnp.int32),
        grid_spec=pltpu.PrefetchScalarGridSpec(
            num_scalar_prefetch=1,
            grid=(1,),
            in_specs=[
                pl.BlockSpec((3, 4, Q, 128), lambda i, st: (0, 0, 0, 0)),
                slot(0),
                slot(1),
                slot(2),
            ],
            out_specs=pl.BlockSpec((64, 8, 384), lambda i, st: (0, 0, 0)),
            scratch_shapes=[pltpu.VMEM((3, 4, 256, 128), F32)],
        ),
        compiler_params=params(),
    )(checkpoint_step, adjoint, checkpoints, checkpoints, checkpoints)


def transform(array, table_ref):
    high, low = in_two(array)
    return jnp.dot(
        jnp.concatenate([high, low, high], axis=1), table_ref[...], preferred_element_type=F32
    )


def spread_line(pieces, k, ht):
    pair = jnp.concatenate([ref[k - f] for ref, f in pieces], axis=0).T
    ht[k * 128 : (k + 1) * 128, :] = low_of(pair)
    row = (k + LINES // 2) * 128
    ht[row : row + 128, :] = high_of(pair)


def row_scales(ht, rows):
    rows[...] = jnp.zeros_like(rows)
    rows[0:Q, :] = (
        ht[pl.ds(Q, Q, stride=QP), :] * 2.0**15 + ht[pl.ds(Q + 1, Q, stride=QP), :]
    ) * (2.0**-30 / LEVELS)


def regroup_kernel(own_ref, own2_ref, left_ref, left2_ref, o_ref, ht, sems):
    copies = []
    for g in range(LINES // 8):
        for k in range(4 * g, 4 * g + 4):
            spread_line([(r, 0) for r in (own_ref, own2_ref, left_ref, left2_ref)], k, ht)
        for part in range(2):
            block = pl.ds(g * 512 + part * LINES * 64, 512)
            copy = pltpu.make_async_copy(ht.at[block, :], o_ref.at[block, :], sems.at[g, part])
            copy.start()
            copies.append(copy)
    for copy in copies:
        copy.wait()


def regroup_half(pieces):
    return pl.pallas_call(
        regroup_kernel,
        out_shape=pltpu.HBM((LINES * 128, 128), F32),
        in_specs=[vmem_spec()] * 4,
        out_specs=pl.BlockSpec(memory_space=pltpu.HBM),
        scratch_shapes=[
            pltpu.VMEM((LINES * 128, 128), F32),
            pltpu.SemaphoreType.DMA((LINES // 8, 2)),
        ],
        compiler_params=params(),
    )(*pieces)


def advance(place_ref, metric_ref, x, v, step, both_ref, fwd_ref, coef):
    chip = place_ref[0]
    for e in range(2):
        m0 = metric_ref[0, chip + 64 * e]
        m1 = metric_ref[1, chip + 64 * e]
        for c in range(3):
            field = x[e * 3 + c]
            high, low = in_two(field)
            large = jnp.dot(both_ref[...], high, preferred_element_type=F32)
            small = jnp.dot(both_ref[0 : 2 * QP, :], low, preferred_element_type=F32)
            slopes = large[0 : 2 * QP] + (large[2 * QP : 4 * QP] + small)
            x[e * 3 + c] = (
                field
                + v[0, e, step] * (m0 * slopes[0:QP])
                + v[1, e, step] * (m1 * slopes[QP : 2 * QP])
            )
    modes = transform(x[...].reshape(6 * QP, 256), fwd_ref)
    coef[0] = modes[:, 0:128]
    coef[1] = modes[:, 128:256]


def first_kernel(place_ref, metric_ref, r_ref, fwd_ref, both_ref, coef, v, x, spread):
    x[...] = jnp.zeros_like(x)
    v[...] = jnp.zeros_like(v)
    for g in range(3):
        stack = []
        for z in range(4):
            if g == 0:
                stack.append(r_ref[:, z * 2, 0:256])
            elif g == 1:
                stack.append(
                    jnp.concatenate(
                        [r_ref[:, z * 2, 256:384], r_ref[:, z * 2 + 1, 0:128]], axis=1
                    )
                )
            else:
                stack.append(r_ref[:, z * 2 + 1, 128:384])
        pair = jnp.concatenate(stack, axis=0).T
        unit = pair[SCALE_LANE : SCALE_LANE + 1, :].astype(F32) * (2.0**-27 / LEVELS)
        for e in range(2):
            spread[...] = (low_of(pair) if e == 0 else high_of(pair)) * unit
            for i in range(3):
                part = spread[i * Q : (i + 1) * Q, :]
                if g == 0:
                    x[e * 3 + i, 0:Q, :] = part
                else:
                    v[(g - 1), e, i, 0:Q, :] = part
    advance(place_ref, metric_ref, x, v, 0, both_ref, fwd_ref, coef)


def first_modes(place, metric, points, fwd, both):
    return pl.pallas_call(
        first_kernel,
        out_shape=(
            jax.ShapeDtypeStruct((2, 6 * QP, 128), F32),
            jax.ShapeDtypeStruct((2, 2, 3, QP, 256), F32),
        ),
        in_specs=[smem_spec(), smem_spec()] + [vmem_spec()] * 3,
        out_specs=(vmem_spec(), vmem_spec()),
        scratch_shapes=[pltpu.VMEM((6, QP, 256), F32), pltpu.VMEM((256, 256), F32)],
        compiler_params=params(),
    )(place, metric, points, fwd, both)


def steps_kernel(
    place_ref, metric_ref, regrouped_ref, right_ref, right2_ref, oa_ref, oa2_ref, ob_ref, ob2_ref,
    first_ref, v, fwd_ref, back_ref, both_ref,
    out_ref,
    ht0, ht1, rows0, rows1, x, coef, solved, wall, turn, sem,
):
    load = pltpu.make_async_copy(regrouped_ref, ht0, sem)
    load.start()
    halves = (ht0, ht1)
    scales = (rows0, rows1)
    for k in range(LINES // 2):
        first, far = (0, (oa_ref, oa2_ref)) if k < 14 else (14, (ob_ref, ob2_ref))
        near = [(right_ref, 0), (right2_ref, 0)]
        spread_line(near + [(ref, first) for ref in far], k, ht1)
    load.wait()
    row_scales(ht0, rows0)
    row_scales(ht1, rows1)

    for step in range(NSTEP):
        if step > 0:
            advance(place_ref, metric_ref, x, v, step, both_ref, fwd_ref, coef)
        modes = coef if step > 0 else first_ref
        for half in range(2):
            for e in range(2):

                def columns(i, sums, half=half, e=e, modes=modes):
                    for t in range(27):
                        r = i * 27 + t
                        h = halves[half][pl.ds(pl.multiple_of(r * QP, 8), QP), :]
                        sums = tuple(
                            sums[c] + h * modes[half, pl.ds((e * 3 + c) * QP + r, 1), :]
                            for c in range(3)
                        )
                    return sums

                zero = jnp.zeros((QP, 128), F32)
                sums = lax.fori_loop(0, Q // 27, columns, (zero, zero, zero))
                for c in range(3):
                    solved[e * 3 + c, :, half * 128 : (half + 1) * 128] = (
                        sums[c] * scales[half][...]
                    )
        planes = transform(solved[...].reshape(6 * QP, 256), back_ref)
        x[...] = planes.reshape(6, QP, 256)
        for e in range(2):
            product = x[e * 3 + 1] * v[1, e, step]
            if step == 0:
                wall[e] = product
            else:
                wall[e] = wall[e] + product

    def levels(array):
        largest = jnp.max(jnp.max(jnp.abs(array), axis=0), axis=0, keepdims=True)
        code = scale_code(largest)
        return code.astype(jnp.int32), LEVELS / scale_of(code)

    code, unit = levels(wall[...])
    turn[0:QP, :] = pair_up(jnp.round(wall[0] * unit), jnp.round(wall[1] * unit))
    turn[QP:128, :] = jnp.broadcast_to(code, (128 - QP, 256))
    turned = turn[0:128, :].T
    for z in range(4):
        out_ref[:, z, 256:384] = turned[z * 64 : (z + 1) * 64, :]
    code, unit = levels(x[...])
    for c in range(3):
        turn[c * Q : (c + 1) * Q, :] = pair_up(
            jnp.round(x[c, 0:Q, :] * unit), jnp.round(x[c + 3, 0:Q, :] * unit)
        )
    turn[3 * Q : 256, :] = jnp.broadcast_to(code, (256 - 3 * Q, 256))
    turned = turn[...].T
    for z in range(4):
        out_ref[:, z, 0:256] = turned[z * 64 : (z + 1) * 64, :]


def steps(place, metric, regrouped, pieces, first, velocity, fwd, back, both):
    return pl.pallas_call(
        steps_kernel,
        out_shape=jax.ShapeDtypeStruct((64, 4, 384), jnp.int32),
        in_specs=[smem_spec(), smem_spec(), pl.BlockSpec(memory_space=pltpu.HBM)]
        + [vmem_spec()] * (len(pieces) + 5),
        out_specs=vmem_spec(),
        scratch_shapes=[
            pltpu.VMEM((LINES * 128, 128), F32),
            pltpu.VMEM((LINES * 128, 128), F32),
            pltpu.VMEM((QP, 128), F32),
            pltpu.VMEM((QP, 128), F32),
            pltpu.VMEM((6, QP, 256), F32),
            pltpu.VMEM((2, 6 * QP, 128), F32),
            pltpu.VMEM((6, QP, 256), F32),
            pltpu.VMEM((2, QP, 256), F32),
            pltpu.VMEM((256, 256), jnp.int32),
            pltpu.SemaphoreType.DMA,
        ],
        compiler_params=params(2 * VMEM_BYTES),
    )(place, metric, regrouped, *pieces, first, velocity, fwd, back, both)


def wall_kernel(r_ref, local_ref, element_ref, o_ref):
    points = local_ref.shape[1]
    mode = lax.broadcasted_iota(jnp.int32, (128, points), 0)
    pick = jnp.where(mode == local_ref[...], 1.0, 0.0).astype(jnp.bfloat16)
    pick = jnp.concatenate([pick, pick], axis=0)
    here = mode == element_ref[...]
    for z in range(4):
        pair = r_ref[:, z, :]
        unit = scale_of(pair[:, QP : QP + 1].astype(F32)) * (1.0 / LEVELS)
        field = jnp.concatenate([low_of(pair) * unit, high_of(pair) * unit], axis=0)
        high, low = in_two(field)
        values = jnp.dot(
            jnp.concatenate([low, high], axis=1), pick, preferred_element_type=F32
        )
        total = jnp.sum(jnp.where(here, values, 0.0), axis=0, keepdims=True)
        o_ref[z : z + 1, :] = total[:, 0 : points // 2] + total[:, points // 2 :]


def wall_sums(received, local, element):
    return pl.pallas_call(
        wall_kernel,
        out_shape=jax.ShapeDtypeStruct((4, local.shape[1] // 2), F32),
        grid=(1,),
        in_specs=[
            pl.BlockSpec((64, 4, 128), lambda i: (0, 0, 2)),
            pl.BlockSpec(local.shape, lambda i: (0, 0)),
            pl.BlockSpec(element.shape, lambda i: (0, 0)),
        ],
        out_specs=pl.BlockSpec((4, local.shape[1] // 2), lambda i: (0, 0)),
        compiler_params=params(),
    )(received, local, element)


def weigh_kernel(weight_ref, p0_ref, p1_ref, p2_ref, p3_ref, weighted_ref, square_ref):
    weighted = weight_ref[...] * ((p0_ref[...] + p1_ref[...]) + (p2_ref[...] + p3_ref[...]))
    weighted_ref[...] = weighted
    square = jnp.sum(jnp.sum(weighted * weighted, axis=0, keepdims=True), axis=1, keepdims=True)
    square_ref[...] = jnp.broadcast_to(square.reshape(1, 1, 1), square_ref.shape)


def weigh(weight, parts, targets):
    return pl.pallas_call(
        weigh_kernel,
        out_shape=(
            jax.ShapeDtypeStruct(weight.shape, F32),
            jax.ShapeDtypeStruct((targets, 1, 128), F32),
        ),
        in_specs=[vmem_spec()] * 5,
        out_specs=(vmem_spec(), vmem_spec()),
        compiler_params=params(),
    )(weight, *parts)


def share_kernel(plane_ref, weighted_ref, squares_ref, o_ref, *, entries):
    width = o_ref.shape[1]
    total = jnp.sum(squares_ref[:, 0, :], axis=0, keepdims=True)[:, 0:1]
    start = pl.multiple_of(plane_ref[0] * width, 128)
    o_ref[...] = weighted_ref[:, pl.ds(start, width)] * lax.rsqrt(total * (1.0 / entries) + 1e-06)


def share(plane, weighted, squares, width, entries):
    return pl.pallas_call(
        functools.partial(share_kernel, entries=entries),
        out_shape=jax.ShapeDtypeStruct((weighted.shape[0], width), F32),
        in_specs=[smem_spec(), vmem_spec(), vmem_spec()],
        out_specs=vmem_spec(),
        compiler_params=params(),
    )(plane, weighted, squares)


def unpack_kernel(r_ref, o_ref, t_ref):
    for z in range(4):
        pair = r_ref[:, z, :].T
        unit = scale_of(pair[SCALE_LANE : SCALE_LANE + 1, :].astype(F32)) * (1.0 / LEVELS)
        t_ref[z] = jnp.concatenate([low_of(pair) * unit, high_of(pair) * unit], axis=1)
        for c in range(3):
            o_ref[c, z] = t_ref[z, c * Q : (c + 1) * Q, :]


def unpack(received):
    return pl.pallas_call(
        unpack_kernel,
        out_shape=jax.ShapeDtypeStruct((3, 4, Q, 128), F32),
        grid=(1,),
        in_specs=[pl.BlockSpec((64, 4, 256), lambda i: (0, 0, 0))],
        out_specs=pl.BlockSpec((3, 4, Q, 128), lambda i: (0, 0, 0, 0)),
        scratch_shapes=[pltpu.VMEM((4, 256, 128), F32)],
        compiler_params=params(),
    )(received)


def on_device(
    adjoint,
    checkpoints,
    checkpoint_step,
    metric,
    helmholtz_inverse,
    wall_element,
    wall_local,
    wall_weight,
):
    span = lax.axis_index("span")
    plane = lax.axis_index("plane")
    span_count = lax.axis_size("span")
    plane_count = lax.axis_size("plane")
    wall_count = wall_element.shape[0]
    core = span % 2
    place = jnp.stack([span, core]).astype(jnp.int32)
    fwd, back = transforms(core, plane)

    def around(block, step):
        return lax.ppermute(
            block, "plane", [(i, (i + step) % plane_count) for i in range(plane_count)]
        )

    def across(block):
        return lax.ppermute(block, "span", [(i, i ^ 1) for i in range(span_count)])

    which = plane.reshape(1).astype(jnp.int32)
    same_core = [list(range(c, span_count, 2)) for c in range(2)]
    own = lax.all_to_all(
        pack_inverse(which, helmholtz_inverse, span_count // 2), "span", 0, 0, tiled=True, axis_index_groups=same_core
    )
    local = wall_local.T.reshape(1, 2 * wall_count)
    element = wall_element.T.reshape(1, 2 * wall_count) - plane * adjoint.shape[3]
    sent = pack_points(adjoint, checkpoints, checkpoint_step)
    own, sent, local, element, place, fwd, back = lax.optimization_barrier(
        (own, sent, local, element, place, fwd, back)
    )
    own = turn_own(own)
    left = around(own, 1)
    right = around(own, 3)
    points = lax.all_to_all(sent, "span", 0, 0, tiled=True)
    oa = around(left[:14], 1)
    ob = around(right[14:], 3)
    both = slope_table()
    first, velocity = first_modes(place, metric, points, fwd, both)
    regrouped = regroup_half((own, across(own), left, across(left)))
    pieces = [right, across(right)]
    oa, ob, regrouped = lax.optimization_barrier((oa, ob, regrouped))
    for piece in (oa, ob):
        pieces += [piece, across(piece)]
    regrouped = pltpu.with_memory_space_constraint(regrouped, pltpu.HBM)
    out = steps(place, metric, regrouped, pieces, first, velocity, fwd, back, both)
    received = lax.all_to_all(out, "span", 0, 0, tiled=True)

    partial_sum = wall_sums(received, local, element)
    parts = [partial_sum] + [around(partial_sum, k) for k in range(1, plane_count)]
    weighted, square = weigh(wall_weight, parts, span_count)
    squares = lax.all_to_all(square, "span", 0, 0, tiled=True)
    gradient = share(
        which,
        weighted,
        squares,
        wall_count // plane_count,
        adjoint.shape[1] * span_count * wall_count,
    )
    return (unpack(received), gradient)


def solution(mesh):
    placed = (
        P(None, "span", None, "plane"),
        P(None, None, "span", None, "plane"),
        P(),
        P(None, "plane"),
        P("span", None, None),
        P(),
        P(),
        P("span", None),
    )
    return jax.shard_map(
        on_device,
        mesh=mesh,
        in_specs=placed,
        out_specs=(P(None, "span", None, "plane"), P("span", "plane")),
        check_vma=False,
    )
```
